32 devices in a mesh: dp: 4 (over z), mp: 8 (over y, x, core).
Axes of the slice: x: 2, y: 2, z: 4, core: 2. Of those that a mesh axis runs over, the one named last changes fastest.
Arguments:
- inputs: bfloat16 [2, 37632, 1024], P(None, ('dp', 'mp')), may hold values from -6 to 6
- norm0_gain: float32 [1024], replicated, may hold values from 0.5 to 1.5
- norm0_bias: float32 [1024], replicated, may hold values from -1.75 to 1.75
- merge_weight: bfloat16 [1024, 512], replicated, may hold values from -0.1875 to 0.1875
- norm1_gain: float32 [512], replicated, may hold values from 0.5 to 1.5
- norm1_bias: float32 [512], replicated, may hold values from -1.75 to 1.75
- qkv_weight: bfloat16 [512, 16, 96], P(None, 'mp'), may hold values from -0.25 to 0.25
- qkv_bias: bfloat16 [16, 96], P('mp'), may hold values from -1.75 to 1.75
- rel_table: bfloat16 [16, 169], P('mp'), may hold values from -4 to 4
- rel_index: int32 [49, 49], replicated, may hold values from 0 to 168
- regions: int32 [2, 37632], P(None, 'dp'), may hold values from 0 to 3, as said below
- live_windows: int32 [2, 4], P(None, 'dp'), may hold values from 96 to 192, as said below
- proj_weight: bfloat16 [16, 32, 512], P('mp'), may hold values from -0.75 to 0.75
- proj_bias: float32 [512], replicated, may hold values from -1.75 to 1.75
- norm2_gain: float32 [512], replicated, may hold values from 0.5 to 1.5
- norm2_bias: float32 [512], replicated, may hold values from -1.75 to 1.75
- up_weight: bfloat16 [512, 2048], P(None, 'mp'), may hold values from -0.25 to 0.25
- up_bias: bfloat16 [2048], P('mp'), may hold values from -1.75 to 1.75
- down_weight: bfloat16 [2048, 512], P('mp'), may hold values from -0.125 to 0.125
- down_bias: float32 [512], replicated, may hold values from -1.75 to 1.75
- cotangent: bfloat16 [2, 37632, 512], P(None, ('dp', 'mp')), may hold values from -6 to 6
Outputs:
- output: float32 [2, 37632, 512], P(None, ('dp', 'mp'))
- grad_input: float32 [2, 37632, 1024], P(None, ('dp', 'mp'))
- grad_norm0_gain: float32 [1024], replicated
- grad_norm0_bias: float32 [1024], replicated
- grad_merge: float32 [1024, 512], replicated
- grad_norm1_gain: float32 [512], replicated
- grad_norm1_bias: float32 [512], replicated
- grad_qkv: float32 [512, 16, 96], P(None, 'mp')
- grad_qkv_bias: float32 [16, 96], P('mp')
- grad_rel_table: float32 [16, 169], P('mp')
- grad_proj: float32 [16, 32, 512], P('mp')
- grad_proj_bias: float32 [512], replicated
- grad_norm2_gain: float32 [512], replicated
- grad_norm2_bias: float32 [512], replicated
- grad_up: float32 [512, 2048], P(None, 'mp')
- grad_up_bias: float32 [2048], P('mp')
- grad_down: float32 [2048, 512], P('mp')
- grad_down_bias: float32 [512], replicated
The draws below stay inside these ranges and needn't reach their ends.
Inputs may be any that keep to these rules, and one draw needn't show every extreme that they name: `regions`: in every window the region ids of its positions are 2 * (row >= r) + (column >= c) for that window's cuts r, c from 0 to 6; the first window of each micro-batch is cut both ways. `live_windows`: for every page group some micro-batch has all 192 windows live; live windows are the first ones of their group.
All inputs are finite; a program needn't handle non-finite values.
Results may differ from the reference program's by a relative error of at most 0.018.
Values may be sent and summed in bfloat16 or wider, within the bound.
A program may use at most 256 MiB of HBM per device.

```python
import math
import jax
import jax.numpy as jnp
from jax import lax

D_IN = 1024
DIM = 512
HEADS = 16
HEAD_DIM = 32
FFN = 2048
WIN_SIDE = 7
WIN_DEV = 24
MICRO = 2
WIN_TOK = 49
REL = 169
GROUP_WIN = 192
WINDOWS = 768
ROWS = 37632
N_DP = 4
N_MP = 8


def draw_regions(key, part):
    key = jax.random.fold_in(key, 11)
    subkeys = jax.random.split(key, 4)
    first_window = jnp.arange(WINDOWS)[None, :] == 0
    cut_list = []
    for dimension in range(2):
        drawn_cut = jax.random.randint(subkeys[dimension], (MICRO, WINDOWS), 0, 2 * WIN_SIDE)
        drawn_cut = jnp.where(drawn_cut < WIN_SIDE, drawn_cut, 0)
        forced = jax.random.randint(subkeys[dimension + 2], (MICRO, 1), 1, WIN_SIDE)
        cut_list.append(jnp.where(first_window, forced, drawn_cut))
    positions = jnp.arange(WIN_TOK)
    row_ids = positions // WIN_SIDE
    col_ids = positions % WIN_SIDE
    upper = (row_ids[None, None, :] >= cut_list[0][:, :, None]).astype(jnp.int32)
    right = (col_ids[None, None, :] >= cut_list[1][:, :, None]).astype(jnp.int32)
    region_ids = 2 * upper + right
    return region_ids.reshape(MICRO, WINDOWS * WIN_TOK).astype(jnp.int32)


def draw_live_windows(key, part):
    key = jax.random.fold_in(key, 23)
    first_key, second_key = jax.random.split(key)
    group_count = WINDOWS // GROUP_WIN
    full_batch = jax.random.randint(first_key, (group_count,), 0, MICRO)
    counts_drawn = jax.random.randint(second_key, (MICRO, group_count), GROUP_WIN // 2, GROUP_WIN + 1)
    batch_ids = jnp.arange(MICRO)[:, None]
    return jnp.where(batch_ids == full_batch[None, :], GROUP_WIN, counts_drawn).astype(jnp.int32)


def plant(values, rng, low, largest):
    extent = values.shape
    spot = [jax.random.randint(jax.random.fold_in(rng, axis), (), 0, extent[axis]) for axis in range(len(extent))]
    values = values.at[tuple(spot)].set(low)
    longest = extent.index(max(extent))
    spot[longest] = (spot[longest] + 1) % extent[longest]
    return values.at[tuple(spot)].set(largest)


def steps_of(own_key, extent, shards, least, top_value):
    def one(position, shards_of):
        heights = jax.random.uniform(jax.random.fold_in(jax.random.fold_in(own_key, 6), position), (shards_of,), jnp.float32, least / len(shards), top_value / len(shards))
        return jnp.repeat(jnp.exp(heights), extent[position] // shards_of).reshape((-1,) + (1,) * (len(extent) - position - 1))

    level = one(*shards[0])
    for cut in shards[1:]:
        level = level * one(*cut)
    return level


def bell_draw(rng, extent, scale, most, cuts=(), held_as=jnp.bfloat16):
    drawn = jax.random.normal(rng, extent, jnp.float32) * scale
    if len(cuts) > 0:
        drawn = steps_of(rng, extent, cuts, -0.22, 0.18) * drawn
    return jnp.clip(drawn, min=-most, max=most).astype(held_as)


def setup_inputs(seed: int = 0) -> dict:
    splits = jax.random.split(jax.random.key(seed), 22)
    inputs = bell_draw(splits[0], (MICRO, ROWS, D_IN), 1.0, 6.0, ((1, 32),))
    norm0_gain = jnp.clip(1.0 + 0.1 * jax.random.normal(splits[1], (D_IN,), jnp.float32), 0.5, 1.5)
    norm0_bias = bell_draw(splits[2], (D_IN,), 0.3, 1.75, (), jnp.float32)
    merge_weight = bell_draw(splits[3], (D_IN, DIM), D_IN ** -0.5, 0.1875)
    norm1_gain = jnp.clip(1.0 + 0.1 * jax.random.normal(splits[4], (DIM,), jnp.float32), 0.5, 1.5)
    norm1_bias = bell_draw(splits[5], (DIM,), 0.3, 1.75, (), jnp.float32)
    qkv_weight = bell_draw(splits[6], (DIM, HEADS, 3 * HEAD_DIM), DIM ** -0.5, 0.25, ((1, 8),))
    qkv_bias = bell_draw(splits[7], (HEADS, 3 * HEAD_DIM), 0.3, 1.75, ((0, 8),))
    rel_table = bell_draw(splits[8], (HEADS, REL), 1.0, 4.0, ((0, 8),))
    rel_index = plant(jax.random.randint(splits[9], (WIN_TOK, WIN_TOK), 0, REL), jax.random.fold_in(splits[9], 1), 0, REL - 1).astype(jnp.int32)
    regions = draw_regions(jax.random.fold_in(splits[21], 71), 0)
    live_windows = draw_live_windows(jax.random.fold_in(splits[21], 71), 0)
    proj_weight = bell_draw(splits[12], (HEADS, HEAD_DIM, DIM), 64 ** -0.5, 0.75, ((0, 8),))
    proj_bias = bell_draw(splits[13], (DIM,), 0.3, 1.75, (), jnp.float32)
    norm2_gain = jnp.clip(1.0 + 0.1 * jax.random.normal(splits[14], (DIM,), jnp.float32), 0.5, 1.5)
    norm2_bias = bell_draw(splits[15], (DIM,), 0.3, 1.75, (), jnp.float32)
    up_weight = bell_draw(splits[16], (DIM, FFN), DIM ** -0.5, 0.25, ((1, 8),))
    up_bias = bell_draw(splits[17], (FFN,), 0.3, 1.75, ((0, 8),))
    down_weight = bell_draw(splits[18], (FFN, DIM), FFN ** -0.5, 0.125, ((0, 8),))
    down_bias = bell_draw(splits[19], (DIM,), 0.3, 1.75, (), jnp.float32)
    cotangent = bell_draw(splits[20], (MICRO, ROWS, DIM), 1.0, 6.0, ((1, 32),))
    return {"inputs": inputs, "norm0_gain": norm0_gain, "norm0_bias": norm0_bias, "merge_weight": merge_weight, "norm1_gain": norm1_gain, "norm1_bias": norm1_bias, "qkv_weight": qkv_weight, "qkv_bias": qkv_bias, "rel_table": rel_table, "rel_index": rel_index, "regions": regions, "live_windows": live_windows, "proj_weight": proj_weight, "proj_bias": proj_bias, "norm2_gain": norm2_gain, "norm2_bias": norm2_bias, "up_weight": up_weight, "up_bias": up_bias, "down_weight": down_weight, "down_bias": down_bias, "cotangent": cotangent}


@jax.custom_vjp
def low(v):
    return lax.optimization_barrier(v.astype(jnp.bfloat16)).astype(jnp.float32)

@jax.custom_vjp
def low_back(v):
    return v

def low_keep(v):
    return (low(v), None)

def low_pass(kept, grad):
    return (grad,)

def back_keep(v):
    return (v, None)

def back_low(kept, grad):
    return (low(grad),)
low.defvjp(low_keep, low_pass)
low_back.defvjp(back_keep, back_low)
EPSILON = 1e-05
MASKED = -1e+30
HIGHEST = lax.Precision.HIGHEST

def layer_norm(values, gain, shift):
    center = values - lax.optimization_barrier(jnp.mean(values, axis=-1, keepdims=True))
    spread = lax.optimization_barrier(jnp.mean(center * center, axis=-1, keepdims=True))
    return center * lax.rsqrt(spread + EPSILON) * gain + shift

def product(left, right):
    return jnp.dot(left, right, precision=HIGHEST)

def block(params, values, region_ids, live_rows, rel_index):
    norm0_gain, norm0_bias, merge_weight, norm1_gain, norm1_bias, qkv_weight, qkv_bias, rel_table, proj_weight, proj_bias, norm2_gain, norm2_bias, up_weight, up_bias, down_weight, down_bias = params
    row_count = values.shape[0]
    window_count = row_count // WIN_TOK
    score_scale = 1.0 / math.sqrt(HEAD_DIM)
    normed_in = low(layer_norm(values, norm0_gain, norm0_bias))
    merged = low_back(product(normed_in, merge_weight))
    normed_mid = low(layer_norm(merged, norm1_gain, norm1_bias))
    packed = product(normed_mid, qkv_weight.reshape(DIM, 3 * DIM)) + qkv_bias.reshape(3 * DIM)
    packed = low(low_back(packed)).reshape(window_count, WIN_TOK, HEADS, 3 * HEAD_DIM)
    queries = packed[..., :HEAD_DIM]
    keys_all = packed[..., HEAD_DIM:2 * HEAD_DIM]
    values_all = packed[..., 2 * HEAD_DIM:]
    table_bias = rel_table[:, rel_index]
    raw_scores = jnp.einsum('wihd,wjhd->whij', queries, keys_all, precision=HIGHEST) * score_scale + table_bias[None]
    raw_scores = low_back(raw_scores)
    window_ids = region_ids.reshape(window_count, WIN_TOK)
    same_region = window_ids[:, None, :, None] == window_ids[:, None, None, :]
    masked = jnp.where(same_region, raw_scores, MASKED)
    top_score = lax.optimization_barrier(jnp.max(masked, axis=-1, keepdims=True))
    weights_exp = jnp.exp(masked - top_score)
    probabilities = low(weights_exp / lax.optimization_barrier(jnp.sum(weights_exp, axis=-1, keepdims=True)))
    attended = jnp.einsum('whij,wjhd->wihd', probabilities, values_all, precision=HIGHEST)
    attended = low(low_back(attended)).reshape(row_count, DIM)
    attn_out = low_back(product(attended, proj_weight.reshape(DIM, DIM)) + proj_bias)
    middle = merged + attn_out
    normed_ffn = low(layer_norm(middle, norm2_gain, norm2_bias))
    pre_act = low_back(product(normed_ffn, up_weight) + up_bias)
    activated = low(jax.nn.gelu(pre_act, approximate=False))
    branch = low_back(product(activated, down_weight) + down_bias)
    return (middle + branch) * live_rows[:, None]

def reference(inputs, norm0_gain, norm0_bias, merge_weight, norm1_gain, norm1_bias, qkv_weight, qkv_bias, rel_table, rel_index, regions, live_windows, proj_weight, proj_bias, norm2_gain, norm2_bias, up_weight, up_bias, down_weight, down_bias, cotangent):
    strip_count = MICRO * N_DP * N_MP
    strip_rows = WIN_DEV * WIN_TOK
    window_index = jnp.arange(WINDOWS, dtype=jnp.int32)
    group_of = (window_index // GROUP_WIN).astype(jnp.int32)
    live_window = (window_index % GROUP_WIN)[None, :] < jnp.take(live_windows, group_of, axis=1)
    live_rows = jnp.repeat(live_window.astype(jnp.float32), WIN_TOK, axis=1).reshape(strip_count, strip_rows)
    params = tuple((parameter.astype(jnp.float32) for parameter in (norm0_gain, norm0_bias, merge_weight, norm1_gain, norm1_bias, qkv_weight, qkv_bias, rel_table, proj_weight, proj_bias, norm2_gain, norm2_bias, up_weight, up_bias, down_weight, down_bias)))
    strips_in = inputs.reshape(strip_count, strip_rows, D_IN)
    strips_cot = cotangent.reshape(strip_count, strip_rows, DIM)
    strips_region = regions.reshape(strip_count, strip_rows)

    def strip_step(totals, pieces):
        piece_in, piece_region, piece_live, piece_cot = pieces

        def forward(param_list, values):
            return block(param_list, values, piece_region, piece_live, rel_index)
        result, pullback = jax.vjp(forward, params, piece_in.astype(jnp.float32))
        param_grads, input_grad = pullback(piece_cot.astype(jnp.float32))
        totals = jax.tree.map(lambda running, grad_part: running + grad_part, totals, param_grads)
        return (totals, (result, input_grad))
    zero_grads = tuple((jnp.zeros(parameter.shape, jnp.float32) for parameter in params))
    totals, (results, input_grads) = lax.scan(strip_step, zero_grads, (strips_in, strips_region, live_rows, strips_cot))
    output = results.reshape(MICRO, ROWS, DIM)
    grad_input = input_grads.reshape(MICRO, ROWS, D_IN)
    return (output, grad_input, totals[0], totals[1], totals[2], totals[3], totals[4], totals[5], totals[6], totals[7], totals[8], totals[9], totals[10], totals[11], totals[12], totals[13], totals[14], totals[15])
```

```python
import functools
import math

import jax
import jax.numpy as jnp
from jax import lax
from jax.experimental import pallas as pl
from jax.experimental.pallas import tpu as pltpu
from jax.sharding import PartitionSpec as P

F32 = jnp.float32
BF16 = jnp.bfloat16
EPSILON = 1e-05
MASKED = -1e30
COVER = 64
TILE = 16
GROUP = 4
VMEM_LIMIT = 60 << 20


def dot(left, right):
    return jnp.dot(left, right, preferred_element_type=F32)


def dot_rt(left, right):
    return lax.dot_general(left, right, (((1,), (1,)), ((), ())), preferred_element_type=F32)


def dot_lt(left, right):
    return lax.dot_general(left, right, (((0,), (0,)), ((), ())), preferred_element_type=F32)


def whole(shape):
    return pl.BlockSpec(shape, lambda i: (0,) * len(shape), pipeline_mode=pl.Buffered(1))


def call(kernel, grid, ins, in_specs, outs, out_specs, scratch, flops, nbytes):
    return pl.pallas_call(
        kernel,
        grid=(grid,),
        in_specs=in_specs,
        out_specs=out_specs,
        out_shape=outs,
        scratch_shapes=scratch,
        compiler_params=pltpu.CompilerParams(
            dimension_semantics=("arbitrary",), vmem_limit_bytes=VMEM_LIMIT
        ),
        cost_estimate=pl.CostEstimate(flops=flops, bytes_accessed=nbytes, transcendentals=0),
    )(*ins)


def spans(total, step):
    return [(start, min(step, total - start)) for start in range(0, total, step)]


def norm_parts(values):
    center = values - jnp.mean(values, axis=-1, keepdims=True)
    inverse = lax.rsqrt(jnp.mean(center * center, axis=-1, keepdims=True) + EPSILON)
    return center * inverse, inverse


def norm_back(grad, normed, inverse):
    mean_grad = jnp.mean(grad, axis=-1, keepdims=True)
    mean_cross = jnp.mean(grad * normed, axis=-1, keepdims=True)
    return inverse * (grad - mean_grad - normed * mean_cross)


def head_mask(head_dim):
    rows = lax.broadcasted_iota(jnp.int32, (GROUP * COVER, GROUP * head_dim), 0) // COVER
    cols = lax.broadcasted_iota(jnp.int32, (GROUP * COVER, GROUP * head_dim), 1) // head_dim
    return (rows == cols).astype(F32).astype(BF16)


def tiled(block, mask):
    return jnp.concatenate([block] * GROUP, axis=0) * mask


def merge_kernel(x_ref, g0_ref, b0_ref, wm_ref, g1_ref, b1_ref, merged_ref, mid_ref):
    normed, _ = norm_parts(x_ref[...].astype(F32))
    normed_in = (normed * g0_ref[...] + b0_ref[...]).astype(BF16)
    merged = dot(normed_in, wm_ref[...])
    merged_ref[...] = merged
    normed1, _ = norm_parts(merged)
    mid_ref[...] = (normed1 * g1_ref[...] + b1_ref[...]).astype(BF16)


def merge_rows(x, g0, b0, wm, g1, b1):
    rows, wide = x.shape
    width = wm.shape[1]
    step = rows // 7
    return call(
        merge_kernel,
        7,
        (x, g0, b0, wm, g1, b1),
        [
            pl.BlockSpec((step, wide), lambda i: (i, 0)),
            whole((1, wide)),
            whole((1, wide)),
            whole((wide, width)),
            whole((1, width)),
            whole((1, width)),
        ],
        [
            jax.ShapeDtypeStruct((rows, width), F32),
            jax.ShapeDtypeStruct((rows, width), BF16),
        ],
        [
            pl.BlockSpec((step, width), lambda i: (i, 0)),
            pl.BlockSpec((step, width), lambda i: (i, 0)),
        ],
        [],
        2 * rows * wide * width,
        rows * (2 * wide + 6 * width),
    )


def index_onehot(row, table_width):
    entry = lax.broadcasted_iota(jnp.int32, (table_width, row.shape[1]), 0)
    return (entry == row).astype(F32).astype(BF16)


def attn_kernel(
    head_dim,
    mid_ref,
    w_ref,
    qb_ref,
    tab_ref,
    idx_ref,
    ridc_ref,
    ridr_ref,
    q_ref,
    k_ref,
    v_ref,
    att_ref,
    rinv_ref,
    p_ref,
    wt_s,
    base_s,
    bias_s,
    mask_s,
):
    step = pl.program_id(0)
    rows, width = mid_ref.shape
    heads = width // head_dim
    lanes = GROUP * head_dim
    groups = heads // GROUP
    scale = 1.0 / math.sqrt(head_dim)
    outs = (q_ref, k_ref, v_ref)

    @pl.when(step == 0)
    def _():
        mask_s[...] = head_mask(head_dim)
        att_ref[...] = jnp.zeros_like(att_ref)
        rinv_ref[...] = jnp.zeros_like(rinv_ref)
        shards, local = w_ref.shape[0], w_ref.shape[1] // (3 * head_dim)
        for s in range(shards):
            for l in range(local):
                for t in range(3):
                    at = t * width + (s * local + l) * head_dim
                    wt_s[at : at + head_dim, :] = w_ref[
                        s, (3 * l + t) * head_dim : (3 * l + t + 1) * head_dim, :
                    ]
        part = rows // 7

        def project(i, _):
            here = pl.ds(pl.multiple_of(i * part, TILE), part)
            x = mid_ref[here, :]
            for t in range(3):
                y = dot_rt(x, wt_s[t * width : (t + 1) * width, :])
                y = y + qb_ref[:, t * width : (t + 1) * width]
                if t == 0:
                    y = y * scale
                outs[t][here, :] = y.astype(BF16)
            return 0

        lax.fori_loop(0, 7, project, 0)
        base_s[...] = jnp.full(base_s.shape, MASKED, F32)
        table = tab_ref[...]
        for pair in range(idx_ref.shape[0]):
            row = idx_ref[pair : pair + 1, :]
            vals = dot(table, index_onehot(row, table.shape[1]))
            vals = jnp.where(row < 0, MASKED, vals)
            base_s[:, 2 * pair, :] = vals[:, :COVER]
            base_s[:, 2 * pair + 1, :] = vals[:, COVER:]
        for g in range(groups):
            full = jnp.concatenate([base_s[g * GROUP + h] for h in range(GROUP)], axis=1)

            def shift(o, _):
                bias_s[o, g] = pltpu.roll(pltpu.roll(full, o, 0), o, 1)
                return 0

            lax.fori_loop(0, TILE, shift, 0)

    low_half = lax.broadcasted_iota(jnp.int32, (COVER, 2 * COVER), 1) < COVER
    sets = ridc_ref.shape[1]
    mask = mask_s[...]
    block = rows // sets
    stride = block // TILE - 1
    starts = [pl.multiple_of(step * stride + u * block, TILE) for u in range(sets)]
    fences = []
    for u in range(sets):
        same = ridc_ref[0, u] == ridr_ref[0, u]
        fences.append(jnp.where(same, 0.0, MASKED))
    for pair in range(0, groups, 2):
        units = [(u, g) for u in range(sets) for g in range(pair, pair + 2)]
        scores = []
        for u, g in units:
            here, cols = pl.ds(starts[u], COVER), pl.ds(g * lanes, lanes)
            scores.append(dot_rt(q_ref[here, cols], tiled(k_ref[here, cols], mask)))
        weights = []
        for (u, g), s in zip(units, scores):
            s = s + bias_s[step, g] + fences[u]
            parts = []
            for c in range(GROUP // 2):
                x = s[:, c * 2 * COVER : (c + 1) * 2 * COVER]
                top0 = jnp.max(jnp.where(low_half, x, MASKED), axis=1, keepdims=True)
                top1 = jnp.max(jnp.where(low_half, MASKED, x), axis=1, keepdims=True)
                top = jnp.maximum(jnp.where(low_half, top0, top1), MASKED * 0.1)
                parts.append(jnp.exp(x - top).astype(BF16))
            w = jnp.concatenate(parts, axis=1)
            p_ref[0, u, g] = w
            weights.append(w)
        mixed = []
        for (u, g), w in zip(units, weights):
            here, cols = pl.ds(starts[u], COVER), pl.ds(g * lanes, lanes)
            vals = jnp.concatenate([tiled(v_ref[here, cols], mask), mask], axis=1)
            mixed.append(dot(w, vals))
        for (u, g), a in zip(units, mixed):
            here, cols = pl.ds(starts[u], COVER), pl.ds(g * lanes, lanes)
            total = a[:, lanes:]
            inv = jnp.where(total > 0.0, 1.0 / jnp.maximum(total, 0.5), 0.0)
            att_ref[here, cols] += (a[:, :lanes] * inv).astype(BF16)
            rinv_ref[here, cols] += inv.astype(BF16)


def attn_rows(mid, w, qb, tab, idx, ridc, ridr, head_dim):
    rows, width = mid.shape
    heads = width // head_dim
    groups = heads // GROUP
    steps, sets = ridc.shape[0], ridc.shape[1]
    wide = GROUP * COVER
    row_out = jax.ShapeDtypeStruct((rows, width), BF16)
    return call(
        functools.partial(attn_kernel, head_dim),
        steps,
        (mid, w, qb, tab, idx, ridc, ridr),
        [
            whole(mid.shape),
            whole(w.shape),
            whole(qb.shape),
            whole(tab.shape),
            whole(idx.shape),
            pl.BlockSpec((1,) + ridc.shape[1:], lambda i: (i, 0, 0, 0)),
            pl.BlockSpec((1,) + ridr.shape[1:], lambda i: (i, 0, 0, 0)),
        ],
        [row_out] * 5 + [jax.ShapeDtypeStruct((steps, sets, groups, COVER, wide), BF16)],
        [whole((rows, width))] * 5
        + [pl.BlockSpec((1, sets, groups, COVER, wide), lambda i: (i, 0, 0, 0, 0))],
        [
            pltpu.VMEM((3 * width, width), BF16),
            pltpu.VMEM((heads, COVER, COVER), F32),
            pltpu.VMEM((TILE, groups, COVER, wide), F32),
            pltpu.VMEM((wide, GROUP * head_dim), BF16),
        ],
        2 * rows * width * 3 * width * 6,
        rows * width * 20,
    )


def gelu_parts(x):
    t = 1.0 / (1.0 + (0.3275911 / math.sqrt(2.0)) * jnp.abs(x))
    bell = jnp.exp(-0.5 * (x * x))
    poly = 0.5 * 1.061405429 * t + 0.5 * -1.453152027
    poly = poly * t + 0.5 * 1.421413741
    poly = poly * t + 0.5 * -0.284496736
    poly = poly * t + 0.5 * 0.254829592
    tail = poly * t * bell
    cdf = jnp.where(x > 0.0, 1.0 - tail, tail)
    return cdf, x * bell * (1.0 / math.sqrt(2.0 * math.pi))


def live_rows(limits_ref, start, count, micro_rows, width):
    row = lax.broadcasted_iota(jnp.int32, (count, width), 0) + start
    live = None
    for m in range(limits_ref.shape[1]):
        inside = (row >= m * micro_rows) & (row < m * micro_rows + limits_ref[0, m])
        live = inside if live is None else live | inside
    return live


def ffn_kernel(
    limits_ref,
    merged_ref,
    att_ref,
    cot_ref,
    rinv_ref,
    wp_ref,
    vecs_ref,
    ub_ref,
    up_ref,
    down_ref,
    out_ref,
    gmid_ref,
    gatt_ref,
    gffn_ref,
    gub_ref,
    gproj_ref,
    sums_ref,
    n2_s,
    inv_s,
    n_s,
    go_s,
    nt_s,
    gt_s,
    act_s,
    gp_s,
):
    chunk = pl.program_id(0)
    last = pl.num_programs(0) - 1
    rows, width = merged_ref.shape
    padded = n_s.shape[0]
    micro_rows = rows // limits_ref.shape[1]
    blocks = spans(rows, 512)

    @pl.when(chunk == 0)
    def _():
        bias_proj, gain2, bias2, bias_down = (vecs_ref[i : i + 1, :] for i in range(4))
        act_s[rows:, :] = jnp.zeros_like(act_s[rows:, :])
        gp_s[rows:, :] = jnp.zeros_like(gp_s[rows:, :])
        down_sum = jnp.zeros((1, width), F32)
        for start, count in blocks:
            here = pl.ds(start, count)
            middle = merged_ref[here, :] + dot(att_ref[here, :], wp_ref[...]) + bias_proj
            out_ref[here, :] = middle + bias_down
            normed, inverse = norm_parts(middle)
            n2_s[here, :] = normed.astype(BF16)
            inv_s[here, :] = jnp.broadcast_to(inverse, (count, inv_s.shape[1]))
            normed_ffn = (normed * gain2 + bias2).astype(BF16)
            n_s[here, :] = normed_ffn
            live = live_rows(limits_ref, start, count, micro_rows, width)
            grad_out = jnp.where(live, cot_ref[here, :].astype(F32), 0.0)
            down_sum = down_sum + jnp.sum(grad_out, axis=0, keepdims=True)
            grad_low = grad_out.astype(BF16)
            go_s[here, :] = grad_low
            whole_count = -(-count // 128) * 128
            if whole_count != count:
                filler = jnp.zeros((whole_count - count, width), BF16)
                normed_ffn = jnp.concatenate([normed_ffn, filler], axis=0)
                grad_low = jnp.concatenate([grad_low, filler], axis=0)
            nt_s[:, start : start + whole_count] = normed_ffn.T
            gt_s[:, start : start + whole_count] = grad_low.T
        sums_ref[...] = jnp.zeros_like(sums_ref)
        sums_ref[3:4, :] = down_sum
        gmid_ref[...] = jnp.zeros_like(gmid_ref)

    up_t, down = up_ref[0], down_ref[0]
    up_bias = ub_ref[0]
    up_sum = jnp.zeros((1, up_t.shape[0]), F32)
    for start, count in blocks:
        here = pl.ds(start, count)
        pre = dot_rt(n_s[here, :], up_t) + up_bias
        cdf, slope = gelu_parts(pre)
        act = (pre * cdf).astype(BF16)
        grad_pre = dot_rt(go_s[here, :], down) * (cdf + slope)
        up_sum = up_sum + jnp.sum(grad_pre, axis=0, keepdims=True)
        grad_pre = grad_pre.astype(BF16)
        act_s[here, :] = act
        gp_s[here, :] = grad_pre
        out_ref[here, :] += dot(act, down)
        gmid_ref[here, :] += dot(grad_pre, up_t)
    gub_ref[0] = up_sum
    hidden = up_t.shape[0]
    gffn_ref[0, :, :hidden] = dot(nt_s[...], gp_s[...]).astype(BF16)
    gffn_ref[0, :, hidden:] = dot(gt_s[...], act_s[...]).astype(BF16)

    @pl.when(chunk == last)
    def _():
        gain2 = vecs_ref[1:2, :]
        gain_sum = jnp.zeros((1, width), F32)
        bias_sum = jnp.zeros((1, width), F32)
        proj_sum = jnp.zeros((1, width), F32)
        gproj_ref[...] = jnp.zeros_like(gproj_ref)
        for start, count in blocks:
            here = pl.ds(start, count)
            live = live_rows(limits_ref, start, count, micro_rows, width)
            out_ref[here, :] = jnp.where(live, out_ref[here, :], 0.0)
            grad_ffn = gmid_ref[here, :]
            normed = n2_s[here, :].astype(F32)
            gain_sum = gain_sum + jnp.sum(grad_ffn * normed, axis=0, keepdims=True)
            bias_sum = bias_sum + jnp.sum(grad_ffn, axis=0, keepdims=True)
            grad_middle = go_s[here, :].astype(F32) + norm_back(
                grad_ffn * gain2, normed, inv_s[here, :1]
            )
            gmid_ref[here, :] = grad_middle
            proj_sum = proj_sum + jnp.sum(grad_middle, axis=0, keepdims=True)
            grad_attn = grad_middle.astype(BF16)
            gproj_ref[...] += dot_lt(att_ref[here, :], grad_attn)
            grad_att = dot_rt(grad_attn, wp_ref[...]) * rinv_ref[here, :].astype(F32)
            gatt_ref[here, :] = grad_att.astype(BF16)
        sums_ref[0:1, :] = proj_sum
        sums_ref[1:2, :] = gain_sum
        sums_ref[2:3, :] = bias_sum


def ffn_rows(limits, merged, att, cot, rinv, wp, vecs, ub, up, down):
    rows, width = merged.shape
    shards, hidden = up.shape[0], up.shape[1]
    padded = -(-rows // 128) * 128
    return call(
        ffn_kernel,
        shards,
        (limits, merged, att, cot, rinv, wp, vecs, ub, up, down),
        [
            pl.BlockSpec(memory_space=pltpu.SMEM),
            whole(merged.shape),
            whole(att.shape),
            whole(cot.shape),
            whole(rinv.shape),
            whole(wp.shape),
            whole(vecs.shape),
            pl.BlockSpec((1, 1, hidden), lambda i: (i, 0, 0)),
            pl.BlockSpec((1, hidden, width), lambda i: (i, 0, 0)),
            pl.BlockSpec((1, hidden, width), lambda i: (i, 0, 0)),
        ],
        [
            jax.ShapeDtypeStruct((rows, width), F32),
            jax.ShapeDtypeStruct((rows, width), F32),
            jax.ShapeDtypeStruct((rows, width), BF16),
            jax.ShapeDtypeStruct((shards, width, 2 * hidden), BF16),
            jax.ShapeDtypeStruct((shards, 1, hidden), F32),
            jax.ShapeDtypeStruct((width, width), F32),
            jax.ShapeDtypeStruct((8, width), F32),
        ],
        [
            whole((rows, width)),
            whole((rows, width)),
            whole((rows, width)),
            pl.BlockSpec((1, width, 2 * hidden), lambda i: (i, 0, 0)),
            pl.BlockSpec((1, 1, hidden), lambda i: (i, 0, 0)),
            whole((width, width)),
            whole((8, width)),
        ],
        [
            pltpu.VMEM((rows, width), BF16),
            pltpu.VMEM((rows, 128), F32),
            pltpu.VMEM((padded, width), BF16),
            pltpu.VMEM((padded, width), BF16),
            pltpu.VMEM((width, padded), BF16),
            pltpu.VMEM((width, padded), BF16),
            pltpu.VMEM((padded, hidden), BF16),
            pltpu.VMEM((padded, hidden), BF16),
        ],
        2 * rows * width * hidden * shards * 6,
        rows * width * 20,
    )


def attn_back_kernel(
    head_dim,
    q_ref,
    k_ref,
    v_ref,
    ga_ref,
    att_ref,
    p_ref,
    idx_ref,
    gq_ref,
    gk_ref,
    gv_ref,
    gtab_ref,
    ds_s,
    base_s,
    mask_s,
):
    step = pl.program_id(0)
    last = pl.num_programs(0) - 1
    rows, width = q_ref.shape
    lanes = GROUP * head_dim
    groups = width // lanes
    scale = 1.0 / math.sqrt(head_dim)
    sets = p_ref.shape[1]
    block = rows // sets

    @pl.when(step == 0)
    def _():
        mask_s[...] = head_mask(head_dim)
        gq_ref[...] = jnp.zeros_like(gq_ref)
        gk_ref[...] = jnp.zeros_like(gk_ref)
        gv_ref[...] = jnp.zeros_like(gv_ref)

    mask = mask_s[...]
    minus = -mask
    starts = [pl.multiple_of(step * (block // TILE - 1) + u * block, TILE) for u in range(sets)]
    lane_head = lax.broadcasted_iota(jnp.int32, (COVER, 2 * lanes), 1) % lanes // head_dim
    zeros = jnp.zeros((COVER, lanes), BF16)
    units = [(u, g) for g in range(groups) for u in range(sets)]

    def at(ref, u, g):
        return ref[pl.ds(starts[u], COVER), pl.ds(g * lanes, lanes)]

    grads = []
    for u, g in units:
        ga = at(ga_ref, u, g)
        left = jnp.concatenate([ga, ga * at(att_ref, u, g)], axis=1)
        right = jnp.concatenate([tiled(at(v_ref, u, g), mask), minus], axis=1)
        grads.append(dot_rt(left, right))
    score_grads = []
    totals = {}
    for (u, g), grad in zip(units, grads):
        ds = p_ref[0, u, g].astype(F32) * grad
        totals[g] = ds if g not in totals else totals[g] + ds
        score_grads.append(ds.astype(BF16))
    for g in range(groups):
        ds_s[step, g] = totals[g]
    query_grads = []
    for (u, g), ds in zip(units, score_grads):
        query_grads.append(dot(ds, tiled(at(k_ref, u, g), mask)))
    pair_grads = []
    for (u, g), ds in zip(units, score_grads):
        left = jnp.concatenate([ds, p_ref[0, u, g]], axis=0)
        right = jnp.concatenate(
            [
                jnp.concatenate([at(q_ref, u, g), zeros], axis=1),
                jnp.concatenate([zeros, at(ga_ref, u, g)], axis=1),
            ],
            axis=0,
        )
        pair_grads.append(dot_lt(left, right))
    for (u, g), grad_q, grad_kv in zip(units, query_grads, pair_grads):
        here, cols = pl.ds(starts[u], COVER), pl.ds(g * lanes, lanes)
        gq_ref[here, cols] += (grad_q * scale).astype(BF16)
        both = jnp.where(lane_head == 0, grad_kv[:COVER], 0.0)
        for h in range(1, GROUP):
            both = jnp.where(lane_head == h, grad_kv[h * COVER : (h + 1) * COVER], both)
        both = both.astype(BF16)
        gk_ref[here, cols] += both[:, :lanes]
        gv_ref[here, cols] += both[:, lanes:]

    @pl.when(step == last)
    def _():
        for g in range(groups):

            def unshift(o, acc):
                turned = pltpu.roll(ds_s[o, g], COVER - o, 0)
                return acc + pltpu.roll(turned, GROUP * COVER - o, 1)

            full = lax.fori_loop(0, TILE, unshift, jnp.zeros((COVER, GROUP * COVER), F32))
            for h in range(GROUP):
                base_s[g * GROUP + h] = full[:, h * COVER : (h + 1) * COVER]
        grad = jnp.zeros(gtab_ref.shape, F32)
        for pair in range(idx_ref.shape[0]):
            row = idx_ref[pair : pair + 1, :]
            vals = jnp.concatenate([base_s[:, 2 * pair, :], base_s[:, 2 * pair + 1, :]], axis=1)
            onehot = index_onehot(row, grad.shape[1])
            high = vals.astype(BF16)
            grad = grad + dot_rt(high, onehot)
            grad = grad + dot_rt((vals - high.astype(F32)).astype(BF16), onehot)
        gtab_ref[...] = grad


def attn_back_rows(q, k, v, ga, att, p, idx, table_width, head_dim):
    rows, width = q.shape
    heads = width // head_dim
    steps, sets, groups, _, wide = p.shape
    row_out = jax.ShapeDtypeStruct((rows, width), BF16)
    return call(
        functools.partial(attn_back_kernel, head_dim),
        steps,
        (q, k, v, ga, att, p, idx),
        [whole((rows, width))] * 5
        + [
            pl.BlockSpec((1, sets, groups, COVER, wide), lambda i: (i, 0, 0, 0, 0)),
            whole(idx.shape),
        ],
        [row_out] * 3 + [jax.ShapeDtypeStruct((heads, table_width), F32)],
        [whole((rows, width))] * 3 + [whole((heads, table_width))],
        [
            pltpu.VMEM((TILE, groups, COVER, wide), F32),
            pltpu.VMEM((heads, COVER, COVER), F32),
            pltpu.VMEM((wide, GROUP * head_dim), BF16),
        ],
        2 * rows * width * 3 * width * 6,
        rows * width * 20,
    )


def dense_back_kernel(
    head_dim,
    gq_ref,
    gk_ref,
    gv_ref,
    mid_ref,
    merged_ref,
    gmid_ref,
    w_ref,
    x_ref,
    g1_ref,
    gm_ref,
    gqkv_ref,
    gqb_ref,
    gmerge_ref,
    sums_ref,
    wt_s,
):
    step = pl.program_id(0)
    width = mid_ref.shape[1]
    grad_refs = (gq_ref, gk_ref, gv_ref)

    @pl.when(step == 0)
    def _():
        shards, local = w_ref.shape[0], w_ref.shape[1] // (3 * head_dim)
        for s in range(shards):
            for l in range(local):
                for t in range(3):
                    at = t * width + (s * local + l) * head_dim
                    wt_s[at : at + head_dim, :] = w_ref[
                        s, (3 * l + t) * head_dim : (3 * l + t + 1) * head_dim, :
                    ]
        gqkv_ref[...] = jnp.zeros_like(gqkv_ref)
        gqb_ref[...] = jnp.zeros_like(gqb_ref)
        gmerge_ref[...] = jnp.zeros_like(gmerge_ref)
        sums_ref[...] = jnp.zeros_like(sums_ref)

    mid_t = mid_ref[...].T
    grad_mid = None
    for t in range(3):
        grad = grad_refs[t][...]
        gqkv_ref[:, t * width : (t + 1) * width] += dot(mid_t, grad)
        gqb_ref[:, t * width : (t + 1) * width] += jnp.sum(
            grad.astype(F32), axis=0, keepdims=True
        )
        part = dot(grad, wt_s[t * width : (t + 1) * width, :])
        grad_mid = part if grad_mid is None else grad_mid + part
    normed1, inverse1 = norm_parts(merged_ref[...])
    sums_ref[0:1, :] += jnp.sum(grad_mid * normed1, axis=0, keepdims=True)
    sums_ref[1:2, :] += jnp.sum(grad_mid, axis=0, keepdims=True)
    grad_merged = gmid_ref[...] + norm_back(grad_mid * g1_ref[...], normed1, inverse1)
    sums_ref[2:3, :] += jnp.sum(grad_merged, axis=0, keepdims=True)
    grad_merged = grad_merged.astype(BF16)
    gm_ref[...] = grad_merged
    normed0, _ = norm_parts(x_ref[...].astype(F32))
    gmerge_ref[...] += dot_lt(grad_merged, normed0.astype(BF16))


def dense_back_rows(gq, gk, gv, mid, merged, gmid, w, x, g1, head_dim):
    rows, width = mid.shape
    wide = x.shape[1]
    step = rows // 3
    row_block = pl.BlockSpec((step, width), lambda i: (i, 0))
    return call(
        functools.partial(dense_back_kernel, head_dim),
        3,
        (gq, gk, gv, mid, merged, gmid, w, x, g1),
        [row_block] * 6
        + [
            whole(w.shape),
            pl.BlockSpec((step, wide), lambda i: (i, 0)),
            whole(g1.shape),
        ],
        [
            jax.ShapeDtypeStruct((rows, width), BF16),
            jax.ShapeDtypeStruct((width, 3 * width), F32),
            jax.ShapeDtypeStruct((1, 3 * width), F32),
            jax.ShapeDtypeStruct((width, wide), F32),
            jax.ShapeDtypeStruct((8, width), F32),
        ],
        [
            row_block,
            whole((width, 3 * width)),
            whole((1, 3 * width)),
            whole((width, wide)),
            whole((8, width)),
        ],
        [pltpu.VMEM((3 * width, width), BF16)],
        2 * rows * width * (6 * width + wide),
        rows * width * 20,
    )


def input_back_kernel(gm_ref, wm_ref, x_ref, g0_ref, out_ref):
    grad_low = dot_rt(gm_ref[...], wm_ref[...])
    normed, inverse = norm_parts(x_ref[...].astype(F32))
    out_ref[...] = norm_back(grad_low * g0_ref[...], normed, inverse)


def input_back_rows(gm, wm, x, g0):
    rows, width = gm.shape
    wide = x.shape[1]
    step = rows // 7
    return call(
        input_back_kernel,
        7,
        (gm, wm, x, g0),
        [
            pl.BlockSpec((step, width), lambda i: (i, 0)),
            whole(wm.shape),
            pl.BlockSpec((step, wide), lambda i: (i, 0)),
            whole(g0.shape),
        ],
        jax.ShapeDtypeStruct((rows, wide), F32),
        pl.BlockSpec((step, wide), lambda i: (i, 0)),
        [],
        2 * rows * width * wide,
        rows * wide * 7,
    )


def swap(block, axis, bit, size):
    return lax.ppermute(block, axis, [(i, i ^ bit) for i in range(size)])


def bits_of(size):
    return [1 << i for i in range(size.bit_length() - 1)]


def gather_relative(own, axis, size):
    blocks = {0: own}
    for bit in reversed(bits_of(size)):
        have = sorted(blocks)
        sent = jnp.stack([blocks[r] for r in have])
        came = swap(sent, axis, bit, size)
        for i, r in enumerate(have):
            blocks[r ^ bit] = came[i]
    return jnp.stack([blocks[r] for r in range(size)])


def scatter_sum(parts, axis, size):
    held = parts
    for bit in bits_of(size):
        halves = held.reshape((held.shape[0] // 2, 2) + held.shape[1:])
        came = swap(halves[:, 1], axis, bit, size)
        held = halves[:, 0] + came
    return held[0]


def total_sum(block, axis, size):
    for bit in bits_of(size):
        block = block + swap(block, axis, bit, size)
    return block


def shards(
    inputs,
    norm0_gain,
    norm0_bias,
    merge_weight,
    norm1_gain,
    norm1_bias,
    qkv_weight,
    qkv_bias,
    rel_table,
    rel_index,
    regions,
    live_windows,
    proj_weight,
    proj_bias,
    norm2_gain,
    norm2_bias,
    up_weight,
    up_bias,
    down_weight,
    down_bias,
    cotangent,
    n_dp,
    n_mp,
):
    micro, strip_rows, wide = inputs.shape
    width = merge_weight.shape[1]
    win = rel_index.shape[0]
    local, packed = qkv_bias.shape
    head_dim = packed // 3
    heads = local * n_mp
    hidden = up_bias.shape[0]
    rel = rel_table.shape[1]
    rows = micro * strip_rows
    windows = rows // win
    sets = windows // TILE
    strip = lax.axis_index("mp")

    small = jnp.zeros((TILE, width), BF16)
    small = small.at[:local, :packed].set(qkv_bias)
    small = small.at[:local, packed : packed + rel].set(rel_table)
    small = small.at[local, :hidden].set(up_bias)
    first = jnp.concatenate(
        [jnp.transpose(qkv_weight, (1, 2, 0)).reshape(local * packed, width), small], axis=0
    )
    first = gather_relative(first, "mp", n_mp)
    second = jnp.concatenate(
        [proj_weight.reshape(local * head_dim, width), up_weight.T, down_weight], axis=0
    )
    second = gather_relative(second, "mp", n_mp)
    qkv_all = first[:, : local * packed]
    small_all = first[:, local * packed :].astype(F32)
    bias_all = small_all[:, :local, :packed].reshape(heads, 3, head_dim)
    bias_all = jnp.transpose(bias_all, (1, 0, 2)).reshape(1, 3 * width)
    table_width = -(-rel // 128) * 128
    table = small_all[:, :local, packed : packed + rel].reshape(heads, rel)
    table = jnp.pad(table, ((0, 0), (0, table_width - rel))).astype(BF16)
    up_bias_all = small_all[:, local, :hidden].reshape(n_mp, 1, hidden)
    proj_all = second[:, : local * head_dim].reshape(width, width)
    up_all = second[:, local * head_dim : local * head_dim + hidden]
    down_all = second[:, local * head_dim + hidden :]

    index = jnp.pad(rel_index, ((0, win % 2), (0, COVER - win)), constant_values=-1)
    index = index.reshape(-1, 2 * COVER)
    region = lax.dynamic_slice_in_dim(regions, strip * strip_rows, strip_rows, axis=1)
    region = jnp.pad(region.reshape(sets, TILE, win), ((0, 0), (0, 0), (0, COVER - win)))
    region = jnp.stack([jnp.roll(region[:, o], o, axis=1) for o in range(TILE)])
    region_col = region[..., None]
    region_row = jnp.tile(region[:, :, None, :], (1, 1, 1, GROUP))
    strip_windows = strip_rows // win
    limits = jnp.clip(live_windows[:, 0] - strip * strip_windows, 0, strip_windows) * win
    limits = limits.reshape(1, micro).astype(jnp.int32)

    x = inputs.reshape(rows, wide)
    merged, mid = merge_rows(
        x, norm0_gain[None], norm0_bias[None], merge_weight, norm1_gain[None], norm1_bias[None]
    )
    q, k, v, att, rinv, p = attn_rows(
        mid, qkv_all, bias_all, table, index, region_col, region_row, head_dim
    )
    vecs = jnp.stack([proj_bias, norm2_gain, norm2_bias, down_bias] + [down_bias] * 4)
    out, gmid, gatt, gffn, gub, gproj, sums2 = ffn_rows(
        limits,
        merged,
        att,
        cotangent.reshape(rows, width),
        rinv,
        proj_all,
        vecs,
        up_bias_all,
        up_all,
        down_all,
    )
    ffn_part = scatter_sum(gffn, "mp", n_mp)
    ffn_part = total_sum(ffn_part, "dp", n_dp).astype(F32)
    gq, gk, gv, gtab = attn_back_rows(q, k, v, gatt, att, p, index, table_width, head_dim)
    gm, gqkv, gqb, gmerge, sums1 = dense_back_rows(
        gq, gk, gv, mid, merged, gmid, qkv_all, x, norm1_gain[None], head_dim
    )
    grad_input = input_back_rows(gm, merge_weight, x, norm0_gain[None])

    gqkv = jnp.transpose(gqkv.astype(BF16).reshape(width, 3, heads, head_dim), (2, 1, 3, 0))
    gqkv = gqkv.reshape(n_mp, local * packed, width)
    gproj = gproj.astype(BF16).reshape(n_mp, local * head_dim, width)
    gqb = jnp.transpose(gqb.reshape(3, heads, head_dim), (1, 0, 2)).reshape(n_mp, local, packed)
    gtab = gtab[:, :rel].reshape(n_mp, local, rel)
    tail = jnp.zeros((n_mp, TILE, width), BF16)
    tail = tail.at[:, :local, :packed].set(gqb.astype(BF16))
    tail = tail.at[:, :local, packed : packed + rel].set(gtab.astype(BF16))
    tail = tail.at[:, local, :hidden].set(gub[:, 0].astype(BF16))
    part = jnp.concatenate([gqkv, gproj, tail], axis=1)
    part = total_sum(scatter_sum(part, "mp", n_mp), "dp", n_dp).astype(F32)
    gqkv = jnp.transpose(part[: local * packed].reshape(local, packed, width), (2, 0, 1))
    gproj = part[local * packed : local * (packed + head_dim)].reshape(local, head_dim, width)
    tail = part[local * (packed + head_dim) :]
    sums = jnp.concatenate([sums2[:4], sums1[:4]], axis=0)
    sums = total_sum(total_sum(sums, "mp", n_mp), "dp", n_dp)
    gmerge = total_sum(total_sum(gmerge.astype(BF16), "mp", n_mp), "dp", n_dp)
    gmerge = gmerge.astype(F32).T
    low_sum = sums[6]
    wide_weight = merge_weight.astype(F32)
    grad_gain0 = jnp.sum(wide_weight * gmerge, axis=1)
    grad_bias0 = jnp.sum(wide_weight * low_sum[None], axis=1)
    gmerge = gmerge * norm0_gain[:, None] + norm0_bias[:, None] * low_sum[None]
    return (
        out.reshape(micro, strip_rows, width),
        grad_input.reshape(micro, strip_rows, wide),
        grad_gain0,
        grad_bias0,
        gmerge,
        sums[4],
        sums[5],
        gqkv,
        tail[:local, :packed],
        tail[:local, packed : packed + rel],
        gproj,
        sums[0],
        sums[1],
        sums[2],
        ffn_part[:, :hidden],
        tail[local, :hidden],
        ffn_part[:, hidden:].T,
        sums[3],
    )


def solution(mesh):
    placed = (
        P(None, ("dp", "mp"), None),
        P(),
        P(),
        P(),
        P(),
        P(),
        P(None, "mp", None),
        P("mp", None),
        P("mp", None),
        P(),
        P(None, "dp"),
        P(None, "dp"),
        P("mp", None, None),
        P(),
        P(),
        P(),
        P(None, "mp"),
        P("mp"),
        P("mp", None),
        P(),
        P(None, ("dp", "mp"), None),
    )
    return jax.shard_map(
        functools.partial(shards, n_dp=mesh.shape["dp"], n_mp=mesh.shape["mp"]),
        mesh=mesh,
        in_specs=placed,
        out_specs=(
            P(None, ("dp", "mp"), None),
            P(None, ("dp", "mp"), None),
            P(),
            P(),
            P(),
            P(),
            P(),
            P(None, "mp", None),
            P("mp", None),
            P("mp", None),
            P("mp", None, None),
            P(),
            P(),
            P(),
            P(None, "mp"),
            P("mp"),
            P("mp", None),
            P(),
        ),
        check_vma=False,
    )
```

```python
import functools
import math

import jax
import jax.numpy as jnp
from jax import lax
from jax.experimental import pallas as pl
from jax.experimental.pallas import tpu as pltpu
from jax.sharding import PartitionSpec as P

F32 = jnp.float32
BF16 = jnp.bfloat16
EPSILON = 1e-05
MASKED = -1e30
COVER = 64
TILE = 16
GROUP = 4
VMEM_LIMIT = 60 << 20


def dot(left, right):
    return jnp.dot(left, right, preferred_element_type=F32)


def dot_rt(left, right):
    return lax.dot_general(left, right, (((1,), (1,)), ((), ())), preferred_element_type=F32)


def dot_lt(left, right):
    return lax.dot_general(left, right, (((0,), (0,)), ((), ())), preferred_element_type=F32)


def whole(shape):
    return pl.BlockSpec(shape, lambda i: (0,) * len(shape), pipeline_mode=pl.Buffered(1))


def anywhere():
    return pl.BlockSpec(memory_space=pl.ANY)


def call(kernel, grid, ins, in_specs, outs, out_specs, scratch, flops, nbytes, group=None):
    extra = {} if group is None else {"collective_id": group, "has_side_effects": True}
    return pl.pallas_call(
        kernel,
        grid=(grid,),
        in_specs=in_specs,
        out_specs=out_specs,
        out_shape=outs,
        scratch_shapes=scratch,
        compiler_params=pltpu.CompilerParams(
            dimension_semantics=("arbitrary",), vmem_limit_bytes=VMEM_LIMIT, **extra
        ),
        cost_estimate=pl.CostEstimate(flops=flops, bytes_accessed=nbytes, transcendentals=0),
    )(*ins)


def partner(axis, flips):
    at = lax.axis_index(axis)
    bit = 1
    while bit <= flips:
        if flips & bit:
            at = at + bit * (1 - 2 * lax.rem(lax.div(at, jnp.int32(bit)), jnp.int32(2)))
        bit *= 2
    return at


def send(axis, flips, src, dst, send_sem, recv_sem):
    return pltpu.make_async_remote_copy(
        src_ref=src,
        dst_ref=dst,
        send_sem=send_sem,
        recv_sem=recv_sem,
        device_id={axis: partner(axis, flips)},
        device_id_type=pl.DeviceIdType.MESH,
    )


def greet(peers):
    barrier = pltpu.get_barrier_semaphore()
    for axis, flips in peers:
        pl.semaphore_signal(
            barrier,
            inc=1,
            device_id={axis: partner(axis, flips)},
            device_id_type=pl.DeviceIdType.MESH,
        )
    pl.semaphore_wait(barrier, len(peers))


class Gather:
    def __init__(self, axis, size, own, held, send_sems, recv_sems, own_sem):
        self.axis, self.size, self.own, self.held = axis, size, own, held
        self.send_sems, self.recv_sems, self.own_sem = send_sems, recv_sems, own_sem

    def straight(self, r):
        return send(
            self.axis, r, self.own, self.held.at[r], self.send_sems.at[r], self.recv_sems.at[r]
        )

    def onward(self, r):
        return send(
            self.axis,
            1,
            self.held.at[r],
            self.held.at[r + 1],
            self.send_sems.at[r + 1],
            self.recv_sems.at[r + 1],
        )

    def keep(self):
        return pltpu.make_async_copy(self.own, self.held.at[0], self.own_sem)

    def start(self):
        for r in list(range(2, self.size, 2)) + [1]:
            self.straight(r).start()
        self.keep().start()

    def forward(self, r):
        self.straight(r).wait_recv()
        self.onward(r).start()

    def finish(self):
        self.keep().wait()
        self.straight(1).wait()
        for r in range(2, self.size, 2):
            self.straight(r).wait_send()
            self.onward(r).wait()


def spans(total, step):
    return [(start, min(step, total - start)) for start in range(0, total, step)]


def norm_parts(values):
    mean = jnp.mean(values, axis=-1, keepdims=True)
    center = values - mean
    spread = jnp.mean(center * center, axis=-1, keepdims=True) + EPSILON
    inverse = lax.rsqrt(spread)
    return center * inverse, mean, inverse, spread


def norm_back(grad, normed, inverse):
    mean_grad = jnp.mean(grad, axis=-1, keepdims=True)
    mean_cross = jnp.mean(grad * normed, axis=-1, keepdims=True)
    return inverse * (grad - mean_grad - normed * mean_cross)


def head_mask(head_dim):
    rows = lax.broadcasted_iota(jnp.int32, (GROUP * COVER, GROUP * head_dim), 0) // COVER
    cols = lax.broadcasted_iota(jnp.int32, (GROUP * COVER, GROUP * head_dim), 1) // head_dim
    return (rows == cols).astype(F32).astype(BF16)


def tiled(block, mask):
    return jnp.concatenate([block] * GROUP, axis=0) * mask


def pair_row(idx_ref, pair):
    win = idx_ref.shape[0]
    gap = jnp.full((1, COVER - win), -1, jnp.int32)
    parts = []
    for i in (2 * pair, 2 * pair + 1):
        parts.append(idx_ref[i : i + 1, :] if i < win else jnp.full((1, win), -1, jnp.int32))
        parts.append(gap)
    return jnp.concatenate(parts, axis=1)


def index_onehot(row, table_width):
    entry = lax.broadcasted_iota(jnp.int32, (table_width, row.shape[1]), 0)
    return (entry == row).astype(F32).astype(BF16)


def fill(x, width):
    return jnp.concatenate([x, jnp.zeros((x.shape[0], width - x.shape[1]), x.dtype)], axis=1)


def front_kernel(
    head_dim,
    local,
    size,
    merge_steps,
    x_ref,
    g0_ref,
    b0_ref,
    wm_ref,
    g1_ref,
    b1_ref,
    qkvw_ref,
    qkvb_ref,
    tab_ref,
    ub_ref,
    up_ref,
    down_ref,
    proj_ref,
    idx_ref,
    rid_ref,
    stats_ref,
    n1_ref,
    q_ref,
    k_ref,
    v_ref,
    att_ref,
    rinv_ref,
    p_ref,
    tiles_ref,
    wt_ref,
    second_ref,
    first_s,
    tiles_s,
    own_s,
    tile_s,
    second_s,
    mid_s,
    q_s,
    k_s,
    v_s,
    att_s,
    rinv_s,
    base_s,
    bias_s,
    mask_s,
    tile_send,
    tile_recv,
    first_send,
    first_recv,
    second_send,
    second_recv,
    own_sems,
    out_sems,
):
    step = pl.program_id(0)
    rows, width = mid_s.shape
    heads = width // head_dim
    lanes = GROUP * head_dim
    groups = heads // GROUP
    per_group = size // groups
    scale = 1.0 / math.sqrt(head_dim)
    span = local * head_dim
    evens = list(range(2, size, 2))
    main = Gather("mp", size, own_s, first_s, first_send, first_recv, own_sems.at[0])
    rest = Gather("mp", size, second_s, second_ref, second_send, second_recv, own_sems.at[1])

    def tile_copy(r):
        return send("mp", r, tile_s, tiles_s.at[r], tile_send.at[r], tile_recv.at[r])

    @pl.when(step == 0)
    def _():
        own_s[...] = qkvw_ref[...].T
        bias = qkvb_ref[...].astype(F32)
        lines = []
        for t in range(3):
            parts = [
                bias[l : l + 1, t * head_dim : (t + 1) * head_dim] for l in range(local)
            ]
            lines.append(fill(jnp.concatenate(parts, axis=1), width))
        lines.append(fill(tab_ref[...].astype(F32), width))
        lines.append(fill(ub_ref[...].astype(F32), width))
        lines.append(jnp.zeros((TILE - 4 - local, width), F32))
        tile_s[...] = jnp.concatenate(lines, axis=0).astype(BF16)
        greet([("mp", r) for r in range(1, size)])
        for r in range(1, size):
            tile_copy(r).start()
        tiles_s[0] = tile_s[...]
        main.start()
        hidden = up_ref.shape[1]
        second_s[:hidden, :] = up_ref[...].T
        second_s[hidden : 2 * hidden, :] = down_ref[...]
        second_s[2 * hidden :, :] = proj_ref[...]

    @pl.when(step == merge_steps - 1)
    def _():
        rest.start()

    @pl.when(step < merge_steps)
    def _():
        count = x_ref.shape[0]
        here = pl.ds(pl.multiple_of(step * count, TILE), count)
        normed, mean, inverse, _ = norm_parts(x_ref[...].astype(F32))
        normed_in = (normed * g0_ref[...] + b0_ref[...]).astype(BF16)
        normed1, mean1, inverse1, spread1 = norm_parts(dot(normed_in, wm_ref[...]))
        n1_ref[...] = normed1.astype(BF16)
        stats = [mean, inverse, mean1, inverse1, spread1 * inverse1]
        stats_ref[...] = jnp.concatenate(stats + [mean] * (8 - len(stats)), axis=1)
        mid_s[here, :] = (normed1 * g1_ref[...] + b1_ref[...]).astype(BF16)

    table_step = merge_steps - 3

    @pl.when(step == table_step)
    def _():
        mask_s[...] = head_mask(head_dim)
        att_s[...] = jnp.zeros_like(att_s)
        rinv_s[...] = jnp.zeros_like(rinv_s)
        base_s[...] = jnp.full(base_s.shape, MASKED, F32)
        for r in range(1, size):
            tile_copy(r).wait_recv()

    all_pairs = list(range((idx_ref.shape[0] + 1) // 2))
    for i in range(2):

        @pl.when(step == table_step + i)
        def _():
            table = jnp.concatenate(
                [tiles_s[r].astype(F32)[3 : 3 + local, : 2 * 128] for r in range(size)], axis=0
            ).astype(BF16)
            here = all_pairs[i::2]
            rows_of = [pair_row(idx_ref, pair) for pair in here]
            found = [dot(table, index_onehot(row, table.shape[1])) for row in rows_of]
            found = [jnp.where(row < 0, MASKED, x) for row, x in zip(rows_of, found)]
            for pair, vals in zip(here, found):
                base_s[:, 2 * pair, :] = vals[:, :COVER]
                base_s[:, 2 * pair + 1, :] = vals[:, COVER:]

    @pl.when(step == table_step + 2)
    def _():
        tiles_ref[...] = tiles_s[...]

        def shift(g, _):
            full = jnp.concatenate([base_s[g * GROUP + h] for h in range(GROUP)], axis=1)
            for o in range(TILE):
                bias_s[g, o] = pltpu.roll(pltpu.roll(full, o, 0), o, 1) if o else full
            return 0

        lax.fori_loop(0, groups, shift, 0)
        for r in range(1, size):
            tile_copy(r).wait_send()

    def outward(ref, out, which, g):
        cols = pl.ds(pl.multiple_of(g * lanes, lanes), lanes)
        return pltpu.make_async_copy(ref.at[:, cols], out.at[:, cols], out_sems.at[which, g])

    def early_out(g):
        return [
            outward(ref, out, i, g)
            for i, (ref, out) in enumerate(((q_s, q_ref), (k_s, k_ref), (v_s, v_ref)))
        ]

    def late_out(g):
        return [outward(att_s, att_ref, 3, g), outward(rinv_s, rinv_ref, 4, g)]

    low_half = lax.broadcasted_iota(jnp.int32, (COVER, 2 * COVER), 1) < COVER
    region_of = lax.broadcasted_iota(jnp.int32, (8, GROUP * COVER), 0)
    sets = rid_ref.shape[1]
    block = rows // sets

    def attend(it, g):
        mask = mask_s[...]
        cols = pl.ds(pl.multiple_of(g * lanes, lanes), lanes)
        units = [(2 * it + i, u) for i in range(2) for u in range(sets)]
        starts = [pl.multiple_of(o * (block // TILE - 1) + u * block, TILE) for o, u in units]
        scores = []
        for start in starts:
            here = pl.ds(start, COVER)
            scores.append(dot_rt(q_s[here, cols], tiled(k_s[here, cols], mask)))
        weights = []
        for (o, u), s in zip(units, scores):
            member = (region_of == rid_ref[o, u]).astype(F32).astype(BF16)
            same = dot_lt(member[:, :COVER], member)
            s = s + bias_s[g, o] + jnp.where(same > 0.5, 0.0, MASKED)
            parts = []
            for c in range(GROUP // 2):
                x = s[:, c * 2 * COVER : (c + 1) * 2 * COVER]
                top0 = jnp.max(jnp.where(low_half, x, MASKED), axis=1, keepdims=True)
                top1 = jnp.max(jnp.where(low_half, MASKED, x), axis=1, keepdims=True)
                top = jnp.maximum(jnp.where(low_half, top0, top1), MASKED * 0.1)
                parts.append(jnp.exp(x - top).astype(BF16))
            w = jnp.concatenate(parts, axis=1)
            p_ref[0, o, u] = w
            weights.append(w)
        mixed = []
        for start, w in zip(starts, weights):
            vals = tiled(v_s[pl.ds(start, COVER), cols], mask)
            mixed.append(dot(w, jnp.concatenate([vals, mask], axis=1)))
        for start, a in zip(starts, mixed):
            here = pl.ds(start, COVER)
            total = a[:, lanes:]
            inv = jnp.where(total > 0.0, 1.0 / jnp.maximum(total, 0.5), 0.0)
            att_s[here, cols] += (a[:, :lanes] * inv).astype(BF16)
            rinv_s[here, cols] += inv.astype(BF16)

    @pl.when(step >= merge_steps)
    def _():
        g = step - merge_steps
        twice = 2 * per_group

        @pl.when(g == 0)
        def _():
            main.keep().wait()
            for r in evens:
                if r < twice:
                    main.forward(r)
            main.straight(1).wait_recv()
            for r in evens:
                if r < twice:
                    main.onward(r).wait_recv()

        for known in range(2, groups, 2):

            @pl.when(g == known)
            def _():
                for r in evens:
                    if known * per_group <= r < known * per_group + twice:
                        main.onward(r).wait_recv()

        @pl.when(g % 2 == 0)
        def _():
            shards = [g * per_group + j for j in range(twice)]
            cols = pl.ds(pl.multiple_of(g * lanes, 2 * lanes), 2 * lanes)
            outs = (q_s, k_s, v_s)
            part = rows // 3
            weights, biases = [], []
            for t in range(3):
                weight = []
                for s in shards:
                    for l in range(local):
                        at = (3 * l + t) * head_dim
                        weight.append(first_s[s, at : at + head_dim, :])
                    biases.append(tiles_s[s].astype(F32)[t : t + 1, :span])
                weight = jnp.concatenate(weight, axis=0)
                spot = pl.ds(pl.multiple_of(t * width + g * lanes, 2 * lanes), 2 * lanes)
                wt_ref[spot, :] = weight
                weights.append(weight.T)
            weight = jnp.concatenate(weights, axis=1)
            bias = jnp.concatenate(biases, axis=1)

            def project(i, _):
                here = pl.ds(pl.multiple_of(i * part, TILE), part)
                y = dot(mid_s[here, :], weight) + bias
                for t in range(3):
                    z = y[:, 2 * t * lanes : 2 * (t + 1) * lanes]
                    outs[t][here, cols] = (z * scale if t == 0 else z).astype(BF16)
                return 0

            lax.fori_loop(0, 3, project, 0)

        for c in early_out(g):
            c.start()

        def run(it, _):
            attend(it, g)
            return 0

        lax.fori_loop(0, TILE // 4, run, 0)

        @pl.when(g == 0)
        def _():
            for r in evens:
                if r >= twice:
                    main.forward(r)

        @pl.when(g == groups - 1)
        def _():
            for r in evens:
                rest.forward(r)

        lax.fori_loop(TILE // 4, TILE // 2, run, 0)
        for c in late_out(g):
            c.start()

        @pl.when(g == groups - 1)
        def _():
            main.straight(1).wait_send()
            for r in evens:
                main.straight(r).wait_send()
                main.onward(r).wait_send()
            rest.finish()
            for known in range(groups):
                for c in early_out(known) + late_out(known):
                    c.wait()


def front_rows(
    x, g0, b0, wm, g1, b1, qkvw, qkvb, tab, ub, up, down, proj, idx, rid, size, head_dim
):
    rows, wide = x.shape
    width = wm.shape[1]
    local = qkvb.shape[0]
    hidden = up.shape[1]
    heads = width // head_dim
    groups = heads // GROUP
    offsets, sets = rid.shape[0], rid.shape[1]
    cover = GROUP * COVER
    merge_steps = 7
    step = rows // merge_steps
    first = (3 * local * head_dim, width)
    second = (2 * hidden + local * head_dim, width)

    def place(i):
        return (jnp.minimum(i, merge_steps - 1), 0)

    def group_place(i):
        return (jnp.maximum(i - merge_steps, 0), 0, 0, 0, 0)

    small = [g0, b0, wm, g1, b1, qkvw, qkvb, tab, ub, up, down, proj, idx, rid]
    row_out = jax.ShapeDtypeStruct((rows, width), BF16)
    sems = [pltpu.SemaphoreType.DMA((size,))] * 6
    return call(
        functools.partial(front_kernel, head_dim, local, size, merge_steps),
        merge_steps + groups,
        [x] + small,
        [pl.BlockSpec((step, wide), place)] + [whole(a.shape) for a in small],
        [jax.ShapeDtypeStruct((rows, 8), F32), row_out]
        + [row_out] * 5
        + [
            jax.ShapeDtypeStruct((groups, offsets, sets, COVER, cover), BF16),
            jax.ShapeDtypeStruct((size, TILE, width), BF16),
            jax.ShapeDtypeStruct((3 * width, width), BF16),
            jax.ShapeDtypeStruct((size,) + second, BF16),
        ],
        [pl.BlockSpec((step, 8), place), pl.BlockSpec((step, width), place)]
        + [anywhere()] * 5
        + [
            pl.BlockSpec((1, offsets, sets, COVER, cover), group_place),
            whole((size, TILE, width)),
            whole((3 * width, width)),
            anywhere(),
        ],
        [
            pltpu.VMEM((size,) + first, BF16),
            pltpu.VMEM((size, TILE, width), BF16),
            pltpu.VMEM(first, BF16),
            pltpu.VMEM((TILE, width), BF16),
            pltpu.VMEM(second, BF16),
        ]
        + [pltpu.VMEM((rows, width), BF16)] * 6
        + [
            pltpu.VMEM((heads, COVER, COVER), F32),
            pltpu.VMEM((groups, TILE, COVER, cover), F32),
            pltpu.VMEM((cover, GROUP * head_dim), BF16),
        ]
        + sems
        + [pltpu.SemaphoreType.DMA((2,)), pltpu.SemaphoreType.DMA((5, groups))],
        2 * rows * width * (wide + 18 * width),
        rows * width * 40,
        group=0,
    )


def gelu_parts(x):
    under = 1.0 + (0.3275911 / math.sqrt(2.0)) * jnp.abs(x)
    t = pl.reciprocal(under, approx=True)
    t = t * (2.0 - under * t)
    bell = jnp.exp(-0.5 * (x * x))
    poly = 0.5 * 1.061405429 * t + 0.5 * -1.453152027
    poly = poly * t + 0.5 * 1.421413741
    poly = poly * t + 0.5 * -0.284496736
    poly = poly * t + 0.5 * 0.254829592
    tail = poly * t * bell
    cdf = jnp.where(x > 0.0, 1.0 - tail, tail)
    return cdf, x * bell * (1.0 / math.sqrt(2.0 * math.pi))


def live_rows(live_ref, start, count, rows, width, window):
    micro = live_ref.shape[0]
    micro_rows = rows // micro
    before = lax.axis_index("mp") * micro_rows
    row = lax.broadcasted_iota(jnp.int32, (count, width), 0) + start
    live = None
    for m in range(micro):
        last = m * micro_rows + jnp.minimum(live_ref[m, 0] * window - before, micro_rows)
        inside = (row >= m * micro_rows) & (row < last)
        live = inside if live is None else live | inside
    return live


def ffn_kernel(
    local,
    window,
    live_ref,
    n1_ref,
    att_ref,
    cot_ref,
    stats_ref,
    wp_ref,
    pb_ref,
    g2_ref,
    b2_ref,
    db_ref,
    tail_ref,
    up_ref,
    down_ref,
    base_ref,
    act_ref,
    gmid_ref,
    gatt_ref,
    part_ref,
    gub_ref,
    gproj_ref,
    sums_ref,
    base_s,
    gffn_s,
    att_s,
    n2_s,
    inv_s,
    n_s,
    go_s,
    nt_s,
    gt_s,
    act_s,
    gp_s,
    odd_s,
    even_s,
    near_s,
    far_s,
    near_send,
    near_recv,
    far_send,
    far_recv,
    in_sems,
    out_sems,
    act_sem,
):
    step = pl.program_id(0)
    pairs = even_s.shape[0]
    pair = pairs - 1 - step
    rows, width = gffn_s.shape
    blocks = spans(rows, 384)
    hidden = up_ref.shape[1]
    wp = wp_ref[...].reshape(width, width)

    def near(p):
        return send("mp", 1, odd_s.at[p % 2], near_s.at[p], near_send.at[p], near_recv.at[p])

    def far(p):
        slot = far_s.at[p - 1]
        return send("mp", 2 * p, even_s.at[p], slot, far_send.at[p], far_recv.at[p])

    def bring(b):
        here = pl.ds(*blocks[b])
        whence = ((n1_ref, n_s), (att_ref, att_s), (cot_ref, go_s))
        return [
            pltpu.make_async_copy(src.at[here], dst.at[here], in_sems.at[i, b])
            for i, (src, dst) in enumerate(whence)
        ]

    def take(which, b):
        here = pl.ds(*blocks[b])
        src, dst = ((base_s, base_ref), (go_s, gmid_ref), (n2_s, gatt_ref))[which]
        return pltpu.make_async_copy(src.at[here], dst.at[here], out_sems.at[which, b])

    def take_act():
        return pltpu.make_async_copy(act_s.at[pl.ds(0, rows)], act_ref.at[pair], act_sem)

    @pl.when(step == 0)
    def _():
        for b in range(len(blocks)):
            for c in bring(b):
                c.start()
        greet([("mp", r) for r in [1] + [2 * p for p in range(1, pairs)]])
        bias_proj, gain2, bias2, bias_down = (x[...] for x in (pb_ref, g2_ref, b2_ref, db_ref))
        act_s[rows:, :] = jnp.zeros_like(act_s[rows:, :])
        gp_s[rows:, :] = jnp.zeros_like(gp_s[rows:, :])
        down_sum = jnp.zeros((1, width), F32)
        for b, (start, count) in enumerate(blocks):
            here = pl.ds(start, count)
            for c in bring(b):
                c.wait()
            stats = stats_ref[here, :]
            merged = n_s[here, :].astype(F32) * stats[:, 4:5] + stats[:, 2:3]
            middle = merged + dot(att_s[here, :], wp) + bias_proj
            base_s[here, :] = (middle + bias_down).astype(BF16)
            take(0, b).start()
            normed, _, inverse, _ = norm_parts(middle)
            n2_s[here, :] = normed.astype(BF16)
            inv_s[here, :] = jnp.broadcast_to(inverse, (count, inv_s.shape[1]))
            normed_ffn = (normed * gain2 + bias2).astype(BF16)
            n_s[here, :] = normed_ffn
            live = live_rows(live_ref, start, count, rows, width, window)
            grad_out = jnp.where(live, go_s[here, :].astype(F32), 0.0)
            down_sum = down_sum + jnp.sum(grad_out, axis=0, keepdims=True)
            grad_low = grad_out.astype(BF16)
            go_s[here, :] = grad_low
            whole_count = -(-count // 128) * 128
            if whole_count != count:
                filler = jnp.zeros((whole_count - count, width), BF16)
                normed_ffn = jnp.concatenate([normed_ffn, filler], axis=0)
                grad_low = jnp.concatenate([grad_low, filler], axis=0)
            nt_s[:, start : start + whole_count] = normed_ffn.T
            gt_s[:, start : start + whole_count] = grad_low.T
        sums_ref[...] = jnp.zeros_like(sums_ref)
        sums_ref[3:4, :] = down_sum
        gffn_s[...] = jnp.zeros_like(gffn_s)

    def pass_on():
        @pl.when(step > 0)
        def _():
            near(pair + 1).wait_recv()
            joined = even_s[pair + 1].astype(F32) + near_s[pair + 1].astype(F32)
            even_s[pair + 1] = joined.astype(BF16)

        for p in range(1, pairs):

            @pl.when(pair + 1 == p)
            def _():
                far(p).start()

    up_t = up_ref[...].reshape(2 * hidden, width)
    down = down_ref[...].reshape(2 * hidden, width)
    up_bias = jnp.concatenate(
        [tail_ref[i].astype(F32)[3 + local : 4 + local, :hidden] for i in range(2)], axis=1
    )
    up_sum = jnp.zeros((1, 2 * hidden), F32)
    for b, (start, count) in enumerate(blocks):
        if b == 1:
            pass_on()
        here = pl.ds(start, count)
        pre = dot_rt(n_s[here, :], up_t) + up_bias
        cdf, slope = gelu_parts(pre)
        act = (pre * cdf).astype(BF16)
        grad_pre = dot_rt(go_s[here, :], down) * (cdf + slope)
        up_sum = up_sum + jnp.sum(grad_pre, axis=0, keepdims=True)
        grad_pre = grad_pre.astype(BF16)
        act_s[here, :] = act
        gp_s[here, :] = grad_pre
        gffn_s[here, :] += dot(grad_pre, up_t)
    take_act().start()
    gub_ref[0] = up_sum

    @pl.when(step > 1)
    def _():
        near(pair + 2).wait_send()

    grad_up = dot(nt_s[...], gp_s[...]).astype(BF16)
    even_s[pair, :, :hidden] = grad_up[:, :hidden]
    odd_s[pair % 2, :, :hidden] = grad_up[:, hidden:]
    grad_down = dot(gt_s[...], act_s[...]).astype(BF16)
    even_s[pair, :, hidden:] = grad_down[:, :hidden]
    odd_s[pair % 2, :, hidden:] = grad_down[:, hidden:]
    near(pair).start()
    take_act().wait()

    @pl.when(step == pairs - 1)
    def _():
        gain2 = g2_ref[...]
        gain_sum = jnp.zeros((1, width), F32)
        bias_sum = jnp.zeros((1, width), F32)
        proj_sum = jnp.zeros((1, width), F32)
        grad_proj = jnp.zeros((width, width), F32)
        for b, (start, count) in enumerate(blocks):
            here = pl.ds(start, count)
            grad_ffn = gffn_s[here, :]
            normed = n2_s[here, :].astype(F32)
            gain_sum = gain_sum + jnp.sum(grad_ffn * normed, axis=0, keepdims=True)
            bias_sum = bias_sum + jnp.sum(grad_ffn, axis=0, keepdims=True)
            grad_middle = go_s[here, :].astype(F32) + norm_back(
                grad_ffn * gain2, normed, inv_s[here, :1]
            )
            proj_sum = proj_sum + jnp.sum(grad_middle, axis=0, keepdims=True)
            grad_attn = grad_middle.astype(BF16)
            go_s[here, :] = grad_attn
            take(1, b).start()
            grad_proj = grad_proj + dot_lt(att_s[here, :], grad_attn)
            n2_s[here, :] = dot_rt(grad_attn, wp).astype(BF16)
            take(2, b).start()
        gproj_ref[...] = grad_proj.astype(BF16)
        sums_ref[0:1, :] = proj_sum
        sums_ref[1:2, :] = gain_sum
        sums_ref[2:3, :] = bias_sum
        near(0).wait_recv()
        total = even_s[0].astype(F32) + near_s[0].astype(F32)
        for p in range(1, pairs):
            far(p).wait_recv()
            total = total + far_s[p - 1].astype(F32)
        part_ref[...] = total.astype(BF16)
        for p in range(pairs):
            if p < 2:
                near(p).wait_send()
            if p:
                far(p).wait_send()
        for b in range(len(blocks)):
            for which in range(3):
                take(which, b).wait()


def ffn_rows(live, n1, att, cot, stats, tiles, second, vecs, local, hidden, window):
    rows, width = n1.shape
    size = tiles.shape[0]
    pairs = size // 2
    padded = -(-rows // 128) * 128
    proj_rows = width // size
    proj_at = 2 * hidden // proj_rows
    blocks = len(spans(rows, 384))
    row_out = jax.ShapeDtypeStruct((rows, width), BF16)
    return call(
        functools.partial(ffn_kernel, local, window),
        pairs,
        (live, n1, att, cot, stats, second) + vecs + (tiles, second, second),
        [
            pl.BlockSpec(memory_space=pltpu.SMEM),
            anywhere(),
            anywhere(),
            anywhere(),
            whole(stats.shape),
            pl.BlockSpec(
                (size, proj_rows, width),
                lambda i: (0, proj_at, 0),
                pipeline_mode=pl.Buffered(1),
            ),
        ]
        + [whole((1, width))] * 4
        + [
            pl.BlockSpec((2, TILE, width), lambda i: (pairs - 1 - i, 0, 0)),
            pl.BlockSpec((2, hidden, width), lambda i: (pairs - 1 - i, 0, 0)),
            pl.BlockSpec((2, hidden, width), lambda i: (pairs - 1 - i, 1, 0)),
        ],
        [
            row_out,
            jax.ShapeDtypeStruct((pairs, rows, 2 * hidden), BF16),
            row_out,
            row_out,
            jax.ShapeDtypeStruct((width, 2 * hidden), BF16),
            jax.ShapeDtypeStruct((pairs, 1, 2 * hidden), F32),
            jax.ShapeDtypeStruct((width, width), BF16),
            jax.ShapeDtypeStruct((8, width), F32),
        ],
        [
            anywhere(),
            anywhere(),
            anywhere(),
            anywhere(),
            whole((width, 2 * hidden)),
            pl.BlockSpec((1, 1, 2 * hidden), lambda i: (pairs - 1 - i, 0, 0)),
            whole((width, width)),
            whole((8, width)),
        ],
        [
            pltpu.VMEM((rows, width), BF16),
            pltpu.VMEM((rows, width), F32),
            pltpu.VMEM((rows, width), BF16),
            pltpu.VMEM((rows, width), BF16),
            pltpu.VMEM((rows, 128), F32),
            pltpu.VMEM((rows, width), BF16),
            pltpu.VMEM((rows, width), BF16),
            pltpu.VMEM((width, padded), BF16),
            pltpu.VMEM((width, padded), BF16),
            pltpu.VMEM((padded, 2 * hidden), BF16),
            pltpu.VMEM((padded, 2 * hidden), BF16),
        ]
        + [pltpu.VMEM((min(pairs, 2), width, 2 * hidden), BF16)]
        + [pltpu.VMEM((pairs, width, 2 * hidden), BF16)] * 2
        + [pltpu.VMEM((max(pairs - 1, 1), width, 2 * hidden), BF16)]
        + [pltpu.SemaphoreType.DMA((pairs,))] * 4
        + [pltpu.SemaphoreType.DMA((3, blocks))] * 2
        + [pltpu.SemaphoreType.DMA(())],
        2 * rows * width * hidden * size * 6,
        rows * width * 20,
        group=1,
    )


LEVELS = 4
PARTS = 3


def back_kernel(
    head_dim,
    local,
    near_size,
    far_size,
    dense_steps,
    q_ref,
    k_ref,
    v_ref,
    ga_ref,
    rinv_ref,
    att_ref,
    n1_ref,
    wt_ref,
    p_ref,
    idx_ref,
    ffn_ref,
    gmid_ref,
    stats_ref,
    x_ref,
    g1_ref,
    b1_ref,
    gproj_ref,
    gub_ref,
    sums2_ref,
    act_ref,
    base_ref,
    second_ref,
    wm_ref,
    g0_ref,
    raw_ref,
    gin_ref,
    ffnsum_ref,
    main_ref,
    tail_ref,
    full_ref,
    sums_ref,
    q_s,
    k_s,
    v_s,
    ga_s,
    rinv_s,
    att_s,
    n1_s,
    wt_s,
    gq_s,
    gk_s,
    gv_s,
    ds_s,
    base_s,
    mask_s,
    gtab_s,
    ffncame_s,
    ffnown_s,
    merge_s,
    merged_s,
    mnear_s,
    mfar_s,
    mpiece_s,
    parts_s,
    pnear_s,
    pfar_s,
    main_s,
    mainsum_s,
    tails_s,
    linein_s,
    lineout_s,
    lines_s,
    n0_s,
    inv0_s,
    wm_s,
    down_s,
    in_sems,
    more_sems,
    late_sems,
    out_sems,
    sems,
):
    step = pl.program_id(0)
    rows, width = gq_s.shape
    lanes = GROUP * head_dim
    groups = width // lanes
    scale = 1.0 / math.sqrt(head_dim)
    sets = p_ref.shape[2]
    block = rows // sets
    jump = block // TILE - 1
    pairs = near_size // 2
    span = local * head_dim
    me, deep = lax.axis_index("mp"), lax.axis_index("dp")
    beside = list(range(1, near_size))
    behind = list(range(1, far_size))
    evens = list(range(2, near_size, 2))
    piece = ffnsum_ref.shape[1]
    at_sem = [0]

    def copy(axis, r, src, dst):
        at_sem[0] += 2
        return send(axis, r, src, dst, sems.at[at_sem[0] - 2], sems.at[at_sem[0] - 1])

    def rows_at(ref, index, count):
        return ref.at[pl.ds(pl.multiple_of(index * count, TILE), count)]

    def bring(level):
        copies = []
        whence = (
            (q_ref, q_s),
            (k_ref, k_s),
            (v_ref, v_s),
            (ga_ref, ga_s),
            (rinv_ref, rinv_s),
            (att_ref, att_s),
        )
        part = TILE // LEVELS * jump
        first = COVER - jump
        for i, (src, dst) in enumerate(whence):
            for u in range(sets):
                if level == 0:
                    here = pl.ds(u * block, part + first)
                else:
                    here = pl.ds(u * block + first + level * part, part)
                copies.append(
                    pltpu.make_async_copy(src.at[here], dst.at[here], in_sems.at[i, level, u])
                )
        return copies

    def bring_more():
        return [
            pltpu.make_async_copy(n1_ref, n1_s, more_sems.at[0]),
            pltpu.make_async_copy(wt_ref, wt_s, more_sems.at[1]),
        ]

    act_bufs = (k_s, v_s, ga_s, rinv_s)
    chunks = act_ref.shape[0] * act_ref.shape[2] // width

    def bring_late():
        copies = [(base_ref, att_s), (wm_ref, wm_s)]
        per = act_ref.shape[2]
        each = width // per
        for p in range(act_ref.shape[0]):
            dst = act_bufs[p // each].at[:, pl.ds(p % each * per, per)]
            copies.append((act_ref.at[p], dst))
        hidden = per // 2
        for r in range(near_size):
            src = second_ref.at[r, pl.ds(hidden, hidden)]
            copies.append((src, down_s.at[pl.ds(r * hidden, hidden)]))
        return [
            pltpu.make_async_copy(src, dst, late_sems.at[i]) for i, (src, dst) in enumerate(copies)
        ]

    def dense_span(j):
        return pl.ds(j * (rows // PARTS), rows // PARTS)

    def take_gin(j):
        here = dense_span(j)
        return pltpu.make_async_copy(n0_s.at[here], gin_ref.at[here], out_sems.at[0, j])

    def take_raw(j):
        here = dense_span(j)
        return pltpu.make_async_copy(att_s.at[here], raw_ref.at[here], out_sems.at[1, j])

    def input_part(j):
        here = dense_span(j)
        grad_low = dot_rt(q_s[here, :], wm_s[...])
        normed = n0_s[here, :].astype(F32)
        grad = norm_back(grad_low * g0_ref[...], normed, inv0_s[here, :1])
        n0_s[here, :] = grad.astype(BF16)
        take_gin(j).start()

    def output_part(j):
        here = dense_span(j)
        total = att_s[here, :].astype(F32)
        for i in range(chunks):
            total = total + dot(act_bufs[i][here, :], down_s[i * width : (i + 1) * width, :])
        att_s[here, :] = total.astype(BF16)
        take_raw(j).start()

    def keep_main():
        return pltpu.make_async_copy(mainsum_s, main_ref.at[deep], more_sems.at[3])

    def keep_merge():
        return pltpu.make_async_copy(mpiece_s.at[0], full_ref.at[me, deep], more_sems.at[4])

    def keep_ffn():
        return pltpu.make_async_copy(ffnown_s, ffnsum_ref.at[deep], more_sems.at[2])

    ffn_out = [
        copy("dp", r, rows_at(ffn_ref, partner("dp", r), piece), ffncame_s.at[r]) for r in behind
    ]
    ffn_all = [copy("dp", r, ffnown_s, ffnsum_ref.at[deep]) for r in behind]

    @pl.when(step == 0)
    def _():
        for level in range(LEVELS):
            for c in bring(level):
                c.start()
        for c in bring_more():
            c.start()
        greet([("mp", r) for r in beside] + [("dp", r) for r in behind])
        for c in ffn_out:
            c.start()
        mask_s[...] = head_mask(head_dim)
        gq_s[...] = jnp.zeros_like(gq_s)
        gk_s[...] = jnp.zeros_like(gk_s)
        gv_s[...] = jnp.zeros_like(gv_s)

    @pl.when(step == TILE // 2)
    def _():
        total = ffn_ref[pl.ds(pl.multiple_of(deep * piece, TILE), piece), :].astype(F32)
        for c, r in zip(ffn_out, behind):
            c.wait_recv()
            total = total + ffncame_s[r].astype(F32)
        ffnown_s[...] = total.astype(BF16)
        keep_ffn().start()
        for c in ffn_all:
            c.start()

    for level in range(LEVELS):

        @pl.when(step == level * (TILE // LEVELS))
        def _():
            for c in bring(level):
                c.wait()

    @pl.when(step < TILE)
    def _():
        mask = mask_s[...]
        minus = -mask
        starts = [pl.multiple_of(step * jump + u * block, TILE) for u in range(sets)]
        lane_head = lax.broadcasted_iota(jnp.int32, (COVER, 2 * lanes), 1) % lanes // head_dim
        zeros = jnp.zeros((COVER, lanes), BF16)
        units = [(u, g) for g in range(groups) for u in range(sets)]

        def at(ref, u, g):
            return ref[pl.ds(starts[u], COVER), pl.ds(g * lanes, lanes)]

        scaled = [at(ga_s, u, g) * at(rinv_s, u, g) for u, g in units]
        grads = []
        for (u, g), ga in zip(units, scaled):
            left = jnp.concatenate([ga, ga * at(att_s, u, g)], axis=1)
            right = jnp.concatenate([tiled(at(v_s, u, g), mask), minus], axis=1)
            grads.append(dot_rt(left, right))
        score_grads = []
        totals = {}
        for (u, g), grad in zip(units, grads):
            ds = p_ref[g, 0, u].astype(F32) * grad
            totals[g] = ds if g not in totals else totals[g] + ds
            score_grads.append(ds.astype(BF16))
        for g in range(groups):
            ds_s[step, g] = totals[g]
        query_grads = []
        for (u, g), ds in zip(units, score_grads):
            query_grads.append(dot(ds, tiled(at(k_s, u, g), mask)))
        pair_grads = []
        for (u, g), ds, ga in zip(units, score_grads, scaled):
            left = jnp.concatenate([ds, p_ref[g, 0, u]], axis=0)
            right = jnp.concatenate(
                [
                    jnp.concatenate([at(q_s, u, g), zeros], axis=1),
                    jnp.concatenate([zeros, ga], axis=1),
                ],
                axis=0,
            )
            pair_grads.append(dot_lt(left, right))
        for (u, g), grad_q, grad_kv in zip(units, query_grads, pair_grads):
            here, cols = pl.ds(starts[u], COVER), pl.ds(g * lanes, lanes)
            gq_s[here, cols] += (grad_q * scale).astype(BF16)
            both = jnp.where(lane_head == 0, grad_kv[:COVER], 0.0)
            for h in range(1, GROUP):
                both = jnp.where(lane_head == h, grad_kv[h * COVER : (h + 1) * COVER], both)
            both = both.astype(BF16)
            gk_s[here, cols] += both[:, :lanes]
            gv_s[here, cols] += both[:, lanes:]

    def table_grads():
        def unshift(g, _):
            full = ds_s[0, g]
            for o in range(1, TILE):
                turned = pltpu.roll(ds_s[o, g], COVER - o, 0)
                full = full + pltpu.roll(turned, GROUP * COVER - o, 1)
            for h in range(GROUP):
                base_s[g * GROUP + h] = full[:, h * COVER : (h + 1) * COVER]
            return 0

        lax.fori_loop(0, groups, unshift, 0)
        sums = []
        for pair in range((idx_ref.shape[0] + 1) // 2):
            onehot = index_onehot(pair_row(idx_ref, pair), gtab_s.shape[1])
            vals = jnp.concatenate([base_s[:, 2 * pair, :], base_s[:, 2 * pair + 1, :]], axis=1)
            high = vals.astype(BF16)
            both = jnp.concatenate([high, (vals - high.astype(F32)).astype(BF16)], axis=0)
            sums.append(dot_rt(both, onehot))
        count = base_s.shape[0]
        grad = sums[0]
        for x in sums[1:]:
            grad = grad + x
        gtab_s[...] = grad[:count] + grad[count:]

    @pl.when(step == TILE)
    def _():
        for c in bring_late():
            c.start()
        merge_s[...] = jnp.zeros_like(merge_s)
        lines_s[...] = jnp.zeros_like(lines_s)
        for c in bring_more():
            c.wait()

    @pl.when(step >= TILE)
    def _():
        count = gmid_ref.shape[0]
        here = pl.ds(pl.multiple_of((step - TILE) * count, TILE), count)
        grad_mid = None
        for t, ref in enumerate((gq_s, gk_s, gv_s)):
            part = dot(ref[here, :], wt_s[t * width : (t + 1) * width, :])
            grad_mid = part if grad_mid is None else grad_mid + part
        stats = stats_ref[...]
        normed1 = n1_s[here, :].astype(F32)
        lines_s[0:1, :] += jnp.sum(grad_mid * normed1, axis=0, keepdims=True)
        lines_s[1:2, :] += jnp.sum(grad_mid, axis=0, keepdims=True)
        grad_merged = gmid_ref[...].astype(F32) + norm_back(
            grad_mid * g1_ref[...], normed1, stats[:, 3:4]
        )
        lines_s[2:3, :] += jnp.sum(grad_merged, axis=0, keepdims=True)
        grad_merged = grad_merged.astype(BF16)
        q_s[here, :] = grad_merged
        normed0 = ((x_ref[...].astype(F32) - stats[:, 0:1]) * stats[:, 1:2]).astype(BF16)
        n0_s[here, :] = normed0
        inv0_s[here, :] = jnp.broadcast_to(stats[:, 1:2], (count, inv0_s.shape[1]))
        merge_s[...] += dot_lt(grad_merged, normed0)

    share = merged_s.shape[0] // near_size
    small = share // far_size
    main_rows = parts_s.shape[1] - TILE
    main_piece = main_rows // far_size
    mnear, mfar = [], {}
    for p in range(pairs):
        src = rows_at(merged_s, partner("mp", 2 * p + 1), share)
        mnear.append(copy("mp", 1, src, mnear_s.at[p]))
    for p in range(1, pairs):
        src = rows_at(merged_s, partner("mp", 2 * p), share)
        mfar[p] = copy("mp", 2 * p, src, mfar_s.at[p])
    lines_in = [copy("mp", r, linein_s.at[0], linein_s.at[r]) for r in beside]
    lines_out = [copy("dp", r, lineout_s.at[0], lineout_s.at[r]) for r in behind]
    across = [
        copy("dp", r, rows_at(mfar_s.at[0], partner("dp", r), small), mpiece_s.at[r])
        for r in behind
    ]
    back = [copy("dp", r, mpiece_s.at[0], full_ref.at[me, deep]) for r in behind]
    spread = [copy("mp", r, full_ref.at[me], full_ref.at[me]) for r in evens + [1]]
    onward = [
        copy("mp", 1, full_ref.at[partner("mp", r)], full_ref.at[partner("mp", r)]) for r in evens
    ]
    pnear = [copy("mp", 1, parts_s.at[2 * p + 1], pnear_s.at[p]) for p in range(pairs)]
    pfar = {p: copy("mp", 2 * p, parts_s.at[2 * p], pfar_s.at[p]) for p in range(1, pairs)}
    main_out = [
        copy("dp", r, rows_at(parts_s.at[0], partner("dp", r), main_piece), main_s.at[r])
        for r in behind
    ]
    tails = [
        copy("dp", r, parts_s.at[0, pl.ds(main_rows, TILE)], tails_s.at[r]) for r in behind
    ]
    main_all = [copy("dp", r, mainsum_s, main_ref.at[deep]) for r in behind]

    @pl.when(step == TILE + dense_steps - 1)
    def _():
        narrow = merged_s.shape[1]
        for j in range(merge_s.shape[1] // narrow):
            part = merge_s[:, j * narrow : (j + 1) * narrow]
            merged_s[j * width : (j + 1) * width, :] = part.astype(BF16)
        for c in mnear:
            c.start()
        linein_s[0] = jnp.concatenate([sums2_ref[0:4, :], lines_s[0:4, :]], axis=0)
        for c in lines_in:
            c.start()

        def merge_far():
            for p in reversed(range(pairs)):
                mnear[p].wait_recv()
                spot = pl.ds(pl.multiple_of(partner("mp", 2 * p) * share, TILE), share)
                joined = merged_s[spot, :].astype(F32) + mnear_s[p].astype(F32)
                merged_s[spot, :] = joined.astype(BF16)
                if p:
                    mfar[p].start()

        normed_t = n1_s[...].T
        bias_sums = []
        for t, ref in enumerate((gq_s, gk_s, gv_s)):
            grad = dot(normed_t, ref[...]).T
            sums = jnp.sum(ref[...].astype(F32), axis=0, keepdims=True)
            bias_sums.append(sums)
            sums = jnp.broadcast_to(sums, (8, width)).T[:, :1]
            grad = (grad * g1_ref[...] + sums * b1_ref[...]).astype(BF16)
            for r in range(near_size):
                parts_s[r, t * span : (t + 1) * span, :] = grad[r * span : (r + 1) * span]
            if t == 0:
                merge_far()
        table_grads()
        for r in range(near_size):
            parts_s[r, 3 * span : 4 * span, :] = gproj_ref[r * span : (r + 1) * span, :]
            lines = [fill(x[:, r * span : (r + 1) * span], width) for x in bias_sums]
            lines.append(fill(gtab_s[r * local : (r + 1) * local, :], width))
            hidden = gub_ref.shape[2] // 2
            half = (r % 2) * hidden
            lines.append(fill(gub_ref[r // 2][:, half : half + hidden], width))
            lines.append(jnp.zeros((TILE - 4 - local, width), F32))
            parts_s[r, 4 * span :, :] = jnp.concatenate(lines, axis=0).astype(BF16)
        for c in pnear:
            c.start()

        total = linein_s[0]
        for c, r in zip(lines_in, beside):
            c.wait_recv()
            total = total + linein_s[r]
        lineout_s[0] = total
        for c in lines_out:
            c.start()

        for c in bring_late():
            c.wait()
        mine = pl.ds(pl.multiple_of(me * share, TILE), share)
        total = merged_s[mine, :].astype(F32)
        for p in reversed(range(1, pairs)):
            mfar[p].wait_recv()
            total = total + mfar_s[p].astype(F32)
        mfar_s[0] = total.astype(BF16)
        for c in across:
            c.start()
        input_part(0)

        for p in reversed(range(pairs)):
            pnear[p].wait_recv()
            joined = parts_s[2 * p].astype(F32) + pnear_s[p].astype(F32)
            parts_s[2 * p] = joined.astype(BF16)
            if p:
                pfar[p].start()
        input_part(1)

        total = mfar_s[0, pl.ds(pl.multiple_of(deep * small, TILE), small), :].astype(F32)
        for c, r in zip(across, behind):
            c.wait_recv()
            total = total + mpiece_s[r].astype(F32)
        mpiece_s[0] = total.astype(BF16)
        keep_merge().start()
        for c in back:
            c.start()
        input_part(2)
        keep_merge().wait()
        for c in back:
            c.wait_recv()
        for c in spread:
            c.start()
        output_part(0)

        total = parts_s[0].astype(F32)
        for p in reversed(range(1, pairs)):
            pfar[p].wait_recv()
            total = total + pfar_s[p].astype(F32)
        parts_s[0] = total.astype(BF16)
        for c in main_out + tails:
            c.start()
        output_part(1)
        total = lineout_s[0]
        for c, r in zip(lines_out, behind):
            c.wait_recv()
            total = total + lineout_s[r]
        sums_ref[...] = total
        spot = pl.ds(pl.multiple_of(deep * main_piece, TILE), main_piece)
        total = parts_s[0, spot, :].astype(F32)
        for c, r in zip(main_out, behind):
            c.wait_recv()
            total = total + main_s[r].astype(F32)
        mainsum_s[...] = total.astype(BF16)
        keep_main().start()
        for c in main_all:
            c.start()
        output_part(2)
        total = parts_s[0, main_rows:, :].astype(F32)
        for c, r in zip(tails, behind):
            c.wait_recv()
            total = total + tails_s[r].astype(F32)
        tail_ref[...] = total

        for c, after in zip(spread, onward):
            c.wait_recv()
            after.start()
        spread[-1].wait_recv()
        for c in onward + main_all + ffn_all:
            c.wait_recv()
        keep_ffn().wait()
        keep_main().wait()
        for c in ffn_out + ffn_all + mnear + list(mfar.values()) + lines_in + lines_out:
            c.wait_send()
        for c in across + back + spread + onward + pnear + list(pfar.values()):
            c.wait_send()
        for c in main_out + tails + main_all:
            c.wait_send()
        for j in range(PARTS):
            take_gin(j).wait()
            take_raw(j).wait()


def back_rows(
    q,
    k,
    v,
    ga,
    rinv,
    att,
    n1,
    wt,
    p,
    idx,
    ffn,
    gmid,
    stats,
    x,
    g1,
    b1,
    gproj,
    gub,
    sums2,
    act,
    base,
    second,
    wm,
    g0,
    table_width,
    head_dim,
    local,
    near_size,
    far_size,
):
    rows, width = q.shape
    wide = x.shape[1]
    heads = width // head_dim
    groups, steps, sets, _, cover = p.shape
    dense_steps = 7
    count = rows // dense_steps
    narrow = 256
    pairs = near_size // 2
    piece = (ffn.shape[0] // far_size, ffn.shape[1])
    part = (4 * local * head_dim + TILE, width)
    main_piece = (4 * local * head_dim // far_size, width)
    total_rows = wide // narrow * width
    share = total_rows // near_size
    small = share // far_size
    near, far = near_size - 1, far_size - 1
    copies = 2 * far + (2 * pairs - 1) + near + 3 * far + 2 * pairs - 1 + 2 * pairs - 1 + 3 * far

    def place(i):
        return (jnp.maximum(i - steps, 0), 0)

    def p_place(i):
        return (0, jnp.minimum(i, steps - 1), 0, 0, 0)

    return call(
        functools.partial(back_kernel, head_dim, local, near_size, far_size, dense_steps),
        steps + dense_steps,
        (q, k, v, ga, rinv, att, n1, wt, p, idx, ffn, gmid, stats, x, g1, b1, gproj, gub, sums2)
        + (act, base, second, wm, g0),
        [anywhere()] * 8
        + [
            pl.BlockSpec((groups, 1, sets, COVER, cover), p_place),
            whole(idx.shape),
            whole(ffn.shape),
            pl.BlockSpec((count, width), place),
            pl.BlockSpec((count, 8), place),
            pl.BlockSpec((count, wide), place),
            whole(g1.shape),
            whole(b1.shape),
            whole(gproj.shape),
            whole(gub.shape),
            whole(sums2.shape),
        ]
        + [anywhere()] * 4
        + [whole(g0.shape)],
        [
            jax.ShapeDtypeStruct((rows, width), BF16),
            jax.ShapeDtypeStruct((rows, wide), BF16),
            jax.ShapeDtypeStruct((far_size,) + piece, BF16),
            jax.ShapeDtypeStruct((far_size,) + main_piece, BF16),
            jax.ShapeDtypeStruct((TILE, width), F32),
            jax.ShapeDtypeStruct((near_size, far_size, small, narrow), BF16),
            jax.ShapeDtypeStruct((8, width), F32),
        ],
        [
            anywhere(),
            anywhere(),
            anywhere(),
            anywhere(),
            whole((TILE, width)),
            anywhere(),
            whole((8, width)),
        ],
        [pltpu.VMEM((rows, width), BF16)] * 7
        + [pltpu.VMEM((3 * width, width), BF16)]
        + [pltpu.VMEM((rows, width), BF16)] * 3
        + [
            pltpu.VMEM((TILE, groups, COVER, cover), F32),
            pltpu.VMEM((heads, COVER, COVER), F32),
            pltpu.VMEM((cover, GROUP * head_dim), BF16),
            pltpu.VMEM((heads, table_width), F32),
            pltpu.VMEM((far_size,) + piece, BF16),
            pltpu.VMEM(piece, BF16),
            pltpu.VMEM((width, wide), F32),
            pltpu.VMEM((total_rows, narrow), BF16),
            pltpu.VMEM((pairs, share, narrow), BF16),
            pltpu.VMEM((pairs, share, narrow), BF16),
            pltpu.VMEM((far_size, small, narrow), BF16),
            pltpu.VMEM((near_size,) + part, BF16),
            pltpu.VMEM((pairs,) + part, BF16),
            pltpu.VMEM((pairs,) + part, BF16),
            pltpu.VMEM((far_size,) + main_piece, BF16),
            pltpu.VMEM(main_piece, BF16),
            pltpu.VMEM((far_size, TILE, width), BF16),
            pltpu.VMEM((near_size, 8, width), F32),
            pltpu.VMEM((far_size, 8, width), F32),
            pltpu.VMEM((8, width), F32),
            pltpu.VMEM((rows, wide), BF16),
            pltpu.VMEM((rows, 128), F32),
            pltpu.VMEM(wm.shape, BF16),
            pltpu.VMEM((act.shape[0] * act.shape[2], width), BF16),
            pltpu.SemaphoreType.DMA((6, LEVELS, sets)),
            pltpu.SemaphoreType.DMA((5,)),
            pltpu.SemaphoreType.DMA((2 + act.shape[0] + near_size,)),
            pltpu.SemaphoreType.DMA((2, PARTS)),
            pltpu.SemaphoreType.DMA((2 * copies,)),
        ],
        2 * rows * width * (24 * width + wide),
        rows * width * 20,
        group=2,
    )


def last_kernel(
    head_dim,
    local,
    window,
    live_ref,
    raw_ref,
    gin16_ref,
    wm_ref,
    g0_ref,
    b0_ref,
    main_ref,
    ffn_ref,
    full_ref,
    sums_ref,
    out_ref,
    gin_ref,
    gain0_ref,
    bias0_ref,
    gmerge_ref,
    gqkv_ref,
    gproj_ref,
    gup_ref,
    gdown_ref,
):
    step = pl.program_id(0)
    count, width = raw_ref.shape
    rows = count * pl.num_programs(0)
    live = live_rows(live_ref, step * count, count, rows, width, window)
    out_ref[...] = jnp.where(live, raw_ref[...].astype(F32), 0.0)
    gin_ref[...] = gin16_ref[...].astype(F32)

    @pl.when(step == 0)
    def _():
        span = local * head_dim
        main = main_ref[...].astype(F32)
        order = [
            main[t * span + l * head_dim : t * span + (l + 1) * head_dim]
            for l in range(local)
            for t in range(3)
        ]
        gqkv_ref[...] = jnp.concatenate(order, axis=0).T
        gproj_ref[...] = main[3 * span :]

    @pl.when(step == 1)
    def _():
        hidden = gup_ref.shape[1]
        gup_ref[...] = ffn_ref[:, :hidden].astype(F32)
        gdown_ref[...] = ffn_ref[:, hidden:].astype(F32).T

    narrow = full_ref.shape[2]
    low_sum = sums_ref[6:7, :]
    for j in range(full_ref.shape[0]):

        @pl.when(step == 2 + j)
        def _():
            cols = pl.ds(j * narrow, narrow)
            grad = full_ref[j].astype(F32).T
            weight = wm_ref[cols, :].astype(F32)
            gain = jnp.sum(weight * grad, axis=1, keepdims=True)
            shift = jnp.sum(weight * low_sum, axis=1, keepdims=True)
            gain0_ref[:, cols] = jnp.broadcast_to(gain, (narrow, 128)).T[:1, :]
            bias0_ref[:, cols] = jnp.broadcast_to(shift, (narrow, 128)).T[:1, :]
            scale = jnp.broadcast_to(g0_ref[:, cols], (8, narrow)).T[:, :1]
            offset = jnp.broadcast_to(b0_ref[:, cols], (8, narrow)).T[:, :1]
            gmerge_ref[cols, :] = grad * scale + offset * low_sum


def last_rows(live, raw, gin16, wm, g0, b0, main, ffn, full, sums, local, head_dim, window):
    rows, width = raw.shape
    wide = gin16.shape[1]
    step = rows // 7
    hidden = ffn.shape[1] // 2
    span = local * head_dim
    narrow_block = pl.BlockSpec((step, width), lambda i: (i, 0))
    wide_block = pl.BlockSpec((step, wide), lambda i: (i, 0))
    rest = [wm, g0, b0, main, ffn, full, sums]
    shapes = [
        (1, wide),
        (1, wide),
        (wide, width),
        (width, 3 * span),
        (span, width),
        (width, hidden),
        (hidden, width),
    ]
    return call(
        functools.partial(last_kernel, head_dim, local, window),
        7,
        [live, raw, gin16] + rest,
        [pl.BlockSpec(memory_space=pltpu.SMEM), narrow_block, wide_block]
        + [whole(a.shape) for a in rest],
        [
            jax.ShapeDtypeStruct((rows, width), F32),
            jax.ShapeDtypeStruct((rows, wide), F32),
        ]
        + [jax.ShapeDtypeStruct(shape, F32) for shape in shapes],
        [narrow_block, wide_block] + [whole(shape) for shape in shapes],
        [],
        2 * rows * width,
        rows * wide * 9,
    )


def shards(
    inputs,
    norm0_gain,
    norm0_bias,
    merge_weight,
    norm1_gain,
    norm1_bias,
    qkv_weight,
    qkv_bias,
    rel_table,
    rel_index,
    regions,
    live_windows,
    proj_weight,
    proj_bias,
    norm2_gain,
    norm2_bias,
    up_weight,
    up_bias,
    down_weight,
    down_bias,
    cotangent,
    n_dp,
    n_mp,
):
    micro, strip_rows, wide = inputs.shape
    width = merge_weight.shape[1]
    win = rel_index.shape[0]
    local, packed = qkv_bias.shape
    head_dim = packed // 3
    heads = local * n_mp
    hidden = up_bias.shape[0]
    rel = rel_table.shape[1]
    rows = micro * strip_rows
    windows = rows // win
    sets = windows // TILE
    strip = lax.axis_index("mp")

    region = lax.dynamic_slice_in_dim(regions, strip * strip_rows, strip_rows, axis=1)
    region = region.reshape(sets, rows // sets)
    jump = rows // sets // TILE - 1
    region = jnp.stack([region[:, o * jump : o * jump + COVER] for o in range(TILE)])
    region = jnp.tile(region[:, :, None, :], (1, 1, 1, GROUP))
    table_width = -(-rel // 128) * 128
    vecs = (proj_bias[None], norm2_gain[None], norm2_bias[None], down_bias[None])
    gain0, bias0 = norm0_gain[None], norm0_bias[None]
    gain1, bias1 = norm1_gain[None], norm1_bias[None]

    x = inputs.reshape(rows, wide)
    stats, n1, q, k, v, att, rinv, p, tiles, wt, second = front_rows(
        x,
        gain0,
        bias0,
        merge_weight,
        gain1,
        bias1,
        qkv_weight.reshape(width, local * packed),
        qkv_bias,
        rel_table,
        up_bias[None],
        up_weight,
        down_weight,
        proj_weight.reshape(local * head_dim, width),
        rel_index,
        region,
        n_mp,
        head_dim,
    )
    base, act, gmid, gatt, ffn_part, gub, gproj, sums2 = ffn_rows(
        live_windows,
        n1,
        att,
        cotangent.reshape(rows, width),
        stats,
        tiles,
        second,
        vecs,
        local,
        hidden,
        win,
    )
    raw, gin16, ffn_sum, main, tail, gmerge, sums = back_rows(
        q,
        k,
        v,
        gatt,
        rinv,
        att,
        n1,
        wt,
        p,
        rel_index,
        ffn_part,
        gmid,
        stats,
        x,
        gain1,
        bias1,
        gproj,
        gub,
        sums2,
        act,
        base,
        second,
        merge_weight,
        gain0,
        table_width,
        head_dim,
        local,
        n_mp,
        n_dp,
    )
    span = local * head_dim
    out, grad_input, ggain0, gbias0, gmerge, gqkv, gproj, gup, gdown = last_rows(
        live_windows,
        raw,
        gin16,
        merge_weight,
        gain0,
        bias0,
        main.reshape(4 * span, width),
        ffn_sum.reshape(width, 2 * hidden),
        gmerge.reshape(-1, width, gmerge.shape[3]),
        sums,
        local,
        head_dim,
        win,
    )
    gqb = jnp.transpose(tail[:3, :span].reshape(3, local, head_dim), (1, 0, 2))
    return (
        out.reshape(micro, strip_rows, width),
        grad_input.reshape(micro, strip_rows, wide),
        ggain0.reshape(wide),
        gbias0.reshape(wide),
        gmerge,
        sums[4],
        sums[5],
        gqkv.reshape(width, local, packed),
        gqb.reshape(local, packed),
        tail[3 : 3 + local, :rel],
        gproj.reshape(local, head_dim, width),
        sums[0],
        sums[1],
        sums[2],
        gup,
        tail[3 + local, :hidden],
        gdown,
        sums[3],
    )


def solution(mesh):
    placed = (
        P(None, ("dp", "mp"), None),
        P(),
        P(),
        P(),
        P(),
        P(),
        P(None, "mp", None),
        P("mp", None),
        P("mp", None),
        P(),
        P(None, "dp"),
        P(None, "dp"),
        P("mp", None, None),
        P(),
        P(),
        P(),
        P(None, "mp"),
        P("mp"),
        P("mp", None),
        P(),
        P(None, ("dp", "mp"), None),
    )
    return jax.shard_map(
        functools.partial(shards, n_dp=mesh.shape["dp"], n_mp=mesh.shape["mp"]),
        mesh=mesh,
        in_specs=placed,
        out_specs=(
            P(None, ("dp", "mp"), None),
            P(None, ("dp", "mp"), None),
            P(),
            P(),
            P(),
            P(),
            P(),
            P(None, "mp", None),
            P("mp", None),
            P("mp", None),
            P("mp", None, None),
            P(),
            P(),
            P(),
            P(None, "mp"),
            P("mp"),
            P("mp", None),
            P(),
        ),
        check_vma=False,
    )
```

```python
import functools
import math

import jax
import jax.numpy as jnp
from jax import lax
from jax.experimental import pallas as pl
from jax.experimental.pallas import tpu as pltpu
from jax.sharding import PartitionSpec as P

F32 = jnp.float32
BF16 = jnp.bfloat16
EPSILON = 1e-05
MASKED = -1e30
COVER = 64
TILE = 16
GROUP = 4
VMEM_LIMIT = 60 << 20


def dot(left, right):
    return jnp.dot(left, right, preferred_element_type=F32)


def dot_rt(left, right):
    return lax.dot_general(left, right, (((1,), (1,)), ((), ())), preferred_element_type=F32)


def dot_lt(left, right):
    return lax.dot_general(left, right, (((0,), (0,)), ((), ())), preferred_element_type=F32)


def whole(shape):
    return pl.BlockSpec(shape, lambda i: (0,) * len(shape), pipeline_mode=pl.Buffered(1))


def anywhere():
    return pl.BlockSpec(memory_space=pl.ANY)


def call(kernel, grid, ins, in_specs, outs, out_specs, scratch, flops, nbytes, group=None):
    extra = {} if group is None else {"collective_id": group, "has_side_effects": True}
    return pl.pallas_call(
        kernel,
        grid=(grid,),
        in_specs=in_specs,
        out_specs=out_specs,
        out_shape=outs,
        scratch_shapes=scratch,
        compiler_params=pltpu.CompilerParams(
            dimension_semantics=("arbitrary",), vmem_limit_bytes=VMEM_LIMIT, **extra
        ),
        cost_estimate=pl.CostEstimate(flops=flops, bytes_accessed=nbytes, transcendentals=0),
    )(*ins)


def partner(axis, flips):
    at = lax.axis_index(axis)
    bit = 1
    while bit <= flips:
        if flips & bit:
            at = at + bit * (1 - 2 * lax.rem(lax.div(at, jnp.int32(bit)), jnp.int32(2)))
        bit *= 2
    return at


def send(axis, flips, src, dst, send_sem, recv_sem):
    return pltpu.make_async_remote_copy(
        src_ref=src,
        dst_ref=dst,
        send_sem=send_sem,
        recv_sem=recv_sem,
        device_id={axis: partner(axis, flips)},
        device_id_type=pl.DeviceIdType.MESH,
    )


def greet(peers):
    barrier = pltpu.get_barrier_semaphore()
    for axis, flips in peers:
        pl.semaphore_signal(
            barrier,
            inc=1,
            device_id={axis: partner(axis, flips)},
            device_id_type=pl.DeviceIdType.MESH,
        )
    pl.semaphore_wait(barrier, len(peers))


class Gather:
    def __init__(self, axis, size, own, held, send_sems, recv_sems, own_sem):
        self.axis, self.size, self.own, self.held = axis, size, own, held
        self.send_sems, self.recv_sems, self.own_sem = send_sems, recv_sems, own_sem

    def straight(self, r):
        return send(
            self.axis, r, self.own, self.held.at[r], self.send_sems.at[r], self.recv_sems.at[r]
        )

    def onward(self, r):
        return send(
            self.axis,
            1,
            self.held.at[r],
            self.held.at[r + 1],
            self.send_sems.at[r + 1],
            self.recv_sems.at[r + 1],
        )

    def keep(self):
        return pltpu.make_async_copy(self.own, self.held.at[0], self.own_sem)

    def start(self, flips=None):
        evens = list(range(2, self.size, 2))
        for r in evens + [1] if flips is None else flips:
            self.straight(r).start()
        if flips is None or 1 in flips:
            self.keep().start()

    def forward(self, r):
        self.straight(r).wait_recv()
        self.onward(r).start()

    def finish(self):
        self.keep().wait()
        self.straight(1).wait()
        for r in range(2, self.size, 2):
            self.straight(r).wait_send()
            self.onward(r).wait()


def spans(total, step):
    return [(start, min(step, total - start)) for start in range(0, total, step)]


def norm_parts(values):
    mean = jnp.mean(values, axis=-1, keepdims=True)
    center = values - mean
    spread = jnp.mean(center * center, axis=-1, keepdims=True) + EPSILON
    inverse = lax.rsqrt(spread)
    return center * inverse, mean, inverse, spread


def norm_back(grad, normed, inverse):
    mean_grad = jnp.mean(grad, axis=-1, keepdims=True)
    mean_cross = jnp.mean(grad * normed, axis=-1, keepdims=True)
    return inverse * (grad - mean_grad - normed * mean_cross)


def head_mask(head_dim):
    rows = lax.broadcasted_iota(jnp.int32, (GROUP * COVER, GROUP * head_dim), 0) // COVER
    cols = lax.broadcasted_iota(jnp.int32, (GROUP * COVER, GROUP * head_dim), 1) // head_dim
    return (rows == cols).astype(F32).astype(BF16)


def tiled(block, mask):
    return jnp.concatenate([block] * GROUP, axis=0) * mask


def pair_row(idx_ref, pair):
    win = idx_ref.shape[0]
    gap = jnp.full((1, COVER - win), -1, jnp.int32)
    parts = []
    for i in (2 * pair, 2 * pair + 1):
        parts.append(idx_ref[i : i + 1, :] if i < win else jnp.full((1, win), -1, jnp.int32))
        parts.append(gap)
    return jnp.concatenate(parts, axis=1)


def index_onehot(row, table_width):
    entry = lax.broadcasted_iota(jnp.int32, (table_width, row.shape[1]), 0)
    return (entry == row).astype(F32).astype(BF16)


def fill(x, width):
    return jnp.concatenate([x, jnp.zeros((x.shape[0], width - x.shape[1]), x.dtype)], axis=1)


def front_kernel(
    head_dim,
    local,
    size,
    merge_steps,
    x_ref,
    g0_ref,
    b0_ref,
    wm_ref,
    g1_ref,
    b1_ref,
    qkvw_ref,
    qkvb_ref,
    tab_ref,
    ub_ref,
    up_ref,
    down_ref,
    proj_ref,
    idx_ref,
    rid_ref,
    stats_ref,
    n1_ref,
    q_ref,
    k_ref,
    v_ref,
    att_ref,
    rinv_ref,
    p_ref,
    tiles_ref,
    wt_ref,
    second_ref,
    first_s,
    tiles_s,
    own_s,
    tile_s,
    second_s,
    mid_s,
    q_s,
    k_s,
    v_s,
    att_s,
    rinv_s,
    base_s,
    bias_s,
    mask_s,
    tile_send,
    tile_recv,
    first_send,
    first_recv,
    second_send,
    second_recv,
    own_sems,
    out_sems,
):
    step = pl.program_id(0)
    rows, width = mid_s.shape
    heads = width // head_dim
    lanes = GROUP * head_dim
    groups = heads // GROUP
    per_group = size // groups
    scale = 1.0 / math.sqrt(head_dim)
    span = local * head_dim
    evens = list(range(2, size, 2))
    main = Gather("mp", size, own_s, first_s, first_send, first_recv, own_sems.at[0])
    rest = Gather("mp", size, second_s, second_ref, second_send, second_recv, own_sems.at[1])

    def tile_copy(r):
        return send("mp", r, tile_s, tiles_s.at[r], tile_send.at[r], tile_recv.at[r])

    @pl.when(step == 0)
    def _():
        own_s[...] = qkvw_ref[...].T
        bias = qkvb_ref[...].astype(F32)
        lines = []
        for t in range(3):
            parts = [
                bias[l : l + 1, t * head_dim : (t + 1) * head_dim] for l in range(local)
            ]
            lines.append(fill(jnp.concatenate(parts, axis=1), width))
        lines.append(fill(tab_ref[...].astype(F32), width))
        lines.append(fill(ub_ref[...].astype(F32), width))
        lines.append(jnp.zeros((TILE - 4 - local, width), F32))
        tile_s[...] = jnp.concatenate(lines, axis=0).astype(BF16)
        greet([("mp", r) for r in range(1, size)])
        for r in range(1, size):
            tile_copy(r).start()
        tiles_s[0] = tile_s[...]
        main.start([r for r in evens if r < 2 * per_group] + [1])
        hidden = up_ref.shape[1]
        second_s[:hidden, :] = up_ref[...].T
        second_s[hidden : 2 * hidden, :] = down_ref[...]
        second_s[2 * hidden :, :] = proj_ref[...]

    @pl.when(step == 2)
    def _():
        main.start([r for r in evens if r >= 2 * per_group])

    @pl.when(step == merge_steps - 3)
    def _():
        rest.start()

    @pl.when(step < merge_steps)
    def _():
        count = x_ref.shape[0]
        here = pl.ds(pl.multiple_of(step * count, TILE), count)
        normed, mean, inverse, _ = norm_parts(x_ref[...].astype(F32))
        normed_in = (normed * g0_ref[...] + b0_ref[...]).astype(BF16)
        normed1, mean1, inverse1, spread1 = norm_parts(dot(normed_in, wm_ref[...]))
        n1_ref[...] = normed1.astype(BF16)
        stats = [mean, inverse, mean1, inverse1, spread1 * inverse1]
        stats_ref[...] = jnp.concatenate(stats + [mean] * (8 - len(stats)), axis=1)
        mid_s[here, :] = (normed1 * g1_ref[...] + b1_ref[...]).astype(BF16)

    table_step = merge_steps - 3

    @pl.when(step == merge_steps - 1)
    def _():
        for r in evens:
            if r < 2 * per_group:
                main.forward(r)

    @pl.when(step == table_step)
    def _():
        mask_s[...] = head_mask(head_dim)
        att_s[...] = jnp.zeros_like(att_s)
        rinv_s[...] = jnp.zeros_like(rinv_s)
        base_s[...] = jnp.full(base_s.shape, MASKED, F32)
        for r in range(1, size):
            tile_copy(r).wait_recv()

    all_pairs = list(range((idx_ref.shape[0] + 1) // 2))
    for i in range(2):

        @pl.when(step == table_step + i)
        def _():
            table = jnp.concatenate(
                [tiles_s[r].astype(F32)[3 : 3 + local, : 2 * 128] for r in range(size)], axis=0
            ).astype(BF16)
            here = all_pairs[i::2]
            rows_of = [pair_row(idx_ref, pair) for pair in here]
            found = [dot(table, index_onehot(row, table.shape[1])) for row in rows_of]
            found = [jnp.where(row < 0, MASKED, x) for row, x in zip(rows_of, found)]
            for pair, vals in zip(here, found):
                base_s[:, 2 * pair, :] = vals[:, :COVER]
                base_s[:, 2 * pair + 1, :] = vals[:, COVER:]

    @pl.when(step == table_step + 2)
    def _():
        tiles_ref[...] = tiles_s[...]

        def shift(g, _):
            full = jnp.concatenate([base_s[g * GROUP + h] for h in range(GROUP)], axis=1)
            for o in range(TILE):
                bias_s[g, o] = pltpu.roll(pltpu.roll(full, o, 0), o, 1) if o else full
            return 0

        lax.fori_loop(0, groups, shift, 0)
        for r in range(1, size):
            tile_copy(r).wait_send()

    def outward(ref, out, which, g):
        cols = pl.ds(pl.multiple_of(g * lanes, lanes), lanes)
        return pltpu.make_async_copy(ref.at[:, cols], out.at[:, cols], out_sems.at[which, g])

    def early_out(g):
        return [
            outward(ref, out, i, g)
            for i, (ref, out) in enumerate(((q_s, q_ref), (k_s, k_ref), (v_s, v_ref)))
        ]

    def late_out(g):
        return [outward(att_s, att_ref, 3, g), outward(rinv_s, rinv_ref, 4, g)]

    low_half = lax.broadcasted_iota(jnp.int32, (COVER, 2 * COVER), 1) < COVER
    region_of = lax.broadcasted_iota(jnp.int32, (8, GROUP * COVER), 0)
    sets = rid_ref.shape[1]
    block = rows // sets

    def attend(it, g):
        mask = mask_s[...]
        cols = pl.ds(pl.multiple_of(g * lanes, lanes), lanes)
        units = [(2 * it + i, u) for i in range(2) for u in range(sets)]
        starts = [pl.multiple_of(o * (block // TILE - 1) + u * block, TILE) for o, u in units]
        scores = []
        for start in starts:
            here = pl.ds(start, COVER)
            scores.append(dot_rt(q_s[here, cols], tiled(k_s[here, cols], mask)))
        weights = []
        for (o, u), s in zip(units, scores):
            member = (region_of == rid_ref[o, u]).astype(F32).astype(BF16)
            same = dot_lt(member[:, :COVER], member)
            s = s + bias_s[g, o] + jnp.where(same > 0.5, 0.0, MASKED)
            parts = []
            for c in range(GROUP // 2):
                x = s[:, c * 2 * COVER : (c + 1) * 2 * COVER]
                top0 = jnp.max(jnp.where(low_half, x, MASKED), axis=1, keepdims=True)
                top1 = jnp.max(jnp.where(low_half, MASKED, x), axis=1, keepdims=True)
                top = jnp.maximum(jnp.where(low_half, top0, top1), MASKED * 0.1)
                parts.append(jnp.exp(x - top).astype(BF16))
            w = jnp.concatenate(parts, axis=1)
            p_ref[0, o, u] = w
            weights.append(w)
        mixed = []
        for start, w in zip(starts, weights):
            vals = tiled(v_s[pl.ds(start, COVER), cols], mask)
            mixed.append(dot(w, jnp.concatenate([vals, mask], axis=1)))
        for start, a in zip(starts, mixed):
            here = pl.ds(start, COVER)
            total = a[:, lanes:]
            inv = jnp.where(total > 0.0, 1.0 / jnp.maximum(total, 0.5), 0.0)
            att_s[here, cols] += (a[:, :lanes] * inv).astype(BF16)
            rinv_s[here, cols] += inv.astype(BF16)

    @pl.when(step >= merge_steps)
    def _():
        g = step - merge_steps
        twice = 2 * per_group

        @pl.when(g == 0)
        def _():
            main.keep().wait()
            main.straight(1).wait_recv()
            for r in evens:
                if r < twice:
                    main.onward(r).wait_recv()

        for known in range(2, groups, 2):

            @pl.when(g == known)
            def _():
                for r in evens:
                    if known * per_group <= r < known * per_group + twice:
                        main.onward(r).wait_recv()

        @pl.when(g % 2 == 0)
        def _():
            shards = [g * per_group + j for j in range(twice)]
            cols = pl.ds(pl.multiple_of(g * lanes, 2 * lanes), 2 * lanes)
            outs = (q_s, k_s, v_s)
            part = rows // 3
            weights, biases = [], []
            for t in range(3):
                weight = []
                for s in shards:
                    for l in range(local):
                        at = (3 * l + t) * head_dim
                        weight.append(first_s[s, at : at + head_dim, :])
                    biases.append(tiles_s[s].astype(F32)[t : t + 1, :span])
                weight = jnp.concatenate(weight, axis=0)
                spot = pl.ds(pl.multiple_of(t * width + g * lanes, 2 * lanes), 2 * lanes)
                wt_ref[spot, :] = weight
                weights.append(weight.T)
            weight = jnp.concatenate(weights, axis=1)
            bias = jnp.concatenate(biases, axis=1)

            def project(i, _):
                here = pl.ds(pl.multiple_of(i * part, TILE), part)
                y = dot(mid_s[here, :], weight) + bias
                for t in range(3):
                    z = y[:, 2 * t * lanes : 2 * (t + 1) * lanes]
                    outs[t][here, cols] = (z * scale if t == 0 else z).astype(BF16)
                return 0

            lax.fori_loop(0, 3, project, 0)

        for c in early_out(g):
            c.start()

        def run(it, _):
            attend(it, g)
            return 0

        lax.fori_loop(0, TILE // 4, run, 0)

        @pl.when(g == 0)
        def _():
            for r in evens:
                if r >= twice:
                    main.forward(r)

        @pl.when(g == groups - 1)
        def _():
            for r in evens:
                rest.forward(r)

        lax.fori_loop(TILE // 4, TILE // 2, run, 0)
        for c in late_out(g):
            c.start()

        @pl.when(g == groups - 1)
        def _():
            main.straight(1).wait_send()
            for r in evens:
                main.straight(r).wait_send()
                main.onward(r).wait_send()
            rest.finish()
            for known in range(groups):
                for c in early_out(known) + late_out(known):
                    c.wait()


def front_rows(
    x, g0, b0, wm, g1, b1, qkvw, qkvb, tab, ub, up, down, proj, idx, rid, size, head_dim
):
    rows, wide = x.shape
    width = wm.shape[1]
    local = qkvb.shape[0]
    hidden = up.shape[1]
    heads = width // head_dim
    groups = heads // GROUP
    offsets, sets = rid.shape[0], rid.shape[1]
    cover = GROUP * COVER
    merge_steps = 7
    step = rows // merge_steps
    first = (3 * local * head_dim, width)
    second = (2 * hidden + local * head_dim, width)

    def place(i):
        return (jnp.minimum(i, merge_steps - 1), 0)

    def group_place(i):
        return (jnp.maximum(i - merge_steps, 0), 0, 0, 0, 0)

    small = [g0, b0, wm, g1, b1, qkvw, qkvb, tab, ub, up, down, proj, idx, rid]
    row_out = jax.ShapeDtypeStruct((rows, width), BF16)
    sems = [pltpu.SemaphoreType.DMA((size,))] * 6
    return call(
        functools.partial(front_kernel, head_dim, local, size, merge_steps),
        merge_steps + groups,
        [x] + small,
        [pl.BlockSpec((step, wide), place)] + [whole(a.shape) for a in small],
        [jax.ShapeDtypeStruct((rows, 8), F32), row_out]
        + [row_out] * 5
        + [
            jax.ShapeDtypeStruct((groups, offsets, sets, COVER, cover), BF16),
            jax.ShapeDtypeStruct((size, TILE, width), BF16),
            jax.ShapeDtypeStruct((3 * width, width), BF16),
            jax.ShapeDtypeStruct((size,) + second, BF16),
        ],
        [pl.BlockSpec((step, 8), place), pl.BlockSpec((step, width), place)]
        + [anywhere()] * 5
        + [
            pl.BlockSpec((1, offsets, sets, COVER, cover), group_place),
            whole((size, TILE, width)),
            whole((3 * width, width)),
            anywhere(),
        ],
        [
            pltpu.VMEM((size,) + first, BF16),
            pltpu.VMEM((size, TILE, width), BF16),
            pltpu.VMEM(first, BF16),
            pltpu.VMEM((TILE, width), BF16),
            pltpu.VMEM(second, BF16),
        ]
        + [pltpu.VMEM((rows, width), BF16)] * 6
        + [
            pltpu.VMEM((heads, COVER, COVER), F32),
            pltpu.VMEM((groups, TILE, COVER, cover), F32),
            pltpu.VMEM((cover, GROUP * head_dim), BF16),
        ]
        + sems
        + [pltpu.SemaphoreType.DMA((2,)), pltpu.SemaphoreType.DMA((5, groups))],
        2 * rows * width * (wide + 18 * width),
        rows * width * 40,
        group=0,
    )


REACH = math.sqrt(2.0) / 0.3275911
CENTRE = 0.125


def centred():
    rational = (0.254829592, -0.284496736, 1.421413741, -1.453152027, 1.061405429)
    plain = [0.5 * a * REACH ** (k + 1) for k, a in enumerate(rational)]
    out = [0.0] * len(plain)
    for k, a in enumerate(plain):
        for j in range(k + 1):
            out[j] += a * math.comb(k, j) * CENTRE ** (k - j)
    return out


def gelu_and_slope(pre):
    x = pre.astype(BF16)
    t = pl.reciprocal(jnp.abs(pre) + REACH, approx=True)
    s = (t - CENTRE).astype(BF16)
    terms = [BF16(a) for a in centred()]
    poly = terms[4]
    for a in reversed(terms[:4]):
        poly = poly * s + a
    part = poly * t.astype(BF16)
    bell = jnp.exp2((x * x) * BF16(-0.5 * math.log2(math.e)))
    size = jnp.abs(x)
    act = jnp.maximum(x, BF16(0.0)) - size * (part * bell)
    under = (part - size * BF16(1.0 / math.sqrt(2.0 * math.pi))) * bell
    return act, jnp.where(x > BF16(0.0), BF16(1.0) - under, under)


def live_rows(live_ref, start, count, rows, width, window):
    micro = live_ref.shape[0]
    micro_rows = rows // micro
    before = lax.axis_index("mp") * micro_rows
    row = lax.broadcasted_iota(jnp.int32, (count, width), 0) + start
    live = None
    for m in range(micro):
        last = m * micro_rows + jnp.minimum(live_ref[m, 0] * window - before, micro_rows)
        inside = (row >= m * micro_rows) & (row < last)
        live = inside if live is None else live | inside
    return live


def ffn_kernel(
    local,
    window,
    live_ref,
    n1_ref,
    att_ref,
    cot_ref,
    stats_ref,
    wp_ref,
    pb_ref,
    g2_ref,
    b2_ref,
    db_ref,
    tail_ref,
    up_ref,
    down_ref,
    base_ref,
    act_ref,
    gmid_ref,
    gatt_ref,
    part_ref,
    gub_ref,
    gproj_ref,
    sums_ref,
    base_s,
    gffn_s,
    att_s,
    n2_s,
    inv_s,
    n_s,
    go_s,
    nt_s,
    gt_s,
    act_s,
    gp_s,
    odd_s,
    even_s,
    near_s,
    far_s,
    near_send,
    near_recv,
    far_send,
    far_recv,
    in_sems,
    out_sems,
    act_sem,
):
    step = pl.program_id(0)
    pairs = even_s.shape[0]
    pair = pairs - 1 - step
    rows, width = gffn_s.shape
    blocks = spans(rows, 384)
    hidden = up_ref.shape[1]
    wp = wp_ref[...].reshape(width, width)

    def near(p):
        return send("mp", 1, odd_s.at[p % 2], near_s.at[p], near_send.at[p], near_recv.at[p])

    def far(p):
        slot = far_s.at[p - 1]
        return send("mp", 2 * p, even_s.at[p], slot, far_send.at[p], far_recv.at[p])

    def bring(b):
        here = pl.ds(*blocks[b])
        whence = ((n1_ref, n_s), (att_ref, att_s), (cot_ref, go_s))
        return [
            pltpu.make_async_copy(src.at[here], dst.at[here], in_sems.at[i, b])
            for i, (src, dst) in enumerate(whence)
        ]

    def take(which, b):
        here = pl.ds(*blocks[b])
        src, dst = ((base_s, base_ref), (go_s, gmid_ref), (n2_s, gatt_ref))[which]
        return pltpu.make_async_copy(src.at[here], dst.at[here], out_sems.at[which, b])

    def take_act():
        return pltpu.make_async_copy(act_s.at[pl.ds(0, rows)], act_ref.at[pair], act_sem)

    @pl.when(step == 0)
    def _():
        for b in range(len(blocks)):
            for c in bring(b):
                c.start()
        greet([("mp", r) for r in [1] + [2 * p for p in range(1, pairs)]])
        bias_proj, gain2, bias2, bias_down = (x[...] for x in (pb_ref, g2_ref, b2_ref, db_ref))
        act_s[rows:, :] = jnp.zeros_like(act_s[rows:, :])
        gp_s[rows:, :] = jnp.zeros_like(gp_s[rows:, :])
        nt_s[width:, :] = jnp.ones_like(nt_s[width:, :])
        down_sum = jnp.zeros((1, width), F32)
        for b, (start, count) in enumerate(blocks):
            here = pl.ds(start, count)
            for c in bring(b):
                c.wait()
            stats = stats_ref[here, :]
            merged = n_s[here, :].astype(F32) * stats[:, 4:5] + stats[:, 2:3]
            middle = merged + dot(att_s[here, :], wp) + bias_proj
            base_s[here, :] = (middle + bias_down).astype(BF16)
            take(0, b).start()
            normed, _, inverse, _ = norm_parts(middle)
            n2_s[here, :] = normed.astype(BF16)
            inv_s[here, :] = jnp.broadcast_to(inverse, (count, inv_s.shape[1]))
            normed_ffn = (normed * gain2 + bias2).astype(BF16)
            n_s[here, :] = normed_ffn
            live = live_rows(live_ref, start, count, rows, width, window)
            grad_out = jnp.where(live, go_s[here, :].astype(F32), 0.0)
            down_sum = down_sum + jnp.sum(grad_out, axis=0, keepdims=True)
            grad_low = grad_out.astype(BF16)
            go_s[here, :] = grad_low
            whole_count = -(-count // 128) * 128
            if whole_count != count:
                filler = jnp.zeros((whole_count - count, width), BF16)
                normed_ffn = jnp.concatenate([normed_ffn, filler], axis=0)
                grad_low = jnp.concatenate([grad_low, filler], axis=0)
            nt_s[:width, start : start + whole_count] = normed_ffn.T
            gt_s[:, start : start + whole_count] = grad_low.T
        sums_ref[...] = jnp.zeros_like(sums_ref)
        sums_ref[3:4, :] = down_sum
        gffn_s[...] = jnp.zeros_like(gffn_s)

    def pass_on():
        @pl.when(step > 0)
        def _():
            near(pair + 1).wait_recv()
            joined = even_s[pair + 1].astype(F32) + near_s[pair + 1].astype(F32)
            even_s[pair + 1] = joined.astype(BF16)

        for p in range(1, pairs):

            @pl.when(pair + 1 == p)
            def _():
                far(p).start()

    up_t = up_ref[...].reshape(2 * hidden, width)
    down = down_ref[...].reshape(2 * hidden, width)
    up_bias = jnp.concatenate(
        [tail_ref[i].astype(F32)[3 + local : 4 + local, :hidden] for i in range(2)], axis=1
    )
    for b, (start, count) in enumerate(blocks):
        if b == 1:
            pass_on()
        here = pl.ds(start, count)
        act, slope = gelu_and_slope(dot_rt(n_s[here, :], up_t) + up_bias)
        grad_pre = dot_rt(go_s[here, :], down).astype(BF16) * slope
        act_s[here, :] = act
        gp_s[here, :] = grad_pre
        gffn_s[here, :] += dot(grad_pre, up_t)
    take_act().start()

    @pl.when(step > 1)
    def _():
        near(pair + 2).wait_send()

    grad_up = dot(nt_s[...], gp_s[...])
    gub_ref[0] = grad_up[width : width + 1, :]
    grad_up = grad_up[:width].astype(BF16)
    even_s[pair, :, :hidden] = grad_up[:, :hidden]
    odd_s[pair % 2, :, :hidden] = grad_up[:, hidden:]
    grad_down = dot(gt_s[...], act_s[...]).astype(BF16)
    even_s[pair, :, hidden:] = grad_down[:, :hidden]
    odd_s[pair % 2, :, hidden:] = grad_down[:, hidden:]
    near(pair).start()
    take_act().wait()

    @pl.when(step == pairs - 1)
    def _():
        gain2 = g2_ref[...]
        gain_sum = jnp.zeros((1, width), F32)
        bias_sum = jnp.zeros((1, width), F32)
        proj_sum = jnp.zeros((1, width), F32)
        grad_proj = jnp.zeros((width, width), F32)
        for b, (start, count) in enumerate(blocks):
            here = pl.ds(start, count)
            grad_ffn = gffn_s[here, :]
            normed = n2_s[here, :].astype(F32)
            gain_sum = gain_sum + jnp.sum(grad_ffn * normed, axis=0, keepdims=True)
            bias_sum = bias_sum + jnp.sum(grad_ffn, axis=0, keepdims=True)
            grad_middle = go_s[here, :].astype(F32) + norm_back(
                grad_ffn * gain2, normed, inv_s[here, :1]
            )
            proj_sum = proj_sum + jnp.sum(grad_middle, axis=0, keepdims=True)
            grad_attn = grad_middle.astype(BF16)
            go_s[here, :] = grad_attn
            take(1, b).start()
            grad_proj = grad_proj + dot_lt(att_s[here, :], grad_attn)
            n2_s[here, :] = dot_rt(grad_attn, wp).astype(BF16)
            take(2, b).start()
        gproj_ref[...] = grad_proj.astype(BF16)
        sums_ref[0:1, :] = proj_sum
        sums_ref[1:2, :] = gain_sum
        sums_ref[2:3, :] = bias_sum
        near(0).wait_recv()
        total = even_s[0].astype(F32) + near_s[0].astype(F32)
        for p in range(1, pairs):
            far(p).wait_recv()
            total = total + far_s[p - 1].astype(F32)
        part_ref[...] = total.astype(BF16)
        for p in range(pairs):
            if p < 2:
                near(p).wait_send()
            if p:
                far(p).wait_send()
        for b in range(len(blocks)):
            for which in range(3):
                take(which, b).wait()


def ffn_rows(live, n1, att, cot, stats, tiles, second, vecs, local, hidden, window):
    rows, width = n1.shape
    size = tiles.shape[0]
    pairs = size // 2
    padded = -(-rows // 128) * 128
    proj_rows = width // size
    proj_at = 2 * hidden // proj_rows
    blocks = len(spans(rows, 384))
    row_out = jax.ShapeDtypeStruct((rows, width), BF16)
    return call(
        functools.partial(ffn_kernel, local, window),
        pairs,
        (live, n1, att, cot, stats, second) + vecs + (tiles, second, second),
        [
            pl.BlockSpec(memory_space=pltpu.SMEM),
            anywhere(),
            anywhere(),
            anywhere(),
            whole(stats.shape),
            pl.BlockSpec(
                (size, proj_rows, width),
                lambda i: (0, proj_at, 0),
                pipeline_mode=pl.Buffered(1),
            ),
        ]
        + [whole((1, width))] * 4
        + [
            pl.BlockSpec((2, TILE, width), lambda i: (pairs - 1 - i, 0, 0)),
            pl.BlockSpec((2, hidden, width), lambda i: (pairs - 1 - i, 0, 0)),
            pl.BlockSpec((2, hidden, width), lambda i: (pairs - 1 - i, 1, 0)),
        ],
        [
            row_out,
            jax.ShapeDtypeStruct((pairs, rows, 2 * hidden), BF16),
            row_out,
            row_out,
            jax.ShapeDtypeStruct((width, 2 * hidden), BF16),
            jax.ShapeDtypeStruct((pairs, 1, 2 * hidden), F32),
            jax.ShapeDtypeStruct((width, width), BF16),
            jax.ShapeDtypeStruct((8, width), F32),
        ],
        [
            anywhere(),
            anywhere(),
            anywhere(),
            anywhere(),
            whole((width, 2 * hidden)),
            pl.BlockSpec((1, 1, 2 * hidden), lambda i: (pairs - 1 - i, 0, 0)),
            whole((width, width)),
            whole((8, width)),
        ],
        [
            pltpu.VMEM((rows, width), BF16),
            pltpu.VMEM((rows, width), F32),
            pltpu.VMEM((rows, width), BF16),
            pltpu.VMEM((rows, width), BF16),
            pltpu.VMEM((rows, 128), F32),
            pltpu.VMEM((rows, width), BF16),
            pltpu.VMEM((rows, width), BF16),
            pltpu.VMEM((width + TILE, padded), BF16),
            pltpu.VMEM((width, padded), BF16),
            pltpu.VMEM((padded, 2 * hidden), BF16),
            pltpu.VMEM((padded, 2 * hidden), BF16),
        ]
        + [pltpu.VMEM((min(pairs, 2), width, 2 * hidden), BF16)]
        + [pltpu.VMEM((pairs, width, 2 * hidden), BF16)] * 2
        + [pltpu.VMEM((max(pairs - 1, 1), width, 2 * hidden), BF16)]
        + [pltpu.SemaphoreType.DMA((pairs,))] * 4
        + [pltpu.SemaphoreType.DMA((3, blocks))] * 2
        + [pltpu.SemaphoreType.DMA(())],
        2 * rows * width * hidden * size * 6,
        rows * width * 20,
        group=1,
    )


LEVELS = 4
PARTS = 3


def back_kernel(
    head_dim,
    local,
    near_size,
    far_size,
    dense_steps,
    q_ref,
    k_ref,
    v_ref,
    ga_ref,
    rinv_ref,
    att_ref,
    n1_ref,
    wt_ref,
    p_ref,
    idx_ref,
    ffn_ref,
    gmid_ref,
    stats_ref,
    x_ref,
    g1_ref,
    b1_ref,
    gproj_ref,
    gub_ref,
    sums2_ref,
    act_ref,
    base_ref,
    second_ref,
    wm_ref,
    g0_ref,
    raw_ref,
    gin_ref,
    ffnsum_ref,
    main_ref,
    tail_ref,
    full_ref,
    sums_ref,
    q_s,
    k_s,
    v_s,
    ga_s,
    rinv_s,
    att_s,
    n1_s,
    wt_s,
    gq_s,
    gk_s,
    gv_s,
    ds_s,
    base_s,
    mask_s,
    gtab_s,
    ffncame_s,
    ffnown_s,
    merge_s,
    merged_s,
    mnear_s,
    mfar_s,
    mpiece_s,
    tparts_s,
    tnear_s,
    tfar_s,
    parts_s,
    pnear_s,
    pfar_s,
    main_s,
    mainsum_s,
    tails_s,
    linein_s,
    lineout_s,
    lines_s,
    n0_s,
    inv0_s,
    wm_s,
    down_s,
    in_sems,
    more_sems,
    late_sems,
    out_sems,
    sems,
):
    step = pl.program_id(0)
    rows, width = gq_s.shape
    lanes = GROUP * head_dim
    groups = width // lanes
    scale = 1.0 / math.sqrt(head_dim)
    sets = p_ref.shape[2]
    block = rows // sets
    jump = block // TILE - 1
    pairs = near_size // 2
    span = local * head_dim
    me, deep = lax.axis_index("mp"), lax.axis_index("dp")
    beside = list(range(1, near_size))
    behind = list(range(1, far_size))
    evens = list(range(2, near_size, 2))
    piece = ffnsum_ref.shape[1]
    at_sem = [0]

    def copy(axis, r, src, dst):
        at_sem[0] += 2
        return send(axis, r, src, dst, sems.at[at_sem[0] - 2], sems.at[at_sem[0] - 1])

    def rows_at(ref, index, count):
        return ref.at[pl.ds(pl.multiple_of(index * count, TILE), count)]

    def bring(level):
        copies = []
        whence = (
            (q_ref, q_s),
            (k_ref, k_s),
            (v_ref, v_s),
            (ga_ref, ga_s),
            (rinv_ref, rinv_s),
            (att_ref, att_s),
        )
        part = TILE // LEVELS * jump
        first = COVER - jump
        for i, (src, dst) in enumerate(whence):
            for u in range(sets):
                if level == 0:
                    here = pl.ds(u * block, part + first)
                else:
                    here = pl.ds(u * block + first + level * part, part)
                copies.append(
                    pltpu.make_async_copy(src.at[here], dst.at[here], in_sems.at[i, level, u])
                )
        return copies

    def bring_more():
        return [
            pltpu.make_async_copy(n1_ref, n1_s, more_sems.at[0]),
            pltpu.make_async_copy(wt_ref, wt_s, more_sems.at[1]),
        ]

    act_bufs = (k_s, v_s, ga_s, rinv_s)
    chunks = act_ref.shape[0] * act_ref.shape[2] // width

    def bring_late():
        copies = [(base_ref, att_s), (wm_ref, wm_s)]
        per = act_ref.shape[2]
        each = width // per
        for p in range(act_ref.shape[0]):
            dst = act_bufs[p // each].at[:, pl.ds(p % each * per, per)]
            copies.append((act_ref.at[p], dst))
        hidden = per // 2
        for r in range(near_size):
            src = second_ref.at[r, pl.ds(hidden, hidden)]
            copies.append((src, down_s.at[pl.ds(r * hidden, hidden)]))
        return [
            pltpu.make_async_copy(src, dst, late_sems.at[i]) for i, (src, dst) in enumerate(copies)
        ]

    def dense_span(j):
        return pl.ds(j * (rows // PARTS), rows // PARTS)

    def take_gin(j):
        here = dense_span(j)
        return pltpu.make_async_copy(n0_s.at[here], gin_ref.at[here], out_sems.at[0, j])

    def take_raw(j):
        here = dense_span(j)
        return pltpu.make_async_copy(att_s.at[here], raw_ref.at[here], out_sems.at[1, j])

    def input_part(j):
        here = dense_span(j)
        grad_low = dot_rt(q_s[here, :], wm_s[...])
        normed = n0_s[here, :].astype(F32)
        grad = norm_back(grad_low * g0_ref[...], normed, inv0_s[here, :1])
        n0_s[here, :] = grad.astype(BF16)
        take_gin(j).start()

    def output_part(j):
        here = dense_span(j)
        total = att_s[here, :].astype(F32)
        for i in range(chunks):
            total = total + dot(act_bufs[i][here, :], down_s[i * width : (i + 1) * width, :])
        att_s[here, :] = total.astype(BF16)
        take_raw(j).start()

    def keep_main():
        return pltpu.make_async_copy(mainsum_s, main_ref.at[deep], more_sems.at[3])

    def keep_merge(h):
        src = mpiece_s.at[h, 0]
        return pltpu.make_async_copy(src, full_ref.at[h, me, deep], more_sems.at[4 + h])

    def keep_ffn():
        return pltpu.make_async_copy(ffnown_s, ffnsum_ref.at[deep], more_sems.at[2])

    ffn_out = [
        copy("dp", r, rows_at(ffn_ref, partner("dp", r), piece), ffncame_s.at[r]) for r in behind
    ]
    ffn_all = [copy("dp", r, ffnown_s, ffnsum_ref.at[deep]) for r in behind]

    halves = mfar_s.shape[0]
    half_rows = merged_s.shape[0] // halves
    share = half_rows // near_size
    small = share // far_size
    main_piece = parts_s.shape[1] // far_size

    def share_at(h, index):
        return h * half_rows + index * share

    def share_of(h, index):
        return merged_s.at[pl.ds(pl.multiple_of(share_at(h, index), TILE), share)]

    mnear, mfar, across, back, spread, onward = [], [], [], [], [], []
    for h in range(halves):
        mnear.append([])
        for p in range(pairs):
            src = share_of(h, partner("mp", 2 * p + 1))
            mnear[h].append(copy("mp", 1, src, mnear_s.at[h, p]))
        mfar.append({})
        for p in range(1, pairs):
            src = share_of(h, partner("mp", 2 * p))
            mfar[h][p] = copy("mp", 2 * p, src, mfar_s.at[h, p])
        across.append([])
        for r in behind:
            src = rows_at(mfar_s.at[h, 0], partner("dp", r), small)
            across[h].append(copy("dp", r, src, mpiece_s.at[h, r]))
        mine = full_ref.at[h, me]
        back.append([copy("dp", r, mpiece_s.at[h, 0], mine.at[deep]) for r in behind])
        spread.append([copy("mp", r, mine, mine) for r in evens + [1]])
        onward.append([])
        for r in evens:
            came = full_ref.at[h, partner("mp", r)]
            onward[h].append(copy("mp", 1, came, came))
    lines_in = [copy("mp", r, linein_s.at[0], linein_s.at[r]) for r in beside]
    lines_out = [copy("dp", r, lineout_s.at[0], lineout_s.at[r]) for r in behind]
    pnear = [copy("mp", 1, parts_s.at[2 * p + 1], pnear_s.at[p]) for p in range(pairs)]
    pfar = {p: copy("mp", 2 * p, parts_s.at[2 * p], pfar_s.at[p]) for p in range(1, pairs)}
    main_out = [
        copy("dp", r, rows_at(parts_s.at[0], partner("dp", r), main_piece), main_s.at[r])
        for r in behind
    ]
    main_all = [copy("dp", r, mainsum_s, main_ref.at[deep]) for r in behind]
    tnear = [copy("mp", 1, tparts_s.at[2 * p + 1], tnear_s.at[p]) for p in range(pairs)]
    tfar = {p: copy("mp", 2 * p, tparts_s.at[2 * p], tfar_s.at[p]) for p in range(1, pairs)}
    tails = [copy("dp", r, tparts_s.at[0], tails_s.at[r]) for r in behind]

    @pl.when(step == 0)
    def _():
        for level in range(LEVELS):
            for c in bring(level):
                c.start()
        for c in bring_more():
            c.start()
        greet([("mp", r) for r in beside] + [("dp", r) for r in behind])
        for c in ffn_out:
            c.start()
        mask_s[...] = head_mask(head_dim)
        gq_s[...] = jnp.zeros_like(gq_s)
        gk_s[...] = jnp.zeros_like(gk_s)
        gv_s[...] = jnp.zeros_like(gv_s)

    @pl.when(step == TILE // 2)
    def _():
        total = ffn_ref[pl.ds(pl.multiple_of(deep * piece, TILE), piece), :].astype(F32)
        for c, r in zip(ffn_out, behind):
            c.wait_recv()
            total = total + ffncame_s[r].astype(F32)
        ffnown_s[...] = total.astype(BF16)
        keep_ffn().start()
        for c in ffn_all:
            c.start()

    for level in range(LEVELS):

        @pl.when(step == level * (TILE // LEVELS))
        def _():
            for c in bring(level):
                c.wait()

    @pl.when(step < TILE)
    def _():
        mask = mask_s[...]
        minus = -mask
        starts = [pl.multiple_of(step * jump + u * block, TILE) for u in range(sets)]
        lane_head = lax.broadcasted_iota(jnp.int32, (COVER, 2 * lanes), 1) % lanes // head_dim
        zeros = jnp.zeros((COVER, lanes), BF16)
        units = [(u, g) for g in range(groups) for u in range(sets)]

        def at(ref, u, g):
            return ref[pl.ds(starts[u], COVER), pl.ds(g * lanes, lanes)]

        scaled = [at(ga_s, u, g) * at(rinv_s, u, g) for u, g in units]
        grads = []
        for (u, g), ga in zip(units, scaled):
            left = jnp.concatenate([ga, ga * at(att_s, u, g)], axis=1)
            right = jnp.concatenate([tiled(at(v_s, u, g), mask), minus], axis=1)
            grads.append(dot_rt(left, right))
        score_grads = []
        totals = {}
        for (u, g), grad in zip(units, grads):
            ds = p_ref[g, 0, u].astype(F32) * grad
            totals[g] = ds if g not in totals else totals[g] + ds
            score_grads.append(ds.astype(BF16))
        for g in range(groups):
            ds_s[step, g] = totals[g]
        query_grads = []
        for (u, g), ds in zip(units, score_grads):
            query_grads.append(dot(ds, tiled(at(k_s, u, g), mask)))
        pair_grads = []
        for (u, g), ds, ga in zip(units, score_grads, scaled):
            left = jnp.concatenate([ds, p_ref[g, 0, u]], axis=0)
            right = jnp.concatenate(
                [
                    jnp.concatenate([at(q_s, u, g), zeros], axis=1),
                    jnp.concatenate([zeros, ga], axis=1),
                ],
                axis=0,
            )
            pair_grads.append(dot_lt(left, right))
        for (u, g), grad_q, grad_kv in zip(units, query_grads, pair_grads):
            here, cols = pl.ds(starts[u], COVER), pl.ds(g * lanes, lanes)
            gq_s[here, cols] += (grad_q * scale).astype(BF16)
            both = jnp.where(lane_head == 0, grad_kv[:COVER], 0.0)
            for h in range(1, GROUP):
                both = jnp.where(lane_head == h, grad_kv[h * COVER : (h + 1) * COVER], both)
            both = both.astype(BF16)
            gk_s[here, cols] += both[:, :lanes]
            gv_s[here, cols] += both[:, lanes:]

    def table_grads():
        def unshift(g, _):
            full = ds_s[0, g]
            for o in range(1, TILE):
                turned = pltpu.roll(ds_s[o, g], COVER - o, 0)
                full = full + pltpu.roll(turned, GROUP * COVER - o, 1)
            for h in range(GROUP):
                base_s[g * GROUP + h] = full[:, h * COVER : (h + 1) * COVER]
            return 0

        lax.fori_loop(0, groups, unshift, 0)
        sums = []
        for pair in range((idx_ref.shape[0] + 1) // 2):
            onehot = index_onehot(pair_row(idx_ref, pair), gtab_s.shape[1])
            vals = jnp.concatenate([base_s[:, 2 * pair, :], base_s[:, 2 * pair + 1, :]], axis=1)
            high = vals.astype(BF16)
            both = jnp.concatenate([high, (vals - high.astype(F32)).astype(BF16)], axis=0)
            sums.append(dot_rt(both, onehot))
        count = base_s.shape[0]
        grad = sums[0]
        for x in sums[1:]:
            grad = grad + x
        gtab_s[...] = grad[:count] + grad[count:]

    @pl.when(step == TILE)
    def _():
        for c in bring_late():
            c.start()
        merge_s[...] = jnp.zeros_like(merge_s)
        lines_s[...] = jnp.zeros_like(lines_s)
        for c in bring_more():
            c.wait()
        normed_t = n1_s[...].T
        for t, ref in enumerate((gq_s, gk_s, gv_s)):
            grad = dot(normed_t, ref[...]).T
            sums = jnp.sum(ref[...].astype(F32), axis=0, keepdims=True)
            lines_s[4 + t : 5 + t, :] = sums
            sums = jnp.broadcast_to(sums, (8, width)).T[:, :1]
            grad = (grad * g1_ref[...] + sums * b1_ref[...]).astype(BF16)
            for r in range(near_size):
                parts_s[r, t * span : (t + 1) * span, :] = grad[r * span : (r + 1) * span]
        for r in range(near_size):
            parts_s[r, 3 * span :, :] = gproj_ref[r * span : (r + 1) * span, :]
        for c in pnear:
            c.start()

    @pl.when(step == TILE + 2)
    def _():
        for p in reversed(range(pairs)):
            pnear[p].wait_recv()
            joined = parts_s[2 * p].astype(F32) + pnear_s[p].astype(F32)
            parts_s[2 * p] = joined.astype(BF16)
            if p:
                pfar[p].start()

    @pl.when(step >= TILE)
    def _():
        count = gmid_ref.shape[0]
        here = pl.ds(pl.multiple_of((step - TILE) * count, TILE), count)
        grad_mid = None
        for t, ref in enumerate((gq_s, gk_s, gv_s)):
            part = dot(ref[here, :], wt_s[t * width : (t + 1) * width, :])
            grad_mid = part if grad_mid is None else grad_mid + part
        stats = stats_ref[...]
        normed1 = n1_s[here, :].astype(F32)
        lines_s[0:1, :] += jnp.sum(grad_mid * normed1, axis=0, keepdims=True)
        lines_s[1:2, :] += jnp.sum(grad_mid, axis=0, keepdims=True)
        grad_merged = gmid_ref[...].astype(F32) + norm_back(
            grad_mid * g1_ref[...], normed1, stats[:, 3:4]
        )
        lines_s[2:3, :] += jnp.sum(grad_merged, axis=0, keepdims=True)
        grad_merged = grad_merged.astype(BF16)
        q_s[here, :] = grad_merged
        normed0 = ((x_ref[...].astype(F32) - stats[:, 0:1]) * stats[:, 1:2]).astype(BF16)
        n0_s[here, :] = normed0
        inv0_s[here, :] = jnp.broadcast_to(stats[:, 1:2], (count, inv0_s.shape[1]))
        merge_s[...] += dot_lt(grad_merged, normed0)

    @pl.when(step == TILE + dense_steps - 1)
    def _():
        narrow = merged_s.shape[1]
        per_half = merge_s.shape[1] // narrow // halves
        for h in range(halves):
            for j in range(h * per_half, (h + 1) * per_half):
                part = merge_s[:, j * narrow : (j + 1) * narrow]
                merged_s[j * width : (j + 1) * width, :] = part.astype(BF16)
            for c in mnear[h]:
                c.start()
        linein_s[0] = jnp.concatenate([sums2_ref[0:4, :], lines_s[0:4, :]], axis=0)
        for c in lines_in:
            c.start()
        for c in bring_late():
            c.wait()
        table_grads()
        for r in range(near_size):
            bias_sums = lines_s[4:7, r * span : (r + 1) * span]
            hidden = gub_ref.shape[2] // 2
            half = (r % 2) * hidden
            lines = [
                fill(bias_sums, width),
                fill(gtab_s[r * local : (r + 1) * local, :], width),
                fill(gub_ref[r // 2][:, half : half + hidden], width),
                jnp.zeros((TILE - 4 - local, width), F32),
            ]
            tparts_s[r] = jnp.concatenate(lines, axis=0).astype(BF16)
        for h in range(halves):
            for p in reversed(range(pairs)):
                mnear[h][p].wait_recv()
                spot = pl.ds(pl.multiple_of(share_at(h, partner("mp", 2 * p)), TILE), share)
                joined = merged_s[spot, :].astype(F32) + mnear_s[h, p].astype(F32)
                merged_s[spot, :] = joined.astype(BF16)
                if p:
                    mfar[h][p].start()
        for c in tnear:
            c.start()
        total = linein_s[0]
        for c, r in zip(lines_in, beside):
            c.wait_recv()
            total = total + linein_s[r]
        lineout_s[0] = total
        for c in lines_out:
            c.start()
        input_part(0)

        total = parts_s[0].astype(F32)
        for p in reversed(range(1, pairs)):
            pfar[p].wait_recv()
            total = total + pfar_s[p].astype(F32)
        parts_s[0] = total.astype(BF16)
        for c in main_out:
            c.start()
        for h in range(halves):
            mine = pl.ds(pl.multiple_of(share_at(h, me), TILE), share)
            total = merged_s[mine, :].astype(F32)
            for p in reversed(range(1, pairs)):
                mfar[h][p].wait_recv()
                total = total + mfar_s[h, p].astype(F32)
            mfar_s[h, 0] = total.astype(BF16)
            for c in across[h]:
                c.start()
        for p in reversed(range(pairs)):
            tnear[p].wait_recv()
            tparts_s[2 * p] = (tparts_s[2 * p].astype(F32) + tnear_s[p].astype(F32)).astype(BF16)
            if p:
                tfar[p].start()
        input_part(1)

        for h in range(halves):
            spot = pl.ds(pl.multiple_of(deep * small, TILE), small)
            total = mfar_s[h, 0, spot, :].astype(F32)
            for c, r in zip(across[h], behind):
                c.wait_recv()
                total = total + mpiece_s[h, r].astype(F32)
            mpiece_s[h, 0] = total.astype(BF16)
            keep_merge(h).start()
            for c in back[h]:
                c.start()
        spot = pl.ds(pl.multiple_of(deep * main_piece, TILE), main_piece)
        total = parts_s[0, spot, :].astype(F32)
        for c, r in zip(main_out, behind):
            c.wait_recv()
            total = total + main_s[r].astype(F32)
        mainsum_s[...] = total.astype(BF16)
        keep_main().start()
        for c in main_all:
            c.start()
        input_part(2)

        for h in range(halves):
            keep_merge(h).wait()
            for c in back[h]:
                c.wait_recv()
            for c in spread[h]:
                c.start()
        total = tparts_s[0].astype(F32)
        for p in reversed(range(1, pairs)):
            tfar[p].wait_recv()
            total = total + tfar_s[p].astype(F32)
        tparts_s[0] = total.astype(BF16)
        for c in tails:
            c.start()
        output_part(0)
        output_part(1)
        for h in range(halves):
            for c, after in zip(spread[h], onward[h]):
                c.wait_recv()
                after.start()
            if h == 0:
                output_part(2)

        total = lineout_s[0]
        for c, r in zip(lines_out, behind):
            c.wait_recv()
            total = total + lineout_s[r]
        sums_ref[...] = total
        total = tparts_s[0].astype(F32)
        for c, r in zip(tails, behind):
            c.wait_recv()
            total = total + tails_s[r].astype(F32)
        tail_ref[...] = total
        for h in range(halves):
            spread[h][-1].wait_recv()
            for c in onward[h]:
                c.wait_recv()
        for c in main_all + ffn_all:
            c.wait_recv()
        keep_ffn().wait()
        keep_main().wait()
        for h in range(halves):
            for c in mnear[h] + list(mfar[h].values()) + across[h] + back[h] + spread[h]:
                c.wait_send()
            for c in onward[h]:
                c.wait_send()
        for c in ffn_out + ffn_all + lines_in + lines_out + tnear + list(tfar.values()):
            c.wait_send()
        for c in pnear + list(pfar.values()) + main_out + tails + main_all:
            c.wait_send()
        for j in range(PARTS):
            take_gin(j).wait()
            take_raw(j).wait()


def back_rows(
    q,
    k,
    v,
    ga,
    rinv,
    att,
    n1,
    wt,
    p,
    idx,
    ffn,
    gmid,
    stats,
    x,
    g1,
    b1,
    gproj,
    gub,
    sums2,
    act,
    base,
    second,
    wm,
    g0,
    table_width,
    head_dim,
    local,
    near_size,
    far_size,
):
    rows, width = q.shape
    wide = x.shape[1]
    heads = width // head_dim
    groups, steps, sets, _, cover = p.shape
    dense_steps = 7
    count = rows // dense_steps
    narrow = 256
    pairs = near_size // 2
    piece = (ffn.shape[0] // far_size, ffn.shape[1])
    part = (4 * local * head_dim, width)
    main_piece = (4 * local * head_dim // far_size, width)
    total_rows = wide // narrow * width
    halves = 2 if total_rows // (2 * near_size * far_size) % TILE == 0 else 1
    share = total_rows // halves // near_size
    small = share // far_size
    near, far = near_size - 1, far_size - 1
    copies = 2 * far + halves * (4 * pairs - 2 + 2 * far) + near + far
    copies += (2 * pairs - 1) + 2 * far + (2 * pairs - 1) + far

    def place(i):
        return (jnp.maximum(i - steps, 0), 0)

    def p_place(i):
        return (0, jnp.minimum(i, steps - 1), 0, 0, 0)

    return call(
        functools.partial(back_kernel, head_dim, local, near_size, far_size, dense_steps),
        steps + dense_steps,
        (q, k, v, ga, rinv, att, n1, wt, p, idx, ffn, gmid, stats, x, g1, b1, gproj, gub, sums2)
        + (act, base, second, wm, g0),
        [anywhere()] * 8
        + [
            pl.BlockSpec((groups, 1, sets, COVER, cover), p_place),
            whole(idx.shape),
            whole(ffn.shape),
            pl.BlockSpec((count, width), place),
            pl.BlockSpec((count, 8), place),
            pl.BlockSpec((count, wide), place),
            whole(g1.shape),
            whole(b1.shape),
            whole(gproj.shape),
            whole(gub.shape),
            whole(sums2.shape),
        ]
        + [anywhere()] * 4
        + [whole(g0.shape)],
        [
            jax.ShapeDtypeStruct((rows, width), BF16),
            jax.ShapeDtypeStruct((rows, wide), BF16),
            jax.ShapeDtypeStruct((far_size,) + piece, BF16),
            jax.ShapeDtypeStruct((far_size,) + main_piece, BF16),
            jax.ShapeDtypeStruct((TILE, width), F32),
            jax.ShapeDtypeStruct((halves, near_size, far_size, small, narrow), BF16),
            jax.ShapeDtypeStruct((8, width), F32),
        ],
        [
            anywhere(),
            anywhere(),
            anywhere(),
            anywhere(),
            whole((TILE, width)),
            anywhere(),
            whole((8, width)),
        ],
        [pltpu.VMEM((rows, width), BF16)] * 7
        + [pltpu.VMEM((3 * width, width), BF16)]
        + [pltpu.VMEM((rows, width), BF16)] * 3
        + [
            pltpu.VMEM((TILE, groups, COVER, cover), F32),
            pltpu.VMEM((heads, COVER, COVER), F32),
            pltpu.VMEM((cover, GROUP * head_dim), BF16),
            pltpu.VMEM((heads, table_width), F32),
            pltpu.VMEM((far_size,) + piece, BF16),
            pltpu.VMEM(piece, BF16),
            pltpu.VMEM((width, wide), F32),
            pltpu.VMEM((total_rows, narrow), BF16),
            pltpu.VMEM((halves, pairs, share, narrow), BF16),
            pltpu.VMEM((halves, pairs, share, narrow), BF16),
            pltpu.VMEM((halves, far_size, small, narrow), BF16),
            pltpu.VMEM((near_size, TILE, width), BF16),
            pltpu.VMEM((pairs, TILE, width), BF16),
            pltpu.VMEM((pairs, TILE, width), BF16),
            pltpu.VMEM((near_size,) + part, BF16),
            pltpu.VMEM((pairs,) + part, BF16),
            pltpu.VMEM((pairs,) + part, BF16),
            pltpu.VMEM((far_size,) + main_piece, BF16),
            pltpu.VMEM(main_piece, BF16),
            pltpu.VMEM((far_size, TILE, width), BF16),
            pltpu.VMEM((near_size, 8, width), F32),
            pltpu.VMEM((far_size, 8, width), F32),
            pltpu.VMEM((8, width), F32),
            pltpu.VMEM((rows, wide), BF16),
            pltpu.VMEM((rows, 128), F32),
            pltpu.VMEM(wm.shape, BF16),
            pltpu.VMEM((act.shape[0] * act.shape[2], width), BF16),
            pltpu.SemaphoreType.DMA((6, LEVELS, sets)),
            pltpu.SemaphoreType.DMA((4 + halves,)),
            pltpu.SemaphoreType.DMA((2 + act.shape[0] + near_size,)),
            pltpu.SemaphoreType.DMA((2, PARTS)),
            pltpu.SemaphoreType.DMA((2 * copies,)),
        ],
        2 * rows * width * (24 * width + wide),
        rows * width * 20,
        group=2,
    )


def last_kernel(
    head_dim,
    local,
    window,
    live_ref,
    raw_ref,
    gin16_ref,
    wm_ref,
    g0_ref,
    b0_ref,
    main_ref,
    ffn_ref,
    full_ref,
    sums_ref,
    tail_ref,
    out_ref,
    gin_ref,
    gain0_ref,
    bias0_ref,
    gmerge_ref,
    gqkv_ref,
    gproj_ref,
    gup_ref,
    gdown_ref,
    gqb_ref,
    gtab_ref,
    gub_ref,
    *line_refs,
):
    step = pl.program_id(0)
    count, width = raw_ref.shape
    rows = count * pl.num_programs(0)
    live = live_rows(live_ref, step * count, count, rows, width, window)
    out_ref[...] = jnp.where(live, raw_ref[...].astype(F32), 0.0)
    gin_ref[...] = gin16_ref[...].astype(F32)

    @pl.when(step == 0)
    def _():
        span = local * head_dim
        main = main_ref[...].astype(F32)
        order = [
            main[t * span + l * head_dim : t * span + (l + 1) * head_dim]
            for l in range(local)
            for t in range(3)
        ]
        grad = jnp.concatenate(order, axis=0).T
        for l in range(local):
            gqkv_ref[:, l, :] = grad[:, 3 * l * head_dim : 3 * (l + 1) * head_dim]
        gproj_ref[...] = main[3 * span :]
        rows_of = []
        for l in range(local):
            here = slice(l * head_dim, (l + 1) * head_dim)
            rows_of.append(
                jnp.concatenate([tail_ref[t : t + 1, here] for t in range(3)], axis=1)
            )
        gqb_ref[...] = jnp.concatenate(rows_of, axis=0)
        gtab_ref[...] = tail_ref[3 : 3 + local, : gtab_ref.shape[1]]
        gub_ref[...] = tail_ref[3 + local : 4 + local, : gub_ref.shape[1]]
        for i, ref in enumerate(line_refs):
            ref[...] = sums_ref[i : i + 1, :]

    @pl.when(step == 1)
    def _():
        hidden = gup_ref.shape[1]
        gup_ref[...] = ffn_ref[:, :hidden].astype(F32)
        gdown_ref[...] = ffn_ref[:, hidden:].astype(F32).T

    narrow = full_ref.shape[2]
    low_sum = sums_ref[6:7, :]
    for j in range(full_ref.shape[0]):

        @pl.when(step == 2 + j)
        def _():
            cols = pl.ds(j * narrow, narrow)
            grad = full_ref[j].astype(F32).T
            weight = wm_ref[cols, :].astype(F32)
            gain = jnp.sum(weight * grad, axis=1, keepdims=True)
            shift = jnp.sum(weight * low_sum, axis=1, keepdims=True)
            gain0_ref[:, cols] = jnp.broadcast_to(gain, (narrow, 128)).T[:1, :]
            bias0_ref[:, cols] = jnp.broadcast_to(shift, (narrow, 128)).T[:1, :]
            scale = jnp.broadcast_to(g0_ref[:, cols], (8, narrow)).T[:, :1]
            offset = jnp.broadcast_to(b0_ref[:, cols], (8, narrow)).T[:, :1]
            gmerge_ref[cols, :] = grad * scale + offset * low_sum


def last_rows(
    live, raw, gin16, wm, g0, b0, main, ffn, full, sums, tail, local, head_dim, rel, window
):
    rows, width = raw.shape
    wide = gin16.shape[1]
    step = rows // 7
    hidden = ffn.shape[1] // 2
    span = local * head_dim
    narrow_block = pl.BlockSpec((step, width), lambda i: (i, 0))
    wide_block = pl.BlockSpec((step, wide), lambda i: (i, 0))
    rest = [wm, g0, b0, main, ffn, full, sums, tail]
    shapes = [
        (1, wide),
        (1, wide),
        (wide, width),
        (width, local, 3 * head_dim),
        (span, width),
        (width, hidden),
        (hidden, width),
        (local, 3 * head_dim),
        (local, rel),
        (1, hidden),
    ] + [(1, width)] * 6
    return call(
        functools.partial(last_kernel, head_dim, local, window),
        7,
        [live, raw, gin16] + rest,
        [pl.BlockSpec(memory_space=pltpu.SMEM), narrow_block, wide_block]
        + [whole(a.shape) for a in rest],
        [
            jax.ShapeDtypeStruct((rows, width), F32),
            jax.ShapeDtypeStruct((rows, wide), F32),
        ]
        + [jax.ShapeDtypeStruct(shape, F32) for shape in shapes],
        [narrow_block, wide_block] + [whole(shape) for shape in shapes],
        [],
        2 * rows * width,
        rows * wide * 9,
    )


def shards(
    inputs,
    norm0_gain,
    norm0_bias,
    merge_weight,
    norm1_gain,
    norm1_bias,
    qkv_weight,
    qkv_bias,
    rel_table,
    rel_index,
    regions,
    live_windows,
    proj_weight,
    proj_bias,
    norm2_gain,
    norm2_bias,
    up_weight,
    up_bias,
    down_weight,
    down_bias,
    cotangent,
    n_dp,
    n_mp,
):
    micro, strip_rows, wide = inputs.shape
    width = merge_weight.shape[1]
    win = rel_index.shape[0]
    local, packed = qkv_bias.shape
    head_dim = packed // 3
    heads = local * n_mp
    hidden = up_bias.shape[0]
    rel = rel_table.shape[1]
    rows = micro * strip_rows
    windows = rows // win
    sets = windows // TILE
    strip = lax.axis_index("mp")

    region = lax.dynamic_slice_in_dim(regions, strip * strip_rows, strip_rows, axis=1)
    region = region.reshape(sets, rows // sets)
    jump = rows // sets // TILE - 1
    region = jnp.stack([region[:, o * jump : o * jump + COVER] for o in range(TILE)])
    region = jnp.tile(region[:, :, None, :], (1, 1, 1, GROUP))
    table_width = -(-rel // 128) * 128
    vecs = (proj_bias[None], norm2_gain[None], norm2_bias[None], down_bias[None])
    gain0, bias0 = norm0_gain[None], norm0_bias[None]
    gain1, bias1 = norm1_gain[None], norm1_bias[None]

    x = inputs.reshape(rows, wide)
    stats, n1, q, k, v, att, rinv, p, tiles, wt, second = front_rows(
        x,
        gain0,
        bias0,
        merge_weight,
        gain1,
        bias1,
        qkv_weight.reshape(width, local * packed),
        qkv_bias,
        rel_table,
        up_bias[None],
        up_weight,
        down_weight,
        proj_weight.reshape(local * head_dim, width),
        rel_index,
        region,
        n_mp,
        head_dim,
    )
    base, act, gmid, gatt, ffn_part, gub, gproj, sums2 = ffn_rows(
        live_windows,
        n1,
        att,
        cotangent.reshape(rows, width),
        stats,
        tiles,
        second,
        vecs,
        local,
        hidden,
        win,
    )
    raw, gin16, ffn_sum, main, tail, gmerge, sums = back_rows(
        q,
        k,
        v,
        gatt,
        rinv,
        att,
        n1,
        wt,
        p,
        rel_index,
        ffn_part,
        gmid,
        stats,
        x,
        gain1,
        bias1,
        gproj,
        gub,
        sums2,
        act,
        base,
        second,
        merge_weight,
        gain0,
        table_width,
        head_dim,
        local,
        n_mp,
        n_dp,
    )
    span = local * head_dim
    out, grad_input, ggain0, gbias0, gmerge, gqkv, gproj, gup, gdown, gqb, gtab, gub, *lines = (
        last_rows(
            live_windows,
            raw,
            gin16,
            merge_weight,
            gain0,
            bias0,
            main.reshape(4 * span, width),
            ffn_sum.reshape(width, 2 * hidden),
            gmerge.reshape(-1, width, gmerge.shape[4]),
            sums,
            tail,
            local,
            head_dim,
            rel,
            win,
        )
    )
    gpb, gain2, bias2, gdb, gain1, bias1 = (x.reshape(width) for x in lines)
    return (
        out.reshape(micro, strip_rows, width),
        grad_input.reshape(micro, strip_rows, wide),
        ggain0.reshape(wide),
        gbias0.reshape(wide),
        gmerge,
        gain1,
        bias1,
        gqkv,
        gqb,
        gtab,
        gproj.reshape(local, head_dim, width),
        gpb,
        gain2,
        bias2,
        gup,
        gub.reshape(hidden),
        gdown,
        gdb,
    )


def solution(mesh):
    placed = (
        P(None, ("dp", "mp"), None),
        P(),
        P(),
        P(),
        P(),
        P(),
        P(None, "mp", None),
        P("mp", None),
        P("mp", None),
        P(),
        P(None, "dp"),
        P(None, "dp"),
        P("mp", None, None),
        P(),
        P(),
        P(),
        P(None, "mp"),
        P("mp"),
        P("mp", None),
        P(),
        P(None, ("dp", "mp"), None),
    )
    return jax.shard_map(
        functools.partial(shards, n_dp=mesh.shape["dp"], n_mp=mesh.shape["mp"]),
        mesh=mesh,
        in_specs=placed,
        out_specs=(
            P(None, ("dp", "mp"), None),
            P(None, ("dp", "mp"), None),
            P(),
            P(),
            P(),
            P(),
            P(),
            P(None, "mp", None),
            P("mp", None),
            P("mp", None),
            P("mp", None, None),
            P(),
            P(),
            P(),
            P(None, "mp"),
            P("mp"),
            P("mp", None),
            P(),
        ),
        check_vma=False,
    )
```

```python
import functools
import math

import jax
import jax.numpy as jnp
from jax import lax
from jax.experimental import pallas as pl
from jax.experimental.pallas import tpu as pltpu
from jax.sharding import PartitionSpec as P

F32 = jnp.float32
BF16 = jnp.bfloat16
EPSILON = 1e-05
MASKED = -1e30
COVER = 64
TILE = 16
GROUP = 4
VMEM_LIMIT = 60 << 20


def dot(left, right):
    return jnp.dot(left, right, preferred_element_type=F32)


def dot_rt(left, right):
    return lax.dot_general(left, right, (((1,), (1,)), ((), ())), preferred_element_type=F32)


def dot_lt(left, right):
    return lax.dot_general(left, right, (((0,), (0,)), ((), ())), preferred_element_type=F32)


def whole(shape):
    return pl.BlockSpec(shape, lambda i: (0,) * len(shape), pipeline_mode=pl.Buffered(1))


def anywhere():
    return pl.BlockSpec(memory_space=pl.ANY)


def call(kernel, grid, ins, in_specs, outs, out_specs, scratch, flops, nbytes, group=None):
    extra = {} if group is None else {"collective_id": group, "has_side_effects": True}
    return pl.pallas_call(
        kernel,
        grid=(grid,),
        in_specs=in_specs,
        out_specs=out_specs,
        out_shape=outs,
        scratch_shapes=scratch,
        compiler_params=pltpu.CompilerParams(
            dimension_semantics=("arbitrary",), vmem_limit_bytes=VMEM_LIMIT, **extra
        ),
        cost_estimate=pl.CostEstimate(flops=flops, bytes_accessed=nbytes, transcendentals=0),
    )(*ins)


def partner(axis, flips):
    at = lax.axis_index(axis)
    bit = 1
    while bit <= flips:
        if flips & bit:
            at = at + bit * (1 - 2 * lax.rem(lax.div(at, jnp.int32(bit)), jnp.int32(2)))
        bit *= 2
    return at


def send(axis, flips, src, dst, send_sem, recv_sem):
    return pltpu.make_async_remote_copy(
        src_ref=src,
        dst_ref=dst,
        send_sem=send_sem,
        recv_sem=recv_sem,
        device_id={axis: partner(axis, flips)},
        device_id_type=pl.DeviceIdType.MESH,
    )


def greet(peers):
    barrier = pltpu.get_barrier_semaphore()
    for axis, flips in peers:
        pl.semaphore_signal(
            barrier,
            inc=1,
            device_id={axis: partner(axis, flips)},
            device_id_type=pl.DeviceIdType.MESH,
        )
    pl.semaphore_wait(barrier, len(peers))


class Gather:
    def __init__(self, axis, size, own, held, send_sems, recv_sems, own_sem):
        self.axis, self.size, self.own, self.held = axis, size, own, held
        self.send_sems, self.recv_sems, self.own_sem = send_sems, recv_sems, own_sem

    def straight(self, r):
        return send(
            self.axis, r, self.own, self.held.at[r], self.send_sems.at[r], self.recv_sems.at[r]
        )

    def onward(self, r):
        return send(
            self.axis,
            1,
            self.held.at[r],
            self.held.at[r + 1],
            self.send_sems.at[r + 1],
            self.recv_sems.at[r + 1],
        )

    def keep(self):
        return pltpu.make_async_copy(self.own, self.held.at[0], self.own_sem)

    def start(self, flips=None):
        evens = list(range(2, self.size, 2))
        for r in evens + [1] if flips is None else flips:
            self.straight(r).start()
        if flips is None or 1 in flips:
            self.keep().start()

    def forward(self, r):
        self.straight(r).wait_recv()
        self.onward(r).start()

    def finish(self):
        self.keep().wait()
        self.straight(1).wait()
        for r in range(2, self.size, 2):
            self.straight(r).wait_send()
            self.onward(r).wait()


def spans(total, step):
    return [(start, min(step, total - start)) for start in range(0, total, step)]


def norm_parts(values):
    mean = jnp.mean(values, axis=-1, keepdims=True)
    center = values - mean
    spread = jnp.mean(center * center, axis=-1, keepdims=True) + EPSILON
    inverse = lax.rsqrt(spread)
    return center * inverse, mean, inverse, spread


def norm_back(grad, normed, inverse):
    mean_grad = jnp.mean(grad, axis=-1, keepdims=True)
    mean_cross = jnp.mean(grad * normed, axis=-1, keepdims=True)
    return inverse * (grad - mean_grad - normed * mean_cross)


def head_mask(head_dim):
    rows = lax.broadcasted_iota(jnp.int32, (GROUP * COVER, GROUP * head_dim), 0) // COVER
    cols = lax.broadcasted_iota(jnp.int32, (GROUP * COVER, GROUP * head_dim), 1) // head_dim
    return (rows == cols).astype(F32).astype(BF16)


def tiled(block, mask):
    return jnp.concatenate([block] * GROUP, axis=0) * mask


def pair_row(idx_ref, pair):
    win = idx_ref.shape[0]
    gap = jnp.full((1, COVER - win), -1, jnp.int32)
    parts = []
    for i in (2 * pair, 2 * pair + 1):
        parts.append(idx_ref[i : i + 1, :] if i < win else jnp.full((1, win), -1, jnp.int32))
        parts.append(gap)
    return jnp.concatenate(parts, axis=1)


def index_onehot(row, table_width):
    entry = lax.broadcasted_iota(jnp.int32, (table_width, row.shape[1]), 0)
    return (entry == row).astype(F32).astype(BF16)


def fill(x, width):
    return jnp.concatenate([x, jnp.zeros((x.shape[0], width - x.shape[1]), x.dtype)], axis=1)


def front_kernel(
    head_dim,
    local,
    size,
    merge_steps,
    x_ref,
    g0_ref,
    b0_ref,
    wm_ref,
    g1_ref,
    b1_ref,
    qkvw_ref,
    qkvb_ref,
    tab_ref,
    ub_ref,
    up_ref,
    down_ref,
    proj_ref,
    idx_ref,
    rid_ref,
    stats_ref,
    n1_ref,
    q_ref,
    k_ref,
    v_ref,
    att_ref,
    rinv_ref,
    p_ref,
    tiles_ref,
    wt_ref,
    second_ref,
    first_s,
    tiles_s,
    own_s,
    tile_s,
    second_s,
    mid_s,
    q_s,
    k_s,
    v_s,
    att_s,
    rinv_s,
    base_s,
    bias_s,
    mask_s,
    tile_send,
    tile_recv,
    first_send,
    first_recv,
    second_send,
    second_recv,
    own_sems,
    out_sems,
):
    step = pl.program_id(0)
    rows, width = mid_s.shape
    heads = width // head_dim
    lanes = GROUP * head_dim
    groups = heads // GROUP
    per_group = size // groups
    scale = 1.0 / math.sqrt(head_dim)
    span = local * head_dim
    evens = list(range(2, size, 2))
    main = Gather("mp", size, own_s, first_s, first_send, first_recv, own_sems.at[0])
    rest = Gather("mp", size, second_s, second_ref, second_send, second_recv, own_sems.at[1])

    def tile_copy(r):
        return send("mp", r, tile_s, tiles_s.at[r], tile_send.at[r], tile_recv.at[r])

    @pl.when(step == 0)
    def _():
        own_s[...] = qkvw_ref[...]
        bias = qkvb_ref[...].astype(F32)
        lines = []
        for t in range(3):
            parts = [
                bias[l : l + 1, t * head_dim : (t + 1) * head_dim] for l in range(local)
            ]
            lines.append(fill(jnp.concatenate(parts, axis=1), width))
        lines.append(fill(tab_ref[...].astype(F32), width))
        lines.append(fill(ub_ref[...].astype(F32), width))
        lines.append(jnp.zeros((TILE - 4 - local, width), F32))
        tile_s[...] = jnp.concatenate(lines, axis=0).astype(BF16)
        greet([("mp", r) for r in range(1, size)])
        for r in range(1, size):
            tile_copy(r).start()
        tiles_s[0] = tile_s[...]
        main.start([r for r in evens if r < 2 * per_group] + [1])
        hidden = up_ref.shape[1]
        second_s[:hidden, :] = up_ref[...].T
        second_s[hidden : 2 * hidden, :] = down_ref[...]
        second_s[2 * hidden :, :] = proj_ref[...]

    @pl.when(step == 2)
    def _():
        main.start([r for r in evens if r >= 2 * per_group])

    @pl.when(step == merge_steps - 3)
    def _():
        rest.start()

    @pl.when(step < merge_steps)
    def _():
        count = x_ref.shape[0]
        here = pl.ds(pl.multiple_of(step * count, TILE), count)
        normed, mean, inverse, _ = norm_parts(x_ref[...].astype(F32))
        normed_in = (normed * g0_ref[...] + b0_ref[...]).astype(BF16)
        normed1, mean1, inverse1, spread1 = norm_parts(dot(normed_in, wm_ref[...]))
        n1_ref[...] = normed1.astype(BF16)
        stats = [mean, inverse, mean1, inverse1, spread1 * inverse1]
        stats_ref[...] = jnp.concatenate(stats + [mean] * (8 - len(stats)), axis=1)
        mid_s[here, :] = (normed1 * g1_ref[...] + b1_ref[...]).astype(BF16)

    table_step = merge_steps - 3

    @pl.when(step == merge_steps - 1)
    def _():
        for r in evens:
            if r < 2 * per_group:
                main.forward(r)

    @pl.when(step == table_step)
    def _():
        mask_s[...] = head_mask(head_dim)
        att_s[...] = jnp.zeros_like(att_s)
        rinv_s[...] = jnp.zeros_like(rinv_s)
        base_s[...] = jnp.full(base_s.shape, MASKED, F32)
        for r in range(1, size):
            tile_copy(r).wait_recv()

    all_pairs = list(range((idx_ref.shape[0] + 1) // 2))
    for i in range(2):

        @pl.when(step == table_step + i)
        def _():
            table = jnp.concatenate(
                [tiles_s[r].astype(F32)[3 : 3 + local, : 2 * 128] for r in range(size)], axis=0
            ).astype(BF16)
            here = all_pairs[i::2]
            rows_of = [pair_row(idx_ref, pair) for pair in here]
            found = [dot(table, index_onehot(row, table.shape[1])) for row in rows_of]
            found = [jnp.where(row < 0, MASKED, x) for row, x in zip(rows_of, found)]
            for pair, vals in zip(here, found):
                base_s[:, 2 * pair, :] = vals[:, :COVER]
                base_s[:, 2 * pair + 1, :] = vals[:, COVER:]

    @pl.when(step == table_step + 2)
    def _():
        tiles_ref[...] = tiles_s[...]

        def shift(g, _):
            full = jnp.concatenate([base_s[g * GROUP + h] for h in range(GROUP)], axis=1)
            for o in range(TILE):
                bias_s[g, o] = pltpu.roll(pltpu.roll(full, o, 0), o, 1) if o else full
            return 0

        lax.fori_loop(0, groups, shift, 0)
        for r in range(1, size):
            tile_copy(r).wait_send()

    def outward(ref, out, which, g):
        cols = pl.ds(pl.multiple_of(g * lanes, lanes), lanes)
        return pltpu.make_async_copy(ref.at[:, cols], out.at[:, cols], out_sems.at[which, g])

    def early_out(g):
        return [
            outward(ref, out, i, g)
            for i, (ref, out) in enumerate(((q_s, q_ref), (k_s, k_ref), (v_s, v_ref)))
        ]

    def late_out(g):
        return [outward(att_s, att_ref, 3, g), outward(rinv_s, rinv_ref, 4, g)]

    low_half = lax.broadcasted_iota(jnp.int32, (COVER, 2 * COVER), 1) < COVER
    region_of = lax.broadcasted_iota(jnp.int32, (8, GROUP * COVER), 0)
    sets = rid_ref.shape[1]
    block = rows // sets

    def attend(it, g):
        mask = mask_s[...]
        cols = pl.ds(pl.multiple_of(g * lanes, lanes), lanes)
        units = [(2 * it + i, u) for i in range(2) for u in range(sets)]
        starts = [pl.multiple_of(o * (block // TILE - 1) + u * block, TILE) for o, u in units]
        scores = []
        for start in starts:
            here = pl.ds(start, COVER)
            scores.append(dot_rt(q_s[here, cols], tiled(k_s[here, cols], mask)))
        weights = []
        for (o, u), s in zip(units, scores):
            member = (region_of == rid_ref[o, u]).astype(F32).astype(BF16)
            same = dot_lt(member[:, :COVER], member)
            s = s + bias_s[g, o] + jnp.where(same > 0.5, 0.0, MASKED)
            parts = []
            for c in range(GROUP // 2):
                x = s[:, c * 2 * COVER : (c + 1) * 2 * COVER]
                top0 = jnp.max(jnp.where(low_half, x, MASKED), axis=1, keepdims=True)
                top1 = jnp.max(jnp.where(low_half, MASKED, x), axis=1, keepdims=True)
                top = jnp.maximum(jnp.where(low_half, top0, top1), MASKED * 0.1)
                parts.append(jnp.exp(x - top).astype(BF16))
            w = jnp.concatenate(parts, axis=1)
            p_ref[0, o, u] = w
            weights.append(w)
        mixed = []
        for start, w in zip(starts, weights):
            vals = tiled(v_s[pl.ds(start, COVER), cols], mask)
            mixed.append(dot(w, jnp.concatenate([vals, mask], axis=1)))
        for start, a in zip(starts, mixed):
            here = pl.ds(start, COVER)
            total = a[:, lanes:]
            inv = jnp.where(total > 0.0, 1.0 / jnp.maximum(total, 0.5), 0.0)
            att_s[here, cols] += (a[:, :lanes] * inv).astype(BF16)
            rinv_s[here, cols] += inv.astype(BF16)

    @pl.when(step >= merge_steps)
    def _():
        g = step - merge_steps
        twice = 2 * per_group

        @pl.when(g == 0)
        def _():
            main.keep().wait()
            main.straight(1).wait_recv()
            for r in evens:
                if r < twice:
                    main.onward(r).wait_recv()

        for known in range(2, groups, 2):

            @pl.when(g == known)
            def _():
                for r in evens:
                    if known * per_group <= r < known * per_group + twice:
                        main.onward(r).wait_recv()

        @pl.when(g % 2 == 0)
        def _():
            shards = [g * per_group + j for j in range(twice)]
            cols = pl.ds(pl.multiple_of(g * lanes, 2 * lanes), 2 * lanes)
            outs = (q_s, k_s, v_s)
            part = rows // 3
            weights, biases = [], []
            for t in range(3):
                weight = []
                for s in shards:
                    for l in range(local):
                        at = (3 * l + t) * head_dim
                        weight.append(first_s[s, at : at + head_dim, :])
                    biases.append(tiles_s[s].astype(F32)[t : t + 1, :span])
                weight = jnp.concatenate(weight, axis=0)
                spot = pl.ds(pl.multiple_of(t * width + g * lanes, 2 * lanes), 2 * lanes)
                wt_ref[spot, :] = weight
                weights.append(weight.T)
            weight = jnp.concatenate(weights, axis=1)
            bias = jnp.concatenate(biases, axis=1)

            def project(i, _):
                here = pl.ds(pl.multiple_of(i * part, TILE), part)
                y = dot(mid_s[here, :], weight) + bias
                for t in range(3):
                    z = y[:, 2 * t * lanes : 2 * (t + 1) * lanes]
                    outs[t][here, cols] = (z * scale if t == 0 else z).astype(BF16)
                return 0

            lax.fori_loop(0, 3, project, 0)

        for c in early_out(g):
            c.start()

        def run(it, _):
            attend(it, g)
            return 0

        lax.fori_loop(0, TILE // 4, run, 0)

        @pl.when(g == 0)
        def _():
            for r in evens:
                if r >= twice:
                    main.forward(r)

        @pl.when(g == groups - 1)
        def _():
            for r in evens:
                rest.forward(r)

        lax.fori_loop(TILE // 4, TILE // 2, run, 0)
        for c in late_out(g):
            c.start()

        @pl.when(g == groups - 1)
        def _():
            main.straight(1).wait_send()
            for r in evens:
                main.straight(r).wait_send()
                main.onward(r).wait_send()
            rest.finish()
            for known in range(groups):
                for c in early_out(known) + late_out(known):
                    c.wait()


def front_rows(
    x, g0, b0, wm, g1, b1, qkvw, qkvb, tab, ub, up, down, proj, idx, rid, size, head_dim
):
    rows, wide = x.shape
    width = wm.shape[1]
    local = qkvb.shape[0]
    hidden = up.shape[1]
    heads = width // head_dim
    groups = heads // GROUP
    offsets, sets = rid.shape[0], rid.shape[1]
    cover = GROUP * COVER
    merge_steps = 7
    step = rows // merge_steps
    first = (3 * local * head_dim, width)
    second = (2 * hidden + local * head_dim, width)

    def place(i):
        return (jnp.minimum(i, merge_steps - 1), 0)

    def group_place(i):
        return (jnp.maximum(i - merge_steps, 0), 0, 0, 0, 0)

    small = [g0, b0, wm, g1, b1, qkvw, qkvb, tab, ub, up, down, proj, idx, rid]
    row_out = jax.ShapeDtypeStruct((rows, width), BF16)
    sems = [pltpu.SemaphoreType.DMA((size,))] * 6
    return call(
        functools.partial(front_kernel, head_dim, local, size, merge_steps),
        merge_steps + groups,
        [x] + small,
        [pl.BlockSpec((step, wide), place)] + [whole(a.shape) for a in small],
        [jax.ShapeDtypeStruct((rows, 8), F32), row_out]
        + [row_out] * 5
        + [
            jax.ShapeDtypeStruct((groups, offsets, sets, COVER, cover), BF16),
            jax.ShapeDtypeStruct((size, TILE, width), BF16),
            jax.ShapeDtypeStruct((3 * width, width), BF16),
            jax.ShapeDtypeStruct((size,) + second, BF16),
        ],
        [pl.BlockSpec((step, 8), place), pl.BlockSpec((step, width), place)]
        + [anywhere()] * 5
        + [
            pl.BlockSpec((1, offsets, sets, COVER, cover), group_place),
            whole((size, TILE, width)),
            whole((3 * width, width)),
            anywhere(),
        ],
        [
            pltpu.VMEM((size,) + first, BF16),
            pltpu.VMEM((size, TILE, width), BF16),
            pltpu.VMEM(first, BF16),
            pltpu.VMEM((TILE, width), BF16),
            pltpu.VMEM(second, BF16),
        ]
        + [pltpu.VMEM((rows, width), BF16)] * 6
        + [
            pltpu.VMEM((heads, COVER, COVER), F32),
            pltpu.VMEM((groups, TILE, COVER, cover), F32),
            pltpu.VMEM((cover, GROUP * head_dim), BF16),
        ]
        + sems
        + [pltpu.SemaphoreType.DMA((2,)), pltpu.SemaphoreType.DMA((5, groups))],
        2 * rows * width * (wide + 18 * width),
        rows * width * 40,
        group=0,
    )


REACH = math.sqrt(2.0) / 0.3275911
CENTRE = 0.125


def centred():
    rational = (0.254829592, -0.284496736, 1.421413741, -1.453152027, 1.061405429)
    plain = [0.5 * a * REACH ** (k + 1) for k, a in enumerate(rational)]
    out = [0.0] * len(plain)
    for k, a in enumerate(plain):
        for j in range(k + 1):
            out[j] += a * math.comb(k, j) * CENTRE ** (k - j)
    return out


def gelu_and_slope(pre):
    x = pre.astype(BF16)
    t = pl.reciprocal(jnp.abs(pre) + REACH, approx=True)
    s = (t - CENTRE).astype(BF16)
    terms = [BF16(a) for a in centred()]
    poly = terms[4]
    for a in reversed(terms[:4]):
        poly = poly * s + a
    part = poly * t.astype(BF16)
    bell = jnp.exp2((x * x) * BF16(-0.5 * math.log2(math.e)))
    size = jnp.abs(x)
    act = jnp.maximum(x, BF16(0.0)) - size * (part * bell)
    under = (part - size * BF16(1.0 / math.sqrt(2.0 * math.pi))) * bell
    return act, jnp.where(x > BF16(0.0), BF16(1.0) - under, under)


def live_rows(live_ref, start, count, rows, width, window):
    micro = live_ref.shape[1]
    micro_rows = rows // micro
    before = lax.axis_index("mp") * micro_rows
    row = lax.broadcasted_iota(jnp.int32, (count, width), 0) + start
    live = None
    for m in range(micro):
        last = m * micro_rows + jnp.minimum(live_ref[0, m] * window - before, micro_rows)
        inside = (row >= m * micro_rows) & (row < last)
        live = inside if live is None else live | inside
    return live


def ffn_kernel(
    local,
    window,
    live_ref,
    n1_ref,
    att_ref,
    cot_ref,
    stats_ref,
    wp_ref,
    pb_ref,
    g2_ref,
    b2_ref,
    db_ref,
    tail_ref,
    up_ref,
    down_ref,
    base_ref,
    act_ref,
    gmid_ref,
    gatt_ref,
    part_ref,
    gub_ref,
    gproj_ref,
    sums_ref,
    base_s,
    gffn_s,
    att_s,
    n2_s,
    inv_s,
    n_s,
    go_s,
    nt_s,
    gt_s,
    act_s,
    gp_s,
    odd_s,
    even_s,
    near_s,
    far_s,
    near_send,
    near_recv,
    far_send,
    far_recv,
    in_sems,
    out_sems,
    act_sem,
):
    step = pl.program_id(0)
    pairs = even_s.shape[0]
    pair = pairs - 1 - step
    rows, width = gffn_s.shape
    blocks = spans(rows, 512)
    hidden = up_ref.shape[1]
    wp = wp_ref[...].reshape(width, width)

    def near(p):
        return send("mp", 1, odd_s.at[p % 2], near_s.at[p], near_send.at[p], near_recv.at[p])

    def far(p):
        slot = far_s.at[p - 1]
        return send("mp", 2 * p, even_s.at[p], slot, far_send.at[p], far_recv.at[p])

    def bring(b):
        here = pl.ds(*blocks[b])
        whence = ((n1_ref, n_s), (att_ref, att_s), (cot_ref, go_s))
        return [
            pltpu.make_async_copy(src.at[here], dst.at[here], in_sems.at[i, b])
            for i, (src, dst) in enumerate(whence)
        ]

    def take(which, b):
        here = pl.ds(*blocks[b])
        src, dst = ((base_s, base_ref), (go_s, gmid_ref), (n2_s, gatt_ref))[which]
        return pltpu.make_async_copy(src.at[here], dst.at[here], out_sems.at[which, b])

    def take_act():
        return pltpu.make_async_copy(act_s.at[pl.ds(0, rows)], act_ref.at[pair], act_sem)

    @pl.when(step == 0)
    def _():
        for b in range(len(blocks)):
            for c in bring(b):
                c.start()
        greet([("mp", r) for r in [1] + [2 * p for p in range(1, pairs)]])
        bias_proj, gain2, bias2, bias_down = (x[...] for x in (pb_ref, g2_ref, b2_ref, db_ref))
        act_s[rows:, :] = jnp.zeros_like(act_s[rows:, :])
        gp_s[rows:, :] = jnp.zeros_like(gp_s[rows:, :])
        nt_s[width:, :] = jnp.ones_like(nt_s[width:, :])
        down_sum = jnp.zeros((1, width), F32)
        for b, (start, count) in enumerate(blocks):
            here = pl.ds(start, count)
            for c in bring(b):
                c.wait()
            stats = stats_ref[here, :]
            merged = n_s[here, :].astype(F32) * stats[:, 4:5] + stats[:, 2:3]
            middle = merged + dot(att_s[here, :], wp) + bias_proj
            base_s[here, :] = (middle + bias_down).astype(BF16)
            take(0, b).start()
            normed, _, inverse, _ = norm_parts(middle)
            n2_s[here, :] = normed.astype(BF16)
            inv_s[here, :] = jnp.broadcast_to(inverse, (count, inv_s.shape[1]))
            normed_ffn = (normed * gain2 + bias2).astype(BF16)
            n_s[here, :] = normed_ffn
            live = live_rows(live_ref, start, count, rows, width, window)
            grad_out = jnp.where(live, go_s[here, :].astype(F32), 0.0)
            down_sum = down_sum + jnp.sum(grad_out, axis=0, keepdims=True)
            grad_low = grad_out.astype(BF16)
            go_s[here, :] = grad_low
            whole_count = -(-count // 128) * 128
            if whole_count != count:
                filler = jnp.zeros((whole_count - count, width), BF16)
                normed_ffn = jnp.concatenate([normed_ffn, filler], axis=0)
                grad_low = jnp.concatenate([grad_low, filler], axis=0)
            nt_s[:width, start : start + whole_count] = normed_ffn.T
            gt_s[:, start : start + whole_count] = grad_low.T
        sums_ref[...] = jnp.zeros_like(sums_ref)
        sums_ref[3:4, :] = down_sum
        gffn_s[...] = jnp.zeros_like(gffn_s)

    def pass_on():
        @pl.when(step > 0)
        def _():
            near(pair + 1).wait_recv()
            joined = even_s[pair + 1].astype(F32) + near_s[pair + 1].astype(F32)
            even_s[pair + 1] = joined.astype(BF16)

        for p in range(1, pairs):

            @pl.when(pair + 1 == p)
            def _():
                far(p).start()

    up_t = up_ref[...].reshape(2 * hidden, width)
    down = down_ref[...].reshape(2 * hidden, width)
    up_bias = jnp.concatenate(
        [tail_ref[i].astype(F32)[3 + local : 4 + local, :hidden] for i in range(2)], axis=1
    )
    for b, (start, count) in enumerate(blocks):
        if b == 1:
            pass_on()
        here = pl.ds(start, count)
        act, slope = gelu_and_slope(dot_rt(n_s[here, :], up_t) + up_bias)
        grad_pre = dot_rt(go_s[here, :], down).astype(BF16) * slope
        act_s[here, :] = act
        gp_s[here, :] = grad_pre
        gffn_s[here, :] += dot(grad_pre, up_t)
    take_act().start()

    @pl.when(step > 1)
    def _():
        near(pair + 2).wait_send()

    grad_up = dot(nt_s[...], gp_s[...])
    gub_ref[0] = grad_up[width : width + 1, :]
    grad_up = grad_up[:width].astype(BF16)
    even_s[pair, :, :hidden] = grad_up[:, :hidden]
    odd_s[pair % 2, :, :hidden] = grad_up[:, hidden:]
    grad_down = dot(gt_s[...], act_s[...]).astype(BF16)
    even_s[pair, :, hidden:] = grad_down[:, :hidden]
    odd_s[pair % 2, :, hidden:] = grad_down[:, hidden:]
    near(pair).start()
    take_act().wait()

    @pl.when(step == pairs - 1)
    def _():
        gain2 = g2_ref[...]
        gain_sum = jnp.zeros((1, width), F32)
        bias_sum = jnp.zeros((1, width), F32)
        proj_sum = jnp.zeros((1, width), F32)
        grad_proj = jnp.zeros((width, width), F32)
        for b, (start, count) in enumerate(blocks):
            here = pl.ds(start, count)
            grad_ffn = gffn_s[here, :]
            normed = n2_s[here, :].astype(F32)
            gain_sum = gain_sum + jnp.sum(grad_ffn * normed, axis=0, keepdims=True)
            bias_sum = bias_sum + jnp.sum(grad_ffn, axis=0, keepdims=True)
            grad_middle = go_s[here, :].astype(F32) + norm_back(
                grad_ffn * gain2, normed, inv_s[here, :1]
            )
            proj_sum = proj_sum + jnp.sum(grad_middle, axis=0, keepdims=True)
            grad_attn = grad_middle.astype(BF16)
            go_s[here, :] = grad_attn
            take(1, b).start()
            grad_proj = grad_proj + dot_lt(att_s[here, :], grad_attn)
            n2_s[here, :] = dot_rt(grad_attn, wp).astype(BF16)
            take(2, b).start()
        gproj_ref[...] = grad_proj.astype(BF16)
        sums_ref[0:1, :] = proj_sum
        sums_ref[1:2, :] = gain_sum
        sums_ref[2:3, :] = bias_sum
        near(0).wait_recv()
        total = even_s[0].astype(F32) + near_s[0].astype(F32)
        for p in range(1, pairs):
            far(p).wait_recv()
            total = total + far_s[p - 1].astype(F32)
        part_ref[...] = total.astype(BF16)
        for p in range(pairs):
            if p < 2:
                near(p).wait_send()
            if p:
                far(p).wait_send()
        for b in range(len(blocks)):
            for which in range(3):
                take(which, b).wait()


def ffn_rows(live, n1, att, cot, stats, tiles, second, vecs, local, hidden, window):
    rows, width = n1.shape
    size = tiles.shape[0]
    pairs = size // 2
    padded = -(-rows // 128) * 128
    proj_rows = width // size
    proj_at = 2 * hidden // proj_rows
    blocks = len(spans(rows, 512))
    row_out = jax.ShapeDtypeStruct((rows, width), BF16)
    return call(
        functools.partial(ffn_kernel, local, window),
        pairs,
        (live, n1, att, cot, stats, second) + vecs + (tiles, second, second),
        [
            pl.BlockSpec(memory_space=pltpu.SMEM),
            anywhere(),
            anywhere(),
            anywhere(),
            whole(stats.shape),
            pl.BlockSpec(
                (size, proj_rows, width),
                lambda i: (0, proj_at, 0),
                pipeline_mode=pl.Buffered(1),
            ),
        ]
        + [whole((1, width))] * 4
        + [
            pl.BlockSpec((2, TILE, width), lambda i: (pairs - 1 - i, 0, 0)),
            pl.BlockSpec((2, hidden, width), lambda i: (pairs - 1 - i, 0, 0)),
            pl.BlockSpec((2, hidden, width), lambda i: (pairs - 1 - i, 1, 0)),
        ],
        [
            row_out,
            jax.ShapeDtypeStruct((pairs, rows, 2 * hidden), BF16),
            row_out,
            row_out,
            jax.ShapeDtypeStruct((width, 2 * hidden), BF16),
            jax.ShapeDtypeStruct((pairs, 1, 2 * hidden), F32),
            jax.ShapeDtypeStruct((width, width), BF16),
            jax.ShapeDtypeStruct((8, width), F32),
        ],
        [
            anywhere(),
            anywhere(),
            anywhere(),
            anywhere(),
            whole((width, 2 * hidden)),
            pl.BlockSpec((1, 1, 2 * hidden), lambda i: (pairs - 1 - i, 0, 0)),
            whole((width, width)),
            whole((8, width)),
        ],
        [
            pltpu.VMEM((rows, width), BF16),
            pltpu.VMEM((rows, width), F32),
            pltpu.VMEM((rows, width), BF16),
            pltpu.VMEM((rows, width), BF16),
            pltpu.VMEM((rows, 128), F32),
            pltpu.VMEM((rows, width), BF16),
            pltpu.VMEM((rows, width), BF16),
            pltpu.VMEM((width + TILE, padded), BF16),
            pltpu.VMEM((width, padded), BF16),
            pltpu.VMEM((padded, 2 * hidden), BF16),
            pltpu.VMEM((padded, 2 * hidden), BF16),
        ]
        + [pltpu.VMEM((min(pairs, 2), width, 2 * hidden), BF16)]
        + [pltpu.VMEM((pairs, width, 2 * hidden), BF16)] * 2
        + [pltpu.VMEM((max(pairs - 1, 1), width, 2 * hidden), BF16)]
        + [pltpu.SemaphoreType.DMA((pairs,))] * 4
        + [pltpu.SemaphoreType.DMA((3, blocks))] * 2
        + [pltpu.SemaphoreType.DMA(())],
        2 * rows * width * hidden * size * 6,
        rows * width * 20,
        group=1,
    )


LEVELS = 4
PARTS = 3


def back_kernel(
    head_dim,
    local,
    near_size,
    far_size,
    dense_steps,
    q_ref,
    k_ref,
    v_ref,
    ga_ref,
    rinv_ref,
    att_ref,
    n1_ref,
    wt_ref,
    p_ref,
    idx_ref,
    ffn_ref,
    gmid_ref,
    stats_ref,
    x_ref,
    g1_ref,
    b1_ref,
    gproj_ref,
    gub_ref,
    sums2_ref,
    act_ref,
    base_ref,
    second_ref,
    wm_ref,
    g0_ref,
    raw_ref,
    gin_ref,
    ffnsum_ref,
    main_ref,
    tail_ref,
    full_ref,
    sums_ref,
    q_s,
    k_s,
    v_s,
    ga_s,
    rinv_s,
    att_s,
    n1_s,
    wt_s,
    gq_s,
    gk_s,
    gv_s,
    ds_s,
    base_s,
    mask_s,
    gtab_s,
    ffncame_s,
    ffnown_s,
    merge_s,
    merged_s,
    mnear_s,
    mfar_s,
    mpiece_s,
    tparts_s,
    tnear_s,
    tfar_s,
    parts_s,
    pnear_s,
    pfar_s,
    main_s,
    mainsum_s,
    tails_s,
    linein_s,
    lineout_s,
    lines_s,
    n0_s,
    inv0_s,
    wm_s,
    down_s,
    in_sems,
    more_sems,
    late_sems,
    out_sems,
    sems,
):
    step = pl.program_id(0)
    rows, width = gq_s.shape
    lanes = GROUP * head_dim
    groups = width // lanes
    scale = 1.0 / math.sqrt(head_dim)
    sets = p_ref.shape[2]
    block = rows // sets
    jump = block // TILE - 1
    pairs = near_size // 2
    span = local * head_dim
    me, deep = lax.axis_index("mp"), lax.axis_index("dp")
    beside = list(range(1, near_size))
    behind = list(range(1, far_size))
    evens = list(range(2, near_size, 2))
    piece = ffnsum_ref.shape[1]
    at_sem = [0]

    def copy(axis, r, src, dst):
        at_sem[0] += 2
        return send(axis, r, src, dst, sems.at[at_sem[0] - 2], sems.at[at_sem[0] - 1])

    def rows_at(ref, index, count):
        return ref.at[pl.ds(pl.multiple_of(index * count, TILE), count)]

    def bring(level):
        copies = []
        whence = (
            (q_ref, q_s),
            (k_ref, k_s),
            (v_ref, v_s),
            (ga_ref, ga_s),
            (rinv_ref, rinv_s),
            (att_ref, att_s),
        )
        part = TILE // LEVELS * jump
        first = COVER - jump
        for i, (src, dst) in enumerate(whence):
            for u in range(sets):
                if level == 0:
                    here = pl.ds(u * block, part + first)
                else:
                    here = pl.ds(u * block + first + level * part, part)
                copies.append(
                    pltpu.make_async_copy(src.at[here], dst.at[here], in_sems.at[i, level, u])
                )
        return copies

    def bring_more():
        return [
            pltpu.make_async_copy(n1_ref, n1_s, more_sems.at[0]),
            pltpu.make_async_copy(wt_ref, wt_s, more_sems.at[1]),
        ]

    act_bufs = (k_s, v_s, ga_s, rinv_s)
    chunks = act_ref.shape[0] * act_ref.shape[2] // width

    def bring_late():
        copies = [(base_ref, att_s), (wm_ref, wm_s)]
        per = act_ref.shape[2]
        each = width // per
        for p in range(act_ref.shape[0]):
            dst = act_bufs[p // each].at[:, pl.ds(p % each * per, per)]
            copies.append((act_ref.at[p], dst))
        hidden = per // 2
        for r in range(near_size):
            src = second_ref.at[r, pl.ds(hidden, hidden)]
            copies.append((src, down_s.at[pl.ds(r * hidden, hidden)]))
        return [
            pltpu.make_async_copy(src, dst, late_sems.at[i]) for i, (src, dst) in enumerate(copies)
        ]

    def dense_span(j):
        return pl.ds(j * (rows // PARTS), rows // PARTS)

    def take_gin(j):
        here = dense_span(j)
        return pltpu.make_async_copy(n0_s.at[here], gin_ref.at[here], out_sems.at[0, j])

    def take_raw(j):
        here = dense_span(j)
        return pltpu.make_async_copy(att_s.at[here], raw_ref.at[here], out_sems.at[1, j])

    def input_part(j):
        here = dense_span(j)
        grad_low = dot_rt(q_s[here, :], wm_s[...])
        normed = n0_s[here, :].astype(F32)
        grad = norm_back(grad_low * g0_ref[...], normed, inv0_s[here, :1])
        n0_s[here, :] = grad.astype(BF16)
        take_gin(j).start()

    def output_part(j):
        here = dense_span(j)
        total = att_s[here, :].astype(F32)
        for i in range(chunks):
            total = total + dot(act_bufs[i][here, :], down_s[i * width : (i + 1) * width, :])
        att_s[here, :] = total.astype(BF16)
        take_raw(j).start()

    def keep_main():
        return pltpu.make_async_copy(mainsum_s, main_ref.at[deep], more_sems.at[3])

    def keep_merge(h):
        src = mpiece_s.at[h, 0]
        return pltpu.make_async_copy(src, full_ref.at[h, me, deep], more_sems.at[4 + h])

    def keep_ffn():
        return pltpu.make_async_copy(ffnown_s, ffnsum_ref.at[deep], more_sems.at[2])

    ffn_out = [
        copy("dp", r, rows_at(ffn_ref, partner("dp", r), piece), ffncame_s.at[r]) for r in behind
    ]
    ffn_all = [copy("dp", r, ffnown_s, ffnsum_ref.at[deep]) for r in behind]

    halves = mfar_s.shape[0]
    half_rows = merged_s.shape[0] // halves
    share = half_rows // near_size
    small = share // far_size
    main_piece = parts_s.shape[1] // far_size

    def share_at(h, index):
        return h * half_rows + index * share

    def share_of(h, index):
        return merged_s.at[pl.ds(pl.multiple_of(share_at(h, index), TILE), share)]

    mnear, mfar, across, back, spread, onward = [], [], [], [], [], []
    for h in range(halves):
        mnear.append([])
        for p in range(pairs):
            src = share_of(h, partner("mp", 2 * p + 1))
            mnear[h].append(copy("mp", 1, src, mnear_s.at[h, p]))
        mfar.append({})
        for p in range(1, pairs):
            src = share_of(h, partner("mp", 2 * p))
            mfar[h][p] = copy("mp", 2 * p, src, mfar_s.at[h, p])
        across.append([])
        for r in behind:
            src = rows_at(mfar_s.at[h, 0], partner("dp", r), small)
            across[h].append(copy("dp", r, src, mpiece_s.at[h, r]))
        mine = full_ref.at[h, me]
        back.append([copy("dp", r, mpiece_s.at[h, 0], mine.at[deep]) for r in behind])
        spread.append([copy("mp", r, mine, mine) for r in evens + [1]])
        onward.append([])
        for r in evens:
            came = full_ref.at[h, partner("mp", r)]
            onward[h].append(copy("mp", 1, came, came))
    lines_in = [copy("mp", r, linein_s.at[0], linein_s.at[r]) for r in beside]
    lines_out = [copy("dp", r, lineout_s.at[0], lineout_s.at[r]) for r in behind]
    pnear = [copy("mp", 1, parts_s.at[2 * p + 1], pnear_s.at[p]) for p in range(pairs)]
    pfar = {p: copy("mp", 2 * p, parts_s.at[2 * p], pfar_s.at[p]) for p in range(1, pairs)}
    main_out = [
        copy("dp", r, rows_at(parts_s.at[0], partner("dp", r), main_piece), main_s.at[r])
        for r in behind
    ]
    main_all = [copy("dp", r, mainsum_s, main_ref.at[deep]) for r in behind]
    tnear = [copy("mp", 1, tparts_s.at[2 * p + 1], tnear_s.at[p]) for p in range(pairs)]
    tfar = {p: copy("mp", 2 * p, tparts_s.at[2 * p], tfar_s.at[p]) for p in range(1, pairs)}
    tails = [copy("dp", r, tparts_s.at[0], tails_s.at[r]) for r in behind]

    @pl.when(step == 0)
    def _():
        for level in range(LEVELS):
            for c in bring(level):
                c.start()
        for c in bring_more():
            c.start()
        greet([("mp", r) for r in beside] + [("dp", r) for r in behind])
        for c in ffn_out:
            c.start()
        mask_s[...] = head_mask(head_dim)
        gq_s[...] = jnp.zeros_like(gq_s)
        gk_s[...] = jnp.zeros_like(gk_s)
        gv_s[...] = jnp.zeros_like(gv_s)

    @pl.when(step == TILE // 2)
    def _():
        total = ffn_ref[pl.ds(pl.multiple_of(deep * piece, TILE), piece), :].astype(F32)
        for c, r in zip(ffn_out, behind):
            c.wait_recv()
            total = total + ffncame_s[r].astype(F32)
        ffnown_s[...] = total.astype(BF16)
        keep_ffn().start()
        for c in ffn_all:
            c.start()

    for level in range(LEVELS):

        @pl.when(step == level * (TILE // LEVELS))
        def _():
            for c in bring(level):
                c.wait()

    @pl.when(step < TILE)
    def _():
        mask = mask_s[...]
        minus = -mask
        starts = [pl.multiple_of(step * jump + u * block, TILE) for u in range(sets)]
        lane_head = lax.broadcasted_iota(jnp.int32, (COVER, 2 * lanes), 1) % lanes // head_dim
        zeros = jnp.zeros((COVER, lanes), BF16)
        units = [(u, g) for g in range(groups) for u in range(sets)]

        def at(ref, u, g):
            return ref[pl.ds(starts[u], COVER), pl.ds(g * lanes, lanes)]

        scaled = [at(ga_s, u, g) * at(rinv_s, u, g) for u, g in units]
        grads = []
        for (u, g), ga in zip(units, scaled):
            left = jnp.concatenate([ga, ga * at(att_s, u, g)], axis=1)
            right = jnp.concatenate([tiled(at(v_s, u, g), mask), minus], axis=1)
            grads.append(dot_rt(left, right))
        score_grads = []
        totals = {}
        for (u, g), grad in zip(units, grads):
            ds = p_ref[g, 0, u].astype(F32) * grad
            totals[g] = ds if g not in totals else totals[g] + ds
            score_grads.append(ds.astype(BF16))
        for g in range(groups):
            ds_s[step, g] = totals[g]
        query_grads = []
        for (u, g), ds in zip(units, score_grads):
            query_grads.append(dot(ds, tiled(at(k_s, u, g), mask)))
        pair_grads = []
        for (u, g), ds, ga in zip(units, score_grads, scaled):
            left = jnp.concatenate([ds, p_ref[g, 0, u]], axis=0)
            right = jnp.concatenate(
                [
                    jnp.concatenate([at(q_s, u, g), zeros], axis=1),
                    jnp.concatenate([zeros, ga], axis=1),
                ],
                axis=0,
            )
            pair_grads.append(dot_lt(left, right))
        for (u, g), grad_q, grad_kv in zip(units, query_grads, pair_grads):
            here, cols = pl.ds(starts[u], COVER), pl.ds(g * lanes, lanes)
            gq_s[here, cols] += (grad_q * scale).astype(BF16)
            both = jnp.where(lane_head == 0, grad_kv[:COVER], 0.0)
            for h in range(1, GROUP):
                both = jnp.where(lane_head == h, grad_kv[h * COVER : (h + 1) * COVER], both)
            both = both.astype(BF16)
            gk_s[here, cols] += both[:, :lanes]
            gv_s[here, cols] += both[:, lanes:]

    def table_grads():
        def unshift(g, _):
            full = ds_s[0, g]
            for o in range(1, TILE):
                turned = pltpu.roll(ds_s[o, g], COVER - o, 0)
                full = full + pltpu.roll(turned, GROUP * COVER - o, 1)
            for h in range(GROUP):
                base_s[g * GROUP + h] = full[:, h * COVER : (h + 1) * COVER]
            return 0

        lax.fori_loop(0, groups, unshift, 0)
        sums = []
        for pair in range((idx_ref.shape[0] + 1) // 2):
            onehot = index_onehot(pair_row(idx_ref, pair), gtab_s.shape[1])
            vals = jnp.concatenate([base_s[:, 2 * pair, :], base_s[:, 2 * pair + 1, :]], axis=1)
            high = vals.astype(BF16)
            both = jnp.concatenate([high, (vals - high.astype(F32)).astype(BF16)], axis=0)
            sums.append(dot_rt(both, onehot))
        count = base_s.shape[0]
        grad = sums[0]
        for x in sums[1:]:
            grad = grad + x
        gtab_s[...] = grad[:count] + grad[count:]

    @pl.when(step == TILE)
    def _():
        for c in bring_late():
            c.start()
        merge_s[...] = jnp.zeros_like(merge_s)
        lines_s[...] = jnp.zeros_like(lines_s)
        for c in bring_more():
            c.wait()
        normed_t = n1_s[...].T
        for t, ref in enumerate((gq_s, gk_s, gv_s)):
            grad = dot(normed_t, ref[...]).T
            sums = jnp.sum(ref[...].astype(F32), axis=0, keepdims=True)
            lines_s[4 + t : 5 + t, :] = sums
            sums = jnp.broadcast_to(sums, (8, width)).T[:, :1]
            grad = (grad * g1_ref[...] + sums * b1_ref[...]).astype(BF16)
            for r in range(near_size):
                parts_s[r, t * span : (t + 1) * span, :] = grad[r * span : (r + 1) * span]
        for r in range(near_size):
            parts_s[r, 3 * span :, :] = gproj_ref[r * span : (r + 1) * span, :]
        for c in pnear:
            c.start()

    @pl.when(step == TILE + 2)
    def _():
        for p in reversed(range(pairs)):
            pnear[p].wait_recv()
            joined = parts_s[2 * p].astype(F32) + pnear_s[p].astype(F32)
            parts_s[2 * p] = joined.astype(BF16)
            if p:
                pfar[p].start()

    @pl.when(step >= TILE)
    def _():
        count = gmid_ref.shape[0]
        here = pl.ds(pl.multiple_of((step - TILE) * count, TILE), count)
        grad_mid = None
        for t, ref in enumerate((gq_s, gk_s, gv_s)):
            part = dot(ref[here, :], wt_s[t * width : (t + 1) * width, :])
            grad_mid = part if grad_mid is None else grad_mid + part
        stats = stats_ref[...]
        normed1 = n1_s[here, :].astype(F32)
        lines_s[0:1, :] += jnp.sum(grad_mid * normed1, axis=0, keepdims=True)
        lines_s[1:2, :] += jnp.sum(grad_mid, axis=0, keepdims=True)
        grad_merged = gmid_ref[...].astype(F32) + norm_back(
            grad_mid * g1_ref[...], normed1, stats[:, 3:4]
        )
        lines_s[2:3, :] += jnp.sum(grad_merged, axis=0, keepdims=True)
        grad_merged = grad_merged.astype(BF16)
        q_s[here, :] = grad_merged
        normed0 = ((x_ref[...].astype(F32) - stats[:, 0:1]) * stats[:, 1:2]).astype(BF16)
        n0_s[here, :] = normed0
        inv0_s[here, :] = jnp.broadcast_to(stats[:, 1:2], (count, inv0_s.shape[1]))
        merge_s[...] += dot_lt(grad_merged, normed0)

    @pl.when(step == TILE + dense_steps - 1)
    def _():
        narrow = merged_s.shape[1]
        per_half = merge_s.shape[1] // narrow // halves
        for h in range(halves):
            for j in range(h * per_half, (h + 1) * per_half):
                part = merge_s[:, j * narrow : (j + 1) * narrow]
                merged_s[j * width : (j + 1) * width, :] = part.astype(BF16)
            for c in mnear[h]:
                c.start()
        linein_s[0] = jnp.concatenate([sums2_ref[0:4, :], lines_s[0:4, :]], axis=0)
        for c in lines_in:
            c.start()
        for c in bring_late():
            c.wait()
        table_grads()
        for r in range(near_size):
            bias_sums = lines_s[4:7, r * span : (r + 1) * span]
            hidden = gub_ref.shape[2] // 2
            half = (r % 2) * hidden
            lines = [
                fill(bias_sums, width),
                fill(gtab_s[r * local : (r + 1) * local, :], width),
                fill(gub_ref[r // 2][:, half : half + hidden], width),
                jnp.zeros((TILE - 4 - local, width), F32),
            ]
            tparts_s[r] = jnp.concatenate(lines, axis=0).astype(BF16)
        for h in range(halves):
            for p in reversed(range(pairs)):
                mnear[h][p].wait_recv()
                spot = pl.ds(pl.multiple_of(share_at(h, partner("mp", 2 * p)), TILE), share)
                joined = merged_s[spot, :].astype(F32) + mnear_s[h, p].astype(F32)
                merged_s[spot, :] = joined.astype(BF16)
                if p:
                    mfar[h][p].start()
        for c in tnear:
            c.start()
        total = linein_s[0]
        for c, r in zip(lines_in, beside):
            c.wait_recv()
            total = total + linein_s[r]
        lineout_s[0] = total
        for c in lines_out:
            c.start()
        input_part(0)

        total = parts_s[0].astype(F32)
        for p in reversed(range(1, pairs)):
            pfar[p].wait_recv()
            total = total + pfar_s[p].astype(F32)
        parts_s[0] = total.astype(BF16)
        for c in main_out:
            c.start()
        for h in range(halves):
            mine = pl.ds(pl.multiple_of(share_at(h, me), TILE), share)
            total = merged_s[mine, :].astype(F32)
            for p in reversed(range(1, pairs)):
                mfar[h][p].wait_recv()
                total = total + mfar_s[h, p].astype(F32)
            mfar_s[h, 0] = total.astype(BF16)
            for c in across[h]:
                c.start()
        for p in reversed(range(pairs)):
            tnear[p].wait_recv()
            tparts_s[2 * p] = (tparts_s[2 * p].astype(F32) + tnear_s[p].astype(F32)).astype(BF16)
            if p:
                tfar[p].start()
        input_part(1)

        for h in range(halves):
            spot = pl.ds(pl.multiple_of(deep * small, TILE), small)
            total = mfar_s[h, 0, spot, :].astype(F32)
            for c, r in zip(across[h], behind):
                c.wait_recv()
                total = total + mpiece_s[h, r].astype(F32)
            mpiece_s[h, 0] = total.astype(BF16)
            keep_merge(h).start()
            for c in back[h]:
                c.start()
        spot = pl.ds(pl.multiple_of(deep * main_piece, TILE), main_piece)
        total = parts_s[0, spot, :].astype(F32)
        for c, r in zip(main_out, behind):
            c.wait_recv()
            total = total + main_s[r].astype(F32)
        mainsum_s[...] = total.astype(BF16)
        keep_main().start()
        for c in main_all:
            c.start()
        input_part(2)

        for h in range(halves):
            keep_merge(h).wait()
            for c in back[h]:
                c.wait_recv()
            for c in spread[h]:
                c.start()
        total = tparts_s[0].astype(F32)
        for p in reversed(range(1, pairs)):
            tfar[p].wait_recv()
            total = total + tfar_s[p].astype(F32)
        tparts_s[0] = total.astype(BF16)
        for c in tails:
            c.start()
        output_part(0)
        output_part(1)
        for h in range(halves):
            for c, after in zip(spread[h], onward[h]):
                c.wait_recv()
                after.start()
            if h == 0:
                output_part(2)

        total = lineout_s[0]
        for c, r in zip(lines_out, behind):
            c.wait_recv()
            total = total + lineout_s[r]
        sums_ref[...] = total
        total = tparts_s[0].astype(F32)
        for c, r in zip(tails, behind):
            c.wait_recv()
            total = total + tails_s[r].astype(F32)
        tail_ref[...] = total
        for h in range(halves):
            spread[h][-1].wait_recv()
            for c in onward[h]:
                c.wait_recv()
        for c in main_all + ffn_all:
            c.wait_recv()
        keep_ffn().wait()
        keep_main().wait()
        for h in range(halves):
            for c in mnear[h] + list(mfar[h].values()) + across[h] + back[h] + spread[h]:
                c.wait_send()
            for c in onward[h]:
                c.wait_send()
        for c in ffn_out + ffn_all + lines_in + lines_out + tnear + list(tfar.values()):
            c.wait_send()
        for c in pnear + list(pfar.values()) + main_out + tails + main_all:
            c.wait_send()
        for j in range(PARTS):
            take_gin(j).wait()
            take_raw(j).wait()


def back_rows(
    q,
    k,
    v,
    ga,
    rinv,
    att,
    n1,
    wt,
    p,
    idx,
    ffn,
    gmid,
    stats,
    x,
    g1,
    b1,
    gproj,
    gub,
    sums2,
    act,
    base,
    second,
    wm,
    g0,
    table_width,
    head_dim,
    local,
    near_size,
    far_size,
):
    rows, width = q.shape
    wide = x.shape[1]
    heads = width // head_dim
    groups, steps, sets, _, cover = p.shape
    dense_steps = 7
    count = rows // dense_steps
    narrow = 256
    pairs = near_size // 2
    piece = (ffn.shape[0] // far_size, ffn.shape[1])
    part = (4 * local * head_dim, width)
    main_piece = (4 * local * head_dim // far_size, width)
    total_rows = wide // narrow * width
    halves = 2 if total_rows // (2 * near_size * far_size) % TILE == 0 else 1
    share = total_rows // halves // near_size
    small = share // far_size
    near, far = near_size - 1, far_size - 1
    copies = 2 * far + halves * (4 * pairs - 2 + 2 * far) + near + far
    copies += (2 * pairs - 1) + 2 * far + (2 * pairs - 1) + far

    def place(i):
        return (jnp.maximum(i - steps, 0), 0)

    def p_place(i):
        return (0, jnp.minimum(i, steps - 1), 0, 0, 0)

    return call(
        functools.partial(back_kernel, head_dim, local, near_size, far_size, dense_steps),
        steps + dense_steps,
        (q, k, v, ga, rinv, att, n1, wt, p, idx, ffn, gmid, stats, x, g1, b1, gproj, gub, sums2)
        + (act, base, second, wm, g0),
        [anywhere()] * 8
        + [
            pl.BlockSpec((groups, 1, sets, COVER, cover), p_place),
            whole(idx.shape),
            whole(ffn.shape),
            pl.BlockSpec((count, width), place),
            pl.BlockSpec((count, 8), place),
            pl.BlockSpec((count, wide), place),
            whole(g1.shape),
            whole(b1.shape),
            whole(gproj.shape),
            whole(gub.shape),
            whole(sums2.shape),
        ]
        + [anywhere()] * 4
        + [whole(g0.shape)],
        [
            jax.ShapeDtypeStruct((rows, width), BF16),
            jax.ShapeDtypeStruct((rows, wide), BF16),
            jax.ShapeDtypeStruct((far_size,) + piece, BF16),
            jax.ShapeDtypeStruct((far_size,) + main_piece, BF16),
            jax.ShapeDtypeStruct((TILE, width), F32),
            jax.ShapeDtypeStruct((halves, near_size, far_size, small, narrow), BF16),
            jax.ShapeDtypeStruct((8, width), F32),
        ],
        [
            anywhere(),
            anywhere(),
            anywhere(),
            anywhere(),
            whole((TILE, width)),
            anywhere(),
            whole((8, width)),
        ],
        [pltpu.VMEM((rows, width), BF16)] * 7
        + [pltpu.VMEM((3 * width, width), BF16)]
        + [pltpu.VMEM((rows, width), BF16)] * 3
        + [
            pltpu.VMEM((TILE, groups, COVER, cover), F32),
            pltpu.VMEM((heads, COVER, COVER), F32),
            pltpu.VMEM((cover, GROUP * head_dim), BF16),
            pltpu.VMEM((heads, table_width), F32),
            pltpu.VMEM((far_size,) + piece, BF16),
            pltpu.VMEM(piece, BF16),
            pltpu.VMEM((width, wide), F32),
            pltpu.VMEM((total_rows, narrow), BF16),
            pltpu.VMEM((halves, pairs, share, narrow), BF16),
            pltpu.VMEM((halves, pairs, share, narrow), BF16),
            pltpu.VMEM((halves, far_size, small, narrow), BF16),
            pltpu.VMEM((near_size, TILE, width), BF16),
            pltpu.VMEM((pairs, TILE, width), BF16),
            pltpu.VMEM((pairs, TILE, width), BF16),
            pltpu.VMEM((near_size,) + part, BF16),
            pltpu.VMEM((pairs,) + part, BF16),
            pltpu.VMEM((pairs,) + part, BF16),
            pltpu.VMEM((far_size,) + main_piece, BF16),
            pltpu.VMEM(main_piece, BF16),
            pltpu.VMEM((far_size, TILE, width), BF16),
            pltpu.VMEM((near_size, 8, width), F32),
            pltpu.VMEM((far_size, 8, width), F32),
            pltpu.VMEM((8, width), F32),
            pltpu.VMEM((rows, wide), BF16),
            pltpu.VMEM((rows, 128), F32),
            pltpu.VMEM(wm.shape, BF16),
            pltpu.VMEM((act.shape[0] * act.shape[2], width), BF16),
            pltpu.SemaphoreType.DMA((6, LEVELS, sets)),
            pltpu.SemaphoreType.DMA((4 + halves,)),
            pltpu.SemaphoreType.DMA((2 + act.shape[0] + near_size,)),
            pltpu.SemaphoreType.DMA((2, PARTS)),
            pltpu.SemaphoreType.DMA((2 * copies,)),
        ],
        2 * rows * width * (24 * width + wide),
        rows * width * 20,
        group=2,
    )


def last_kernel(
    head_dim,
    local,
    window,
    live_ref,
    raw_ref,
    gin16_ref,
    g0_ref,
    b0_ref,
    sums_ref,
    tail_ref,
    wm_hbm,
    main_hbm,
    ffn_hbm,
    full_hbm,
    out_ref,
    gin_ref,
    gain0_ref,
    bias0_ref,
    gqkv_ref,
    gproj_ref,
    gqb_ref,
    gtab_ref,
    gub_ref,
    *rest,
):
    line_refs, rest = rest[:6], rest[6:]
    gmerge_hbm, gup_hbm, gdown_hbm, wm_ref, main_ref, ffn_ref, full_ref = rest[:7]
    gmerge_ref, gup_ref, gdown_ref, in_sems, out_sems = rest[7:]
    step = pl.program_id(0)
    count, width = raw_ref.shape
    rows = count * pl.num_programs(0)
    halves = full_ref.shape[0]
    narrow = full_ref.shape[2]

    def bring(i):
        pair = (
            (main_hbm, main_ref),
            (ffn_hbm, ffn_ref),
            (wm_hbm, wm_ref),
            (full_hbm, full_ref),
        )[i]
        return pltpu.make_async_copy(*pair, in_sems.at[i])

    def take(i):
        if i < 2:
            pair = ((gup_ref, gup_hbm), (gdown_ref, gdown_hbm))[i]
        else:
            here = pl.ds((i - 2) * narrow, narrow)
            pair = (gmerge_ref.at[here], gmerge_hbm.at[here])
        return pltpu.make_async_copy(*pair, out_sems.at[i])

    @pl.when(step == 0)
    def _():
        for i in range(4):
            bring(i).start()

    live = live_rows(live_ref, step * count, count, rows, width, window)
    out_ref[...] = jnp.where(live, raw_ref[...].astype(F32), 0.0)
    gin_ref[...] = gin16_ref[...].astype(F32)

    @pl.when(step == 0)
    def _():
        span = local * head_dim
        bring(0).wait()
        main = main_ref[...].astype(F32)
        for l in range(local):
            for t in range(3):
                at = t * span + l * head_dim
                gqkv_ref[l, t * head_dim : (t + 1) * head_dim, :] = main[at : at + head_dim]
        gproj_ref[...] = main[3 * span :]
        rows_of = []
        for l in range(local):
            here = slice(l * head_dim, (l + 1) * head_dim)
            rows_of.append(
                jnp.concatenate([tail_ref[t : t + 1, here] for t in range(3)], axis=1)
            )
        gqb_ref[...] = jnp.concatenate(rows_of, axis=0)
        gtab_ref[...] = tail_ref[3 : 3 + local, : gtab_ref.shape[1]]
        gub_ref[...] = tail_ref[3 + local : 4 + local, : gub_ref.shape[1]]
        for i, ref in enumerate(line_refs):
            ref[...] = sums_ref[i : i + 1, :]

    @pl.when(step == 1)
    def _():
        hidden = gup_ref.shape[1]
        bring(1).wait()
        gup_ref[...] = ffn_ref[:, :hidden].astype(F32)
        take(0).start()
        gdown_ref[...] = ffn_ref[:, hidden:].astype(F32).T
        take(1).start()
        bring(2).wait()
        bring(3).wait()

    low_sum = sums_ref[6:7, :]
    for j in range(halves):

        @pl.when(step == 2 + j)
        def _():
            cols = pl.ds(j * narrow, narrow)
            grad = full_ref[j].astype(F32).T
            weight = wm_ref[cols, :].astype(F32)
            gain = jnp.sum(weight * grad, axis=1, keepdims=True)
            shift = jnp.sum(weight * low_sum, axis=1, keepdims=True)
            gain0_ref[:, cols] = jnp.broadcast_to(gain, (narrow, 128)).T[:1, :]
            bias0_ref[:, cols] = jnp.broadcast_to(shift, (narrow, 128)).T[:1, :]
            scale = jnp.broadcast_to(g0_ref[:, cols], (8, narrow)).T[:, :1]
            offset = jnp.broadcast_to(b0_ref[:, cols], (8, narrow)).T[:, :1]
            gmerge_ref[cols, :] = grad * scale + offset * low_sum
            take(2 + j).start()

    @pl.when(step == pl.num_programs(0) - 1)
    def _():
        for i in range(2 + halves):
            take(i).wait()


def last_rows(
    live, raw, gin16, wm, g0, b0, main, ffn, full, sums, tail, local, head_dim, rel, window
):
    rows, width = raw.shape
    wide = gin16.shape[1]
    step = rows // 7
    hidden = ffn.shape[1] // 2
    span = local * head_dim
    narrow_block = pl.BlockSpec((step, width), lambda i: (i, 0))
    wide_block = pl.BlockSpec((step, wide), lambda i: (i, 0))
    rest = [g0, b0, sums, tail]
    later = [wm, main, ffn, full]
    shapes = [
        (1, wide),
        (1, wide),
        (local, 3 * head_dim, width),
        (span, width),
        (local, 3 * head_dim),
        (local, rel),
        (1, hidden),
    ] + [(1, width)] * 6
    large = [(wide, width), (width, hidden), (hidden, width)]
    return call(
        functools.partial(last_kernel, head_dim, local, window),
        7,
        [live, raw, gin16] + rest + later,
        [pl.BlockSpec(memory_space=pltpu.SMEM), narrow_block, wide_block]
        + [whole(a.shape) for a in rest]
        + [anywhere()] * len(later),
        [
            jax.ShapeDtypeStruct((rows, width), F32),
            jax.ShapeDtypeStruct((rows, wide), F32),
        ]
        + [jax.ShapeDtypeStruct(shape, F32) for shape in shapes + large],
        [narrow_block, wide_block]
        + [whole(shape) for shape in shapes]
        + [anywhere()] * len(large),
        [pltpu.VMEM(a.shape, BF16) for a in later]
        + [pltpu.VMEM(shape, F32) for shape in large]
        + [
            pltpu.SemaphoreType.DMA((len(later),)),
            pltpu.SemaphoreType.DMA((2 + full.shape[0],)),
        ],
        2 * rows * width,
        rows * wide * 9,
    )


def shards(
    inputs,
    norm0_gain,
    norm0_bias,
    merge_weight,
    norm1_gain,
    norm1_bias,
    qkv_weight,
    qkv_bias,
    rel_table,
    rel_index,
    regions,
    live_windows,
    proj_weight,
    proj_bias,
    norm2_gain,
    norm2_bias,
    up_weight,
    up_bias,
    down_weight,
    down_bias,
    cotangent,
    n_dp,
    n_mp,
):
    micro, strip_rows, wide = inputs.shape
    width = merge_weight.shape[1]
    win = rel_index.shape[0]
    local, packed = qkv_bias.shape
    head_dim = packed // 3
    heads = local * n_mp
    hidden = up_bias.shape[0]
    rel = rel_table.shape[1]
    rows = micro * strip_rows
    windows = rows // win
    sets = windows // TILE
    strip = lax.axis_index("mp")

    region = lax.dynamic_slice_in_dim(regions, strip * strip_rows, strip_rows, axis=1)
    region = region.reshape(sets, rows // sets)
    jump = rows // sets // TILE - 1
    region = jnp.stack([region[:, o * jump : o * jump + COVER] for o in range(TILE)])
    region = jnp.tile(region[:, :, None, :], (1, 1, 1, GROUP))
    table_width = -(-rel // 128) * 128
    live = live_windows.T
    vecs = (proj_bias[None], norm2_gain[None], norm2_bias[None], down_bias[None])
    gain0, bias0 = norm0_gain[None], norm0_bias[None]
    gain1, bias1 = norm1_gain[None], norm1_bias[None]

    x = inputs.reshape(rows, wide)
    stats, n1, q, k, v, att, rinv, p, tiles, wt, second = front_rows(
        x,
        gain0,
        bias0,
        merge_weight,
        gain1,
        bias1,
        jnp.transpose(qkv_weight, (1, 2, 0)).reshape(local * packed, width),
        qkv_bias,
        rel_table,
        up_bias[None],
        up_weight,
        down_weight,
        proj_weight.reshape(local * head_dim, width),
        rel_index,
        region,
        n_mp,
        head_dim,
    )
    base, act, gmid, gatt, ffn_part, gub, gproj, sums2 = ffn_rows(
        live,
        n1,
        att,
        cotangent.reshape(rows, width),
        stats,
        tiles,
        second,
        vecs,
        local,
        hidden,
        win,
    )
    raw, gin16, ffn_sum, main, tail, gmerge, sums = back_rows(
        q,
        k,
        v,
        gatt,
        rinv,
        att,
        n1,
        wt,
        p,
        rel_index,
        ffn_part,
        gmid,
        stats,
        x,
        gain1,
        bias1,
        gproj,
        gub,
        sums2,
        act,
        base,
        second,
        merge_weight,
        gain0,
        table_width,
        head_dim,
        local,
        n_mp,
        n_dp,
    )
    span = local * head_dim
    out, grad_input, ggain0, gbias0, gqkv, gproj, gqb, gtab, gub, *lines, gmerge, gup, gdown = (
        last_rows(
            live,
            raw,
            gin16,
            merge_weight,
            gain0,
            bias0,
            main.reshape(4 * span, width),
            ffn_sum.reshape(width, 2 * hidden),
            gmerge.reshape(-1, width, gmerge.shape[4]),
            sums,
            tail,
            local,
            head_dim,
            rel,
            win,
        )
    )
    gpb, gain2, bias2, gdb, gain1, bias1 = (x.reshape(width) for x in lines)
    return (
        out.reshape(micro, strip_rows, width),
        grad_input.reshape(micro, strip_rows, wide),
        ggain0.reshape(wide),
        gbias0.reshape(wide),
        gmerge,
        gain1,
        bias1,
        jnp.transpose(gqkv, (2, 0, 1)),
        gqb,
        gtab,
        gproj.reshape(local, head_dim, width),
        gpb,
        gain2,
        bias2,
        gup,
        gub.reshape(hidden),
        gdown,
        gdb,
    )


def solution(mesh):
    placed = (
        P(None, ("dp", "mp"), None),
        P(),
        P(),
        P(),
        P(),
        P(),
        P(None, "mp", None),
        P("mp", None),
        P("mp", None),
        P(),
        P(None, "dp"),
        P(None, "dp"),
        P("mp", None, None),
        P(),
        P(),
        P(),
        P(None, "mp"),
        P("mp"),
        P("mp", None),
        P(),
        P(None, ("dp", "mp"), None),
    )
    return jax.shard_map(
        functools.partial(shards, n_dp=mesh.shape["dp"], n_mp=mesh.shape["mp"]),
        mesh=mesh,
        in_specs=placed,
        out_specs=(
            P(None, ("dp", "mp"), None),
            P(None, ("dp", "mp"), None),
            P(),
            P(),
            P(),
            P(),
            P(),
            P(None, "mp", None),
            P("mp", None),
            P("mp", None),
            P("mp", None, None),
            P(),
            P(),
            P(),
            P(None, "mp"),
            P("mp"),
            P("mp", None),
            P(),
        ),
        check_vma=False,
    )
```

```python
import functools
import math

import jax
import jax.numpy as jnp
from jax import lax
from jax.experimental import pallas as pl
from jax.experimental.pallas import tpu as pltpu
from jax.sharding import PartitionSpec as P

F32 = jnp.float32
BF16 = jnp.bfloat16
EPSILON = 1e-05
MASKED = -1e30
COVER = 64
TILE = 16
GROUP = 4
VMEM_LIMIT = 60 << 20


def dot(left, right):
    return jnp.dot(left, right, preferred_element_type=F32)


def dot_rt(left, right):
    return lax.dot_general(left, right, (((1,), (1,)), ((), ())), preferred_element_type=F32)


def dot_lt(left, right):
    return lax.dot_general(left, right, (((0,), (0,)), ((), ())), preferred_element_type=F32)


def whole(shape):
    return pl.BlockSpec(shape, lambda i: (0,) * len(shape), pipeline_mode=pl.Buffered(1))


def anywhere():
    return pl.BlockSpec(memory_space=pl.ANY)


def call(kernel, grid, ins, in_specs, outs, out_specs, scratch, flops, nbytes, group=None):
    extra = {} if group is None else {"collective_id": group, "has_side_effects": True}
    return pl.pallas_call(
        kernel,
        grid=(grid,),
        in_specs=in_specs,
        out_specs=out_specs,
        out_shape=outs,
        scratch_shapes=scratch,
        compiler_params=pltpu.CompilerParams(
            dimension_semantics=("arbitrary",), vmem_limit_bytes=VMEM_LIMIT, **extra
        ),
        cost_estimate=pl.CostEstimate(flops=flops, bytes_accessed=nbytes, transcendentals=0),
    )(*ins)


def partner(axis, flips):
    at = lax.axis_index(axis)
    bit = 1
    while bit <= flips:
        if flips & bit:
            at = at + bit * (1 - 2 * lax.rem(lax.div(at, jnp.int32(bit)), jnp.int32(2)))
        bit *= 2
    return at


def send(axis, flips, src, dst, send_sem, recv_sem):
    return pltpu.make_async_remote_copy(
        src_ref=src,
        dst_ref=dst,
        send_sem=send_sem,
        recv_sem=recv_sem,
        device_id={axis: partner(axis, flips)},
        device_id_type=pl.DeviceIdType.MESH,
    )


def greet(peers):
    barrier = pltpu.get_barrier_semaphore()
    for axis, flips in peers:
        pl.semaphore_signal(
            barrier,
            inc=1,
            device_id={axis: partner(axis, flips)},
            device_id_type=pl.DeviceIdType.MESH,
        )
    pl.semaphore_wait(barrier, len(peers))


class Gather:
    def __init__(self, axis, size, own, held, send_sems, recv_sems, own_sem):
        self.axis, self.size, self.own, self.held = axis, size, own, held
        self.send_sems, self.recv_sems, self.own_sem = send_sems, recv_sems, own_sem

    def straight(self, r):
        return send(
            self.axis, r, self.own, self.held.at[r], self.send_sems.at[r], self.recv_sems.at[r]
        )

    def onward(self, r):
        return send(
            self.axis,
            1,
            self.held.at[r],
            self.held.at[r + 1],
            self.send_sems.at[r + 1],
            self.recv_sems.at[r + 1],
        )

    def keep(self):
        return pltpu.make_async_copy(self.own, self.held.at[0], self.own_sem)

    def start(self, flips=None):
        evens = list(range(2, self.size, 2))
        for r in evens + [1] if flips is None else flips:
            self.straight(r).start()
        if flips is None or 1 in flips:
            self.keep().start()

    def forward(self, r):
        self.straight(r).wait_recv()
        self.onward(r).start()

    def finish(self):
        self.keep().wait()
        self.straight(1).wait()
        for r in range(2, self.size, 2):
            self.straight(r).wait_send()
            self.onward(r).wait()


def spans(total, step):
    return [(start, min(step, total - start)) for start in range(0, total, step)]


def norm_parts(values):
    mean = jnp.mean(values, axis=-1, keepdims=True)
    center = values - mean
    spread = jnp.mean(center * center, axis=-1, keepdims=True) + EPSILON
    inverse = lax.rsqrt(spread)
    return center * inverse, mean, inverse, spread


def norm_back(grad, normed, inverse):
    mean_grad = jnp.mean(grad, axis=-1, keepdims=True)
    mean_cross = jnp.mean(grad * normed, axis=-1, keepdims=True)
    return inverse * (grad - mean_grad - normed * mean_cross)


def head_mask(head_dim):
    rows = lax.broadcasted_iota(jnp.int32, (GROUP * COVER, GROUP * head_dim), 0) // COVER
    cols = lax.broadcasted_iota(jnp.int32, (GROUP * COVER, GROUP * head_dim), 1) // head_dim
    return (rows == cols).astype(F32).astype(BF16)


def tiled(block, mask):
    return jnp.concatenate([block] * GROUP, axis=0) * mask


def pair_row(idx_ref, pair):
    win = idx_ref.shape[0]
    gap = jnp.full((1, COVER - win), -1, jnp.int32)
    parts = []
    for i in (2 * pair, 2 * pair + 1):
        parts.append(idx_ref[i : i + 1, :] if i < win else jnp.full((1, win), -1, jnp.int32))
        parts.append(gap)
    return jnp.concatenate(parts, axis=1)


def index_onehot(row, table_width):
    entry = lax.broadcasted_iota(jnp.int32, (table_width, row.shape[1]), 0)
    return (entry == row).astype(F32).astype(BF16)


def fill(x, width):
    return jnp.concatenate([x, jnp.zeros((x.shape[0], width - x.shape[1]), x.dtype)], axis=1)


def front_kernel(
    head_dim,
    local,
    size,
    merge_steps,
    x_ref,
    g0_ref,
    b0_ref,
    wm_ref,
    g1_ref,
    b1_ref,
    qkvw_ref,
    qkvb_ref,
    tab_ref,
    ub_ref,
    up_ref,
    down_ref,
    proj_ref,
    idx_ref,
    rid_ref,
    stats_ref,
    n1_ref,
    q_ref,
    k_ref,
    v_ref,
    att_ref,
    rinv_ref,
    p_ref,
    tiles_ref,
    wt_ref,
    second_ref,
    first_s,
    tiles_s,
    own_s,
    tile_s,
    second_s,
    mid_s,
    q_s,
    k_s,
    v_s,
    att_s,
    rinv_s,
    base_s,
    bias_s,
    mask_s,
    tile_send,
    tile_recv,
    first_send,
    first_recv,
    second_send,
    second_recv,
    own_sems,
    out_sems,
):
    step = pl.program_id(0)
    rows, width = mid_s.shape
    heads = width // head_dim
    lanes = GROUP * head_dim
    groups = heads // GROUP
    per_group = size // groups
    scale = 1.0 / math.sqrt(head_dim)
    span = local * head_dim
    evens = list(range(2, size, 2))
    main = Gather("mp", size, own_s, first_s, first_send, first_recv, own_sems.at[0])
    rest = Gather("mp", size, second_s, second_ref, second_send, second_recv, own_sems.at[1])

    def tile_copy(r):
        return send("mp", r, tile_s, tiles_s.at[r], tile_send.at[r], tile_recv.at[r])

    @pl.when(step == 0)
    def _():
        own_s[...] = qkvw_ref[...]
        bias = qkvb_ref[...].astype(F32)
        lines = []
        for t in range(3):
            parts = [
                bias[l : l + 1, t * head_dim : (t + 1) * head_dim] for l in range(local)
            ]
            lines.append(fill(jnp.concatenate(parts, axis=1), width))
        lines.append(fill(tab_ref[...].astype(F32), width))
        up_bias = ub_ref[...].astype(F32)
        parts = [up_bias[i : i + 1, :] for i in range(up_bias.shape[0])]
        lines.append(fill(jnp.concatenate(parts, axis=1), width))
        lines.append(jnp.zeros((TILE - 4 - local, width), F32))
        tile_s[...] = jnp.concatenate(lines, axis=0).astype(BF16)
        greet([("mp", r) for r in range(1, size)])
        for r in range(1, size):
            tile_copy(r).start()
        tiles_s[0] = tile_s[...]
        main.start([r for r in evens if r < 2 * per_group] + [1])
        hidden = up_ref.shape[1]
        second_s[:hidden, :] = up_ref[...].T
        second_s[hidden : 2 * hidden, :] = down_ref[...]
        second_s[2 * hidden :, :] = proj_ref[...]

    @pl.when(step == 2)
    def _():
        main.start([r for r in evens if r >= 2 * per_group])

    @pl.when(step == merge_steps - 3)
    def _():
        rest.start()

    @pl.when(step < merge_steps)
    def _():
        count = x_ref.shape[0]
        here = pl.ds(pl.multiple_of(step * count, TILE), count)
        normed, mean, inverse, _ = norm_parts(x_ref[...].astype(F32))
        normed_in = (normed * g0_ref[...] + b0_ref[...]).astype(BF16)
        normed1, mean1, inverse1, spread1 = norm_parts(dot(normed_in, wm_ref[...]))
        n1_ref[...] = normed1.astype(BF16)
        stats = [mean, inverse, mean1, inverse1, spread1 * inverse1]
        stats_ref[...] = jnp.concatenate(stats + [mean] * (8 - len(stats)), axis=1)
        mid_s[here, :] = (normed1 * g1_ref[...] + b1_ref[...]).astype(BF16)

    table_step = merge_steps - 3

    @pl.when(step == merge_steps - 1)
    def _():
        for r in evens:
            if r < 2 * per_group:
                main.forward(r)

    @pl.when(step == table_step)
    def _():
        mask_s[...] = head_mask(head_dim)
        att_s[...] = jnp.zeros_like(att_s)
        rinv_s[...] = jnp.zeros_like(rinv_s)
        base_s[...] = jnp.full(base_s.shape, MASKED, F32)
        for r in range(1, size):
            tile_copy(r).wait_recv()

    all_pairs = list(range((idx_ref.shape[0] + 1) // 2))
    for i in range(2):

        @pl.when(step == table_step + i)
        def _():
            table = jnp.concatenate(
                [tiles_s[r].astype(F32)[3 : 3 + local, : 2 * 128] for r in range(size)], axis=0
            ).astype(BF16)
            here = all_pairs[i::2]
            rows_of = [pair_row(idx_ref, pair) for pair in here]
            found = [dot(table, index_onehot(row, table.shape[1])) for row in rows_of]
            found = [jnp.where(row < 0, MASKED, x) for row, x in zip(rows_of, found)]
            for pair, vals in zip(here, found):
                base_s[:, 2 * pair, :] = vals[:, :COVER]
                base_s[:, 2 * pair + 1, :] = vals[:, COVER:]

    @pl.when(step == table_step + 2)
    def _():
        tiles_ref[...] = tiles_s[...]

        def shift(g, _):
            full = jnp.concatenate([base_s[g * GROUP + h] for h in range(GROUP)], axis=1)
            for o in range(TILE):
                bias_s[g, o] = pltpu.roll(pltpu.roll(full, o, 0), o, 1) if o else full
            return 0

        lax.fori_loop(0, groups, shift, 0)
        for r in range(1, size):
            tile_copy(r).wait_send()

    def outward(ref, out, which, g):
        cols = pl.ds(pl.multiple_of(g * lanes, lanes), lanes)
        return pltpu.make_async_copy(ref.at[:, cols], out.at[:, cols], out_sems.at[which, g])

    def early_out(g):
        return [
            outward(ref, out, i, g)
            for i, (ref, out) in enumerate(((q_s, q_ref), (k_s, k_ref), (v_s, v_ref)))
        ]

    def late_out(g):
        return [outward(att_s, att_ref, 3, g), outward(rinv_s, rinv_ref, 4, g)]

    low_half = lax.broadcasted_iota(jnp.int32, (COVER, 2 * COVER), 1) < COVER
    region_of = lax.broadcasted_iota(jnp.int32, (8, GROUP * COVER), 0)
    sets = rid_ref.shape[1]
    block = rows // sets

    def attend(it, g):
        mask = mask_s[...]
        cols = pl.ds(pl.multiple_of(g * lanes, lanes), lanes)
        units = [(2 * it + i, u) for i in range(2) for u in range(sets)]
        starts = [pl.multiple_of(o * (block // TILE - 1) + u * block, TILE) for o, u in units]
        scores = []
        for start in starts:
            here = pl.ds(start, COVER)
            scores.append(dot_rt(q_s[here, cols], tiled(k_s[here, cols], mask)))
        weights = []
        for (o, u), s in zip(units, scores):
            member = (region_of == rid_ref[o, u]).astype(F32).astype(BF16)
            same = dot_lt(member[:, :COVER], member)
            s = s + bias_s[g, o] + jnp.where(same > 0.5, 0.0, MASKED)
            parts = []
            for c in range(GROUP // 2):
                x = s[:, c * 2 * COVER : (c + 1) * 2 * COVER]
                top0 = jnp.max(jnp.where(low_half, x, MASKED), axis=1, keepdims=True)
                top1 = jnp.max(jnp.where(low_half, MASKED, x), axis=1, keepdims=True)
                top = jnp.maximum(jnp.where(low_half, top0, top1), MASKED * 0.1)
                parts.append(jnp.exp(x - top).astype(BF16))
            w = jnp.concatenate(parts, axis=1)
            p_ref[0, o, u] = w
            weights.append(w)
        mixed = []
        for start, w in zip(starts, weights):
            vals = tiled(v_s[pl.ds(start, COVER), cols], mask)
            mixed.append(dot(w, jnp.concatenate([vals, mask], axis=1)))
        for start, a in zip(starts, mixed):
            here = pl.ds(start, COVER)
            total = a[:, lanes:]
            inv = jnp.where(total > 0.0, 1.0 / jnp.maximum(total, 0.5), 0.0)
            att_s[here, cols] += (a[:, :lanes] * inv).astype(BF16)
            rinv_s[here, cols] += inv.astype(BF16)

    @pl.when(step >= merge_steps)
    def _():
        g = step - merge_steps
        twice = 2 * per_group

        @pl.when(g == 0)
        def _():
            main.keep().wait()
            main.straight(1).wait_recv()
            for r in evens:
                if r < twice:
                    main.onward(r).wait_recv()

        for known in range(2, groups, 2):

            @pl.when(g == known)
            def _():
                for r in evens:
                    if known * per_group <= r < known * per_group + twice:
                        main.onward(r).wait_recv()

        @pl.when(g % 2 == 0)
        def _():
            shards = [g * per_group + j for j in range(twice)]
            cols = pl.ds(pl.multiple_of(g * lanes, 2 * lanes), 2 * lanes)
            outs = (q_s, k_s, v_s)
            part = rows // 3
            weights, biases = [], []
            for t in range(3):
                weight = []
                for s in shards:
                    for l in range(local):
                        at = (3 * l + t) * head_dim
                        weight.append(first_s[s, at : at + head_dim, :])
                    biases.append(tiles_s[s].astype(F32)[t : t + 1, :span])
                weight = jnp.concatenate(weight, axis=0)
                spot = pl.ds(pl.multiple_of(t * width + g * lanes, 2 * lanes), 2 * lanes)
                wt_ref[spot, :] = weight
                weights.append(weight.T)
            weight = jnp.concatenate(weights, axis=1)
            bias = jnp.concatenate(biases, axis=1)

            def project(i, _):
                here = pl.ds(pl.multiple_of(i * part, TILE), part)
                y = dot(mid_s[here, :], weight) + bias
                for t in range(3):
                    z = y[:, 2 * t * lanes : 2 * (t + 1) * lanes]
                    outs[t][here, cols] = (z * scale if t == 0 else z).astype(BF16)
                return 0

            lax.fori_loop(0, 3, project, 0)

        for c in early_out(g):
            c.start()

        def run(it, _):
            attend(it, g)
            return 0

        lax.fori_loop(0, TILE // 4, run, 0)

        @pl.when(g == 0)
        def _():
            for r in evens:
                if r >= twice:
                    main.forward(r)

        @pl.when(g == groups - 1)
        def _():
            for r in evens:
                rest.forward(r)

        lax.fori_loop(TILE // 4, TILE // 2, run, 0)
        for c in late_out(g):
            c.start()

        @pl.when(g == groups - 1)
        def _():
            main.straight(1).wait_send()
            for r in evens:
                main.straight(r).wait_send()
                main.onward(r).wait_send()
            rest.finish()
            for known in range(groups):
                for c in early_out(known) + late_out(known):
                    c.wait()


def front_rows(
    x, g0, b0, wm, g1, b1, qkvw, qkvb, tab, ub, up, down, proj, idx, rid, size, head_dim
):
    rows, wide = x.shape
    width = wm.shape[1]
    local = qkvb.shape[0]
    hidden = up.shape[1]
    heads = width // head_dim
    groups = heads // GROUP
    offsets, sets = rid.shape[0], rid.shape[1]
    cover = GROUP * COVER
    merge_steps = 7
    step = rows // merge_steps
    first = (3 * local * head_dim, width)
    second = (2 * hidden + local * head_dim, width)

    def place(i):
        return (jnp.minimum(i, merge_steps - 1), 0)

    def group_place(i):
        return (jnp.maximum(i - merge_steps, 0), 0, 0, 0, 0)

    small = [g0, b0, wm, g1, b1, qkvw, qkvb, tab, ub, up, down, proj, idx, rid]
    row_out = jax.ShapeDtypeStruct((rows, width), BF16)
    sems = [pltpu.SemaphoreType.DMA((size,))] * 6
    return call(
        functools.partial(front_kernel, head_dim, local, size, merge_steps),
        merge_steps + groups,
        [x] + small,
        [pl.BlockSpec((step, wide), place)] + [whole(a.shape) for a in small],
        [jax.ShapeDtypeStruct((rows, 8), F32), row_out]
        + [row_out] * 5
        + [
            jax.ShapeDtypeStruct((groups, offsets, sets, COVER, cover), BF16),
            jax.ShapeDtypeStruct((size, TILE, width), BF16),
            jax.ShapeDtypeStruct((3 * width, width), BF16),
            jax.ShapeDtypeStruct((size,) + second, BF16),
        ],
        [pl.BlockSpec((step, 8), place), pl.BlockSpec((step, width), place)]
        + [anywhere()] * 5
        + [
            pl.BlockSpec((1, offsets, sets, COVER, cover), group_place),
            whole((size, TILE, width)),
            whole((3 * width, width)),
            anywhere(),
        ],
        [
            pltpu.VMEM((size,) + first, BF16),
            pltpu.VMEM((size, TILE, width), BF16),
            pltpu.VMEM(first, BF16),
            pltpu.VMEM((TILE, width), BF16),
            pltpu.VMEM(second, BF16),
        ]
        + [pltpu.VMEM((rows, width), BF16)] * 6
        + [
            pltpu.VMEM((heads, COVER, COVER), F32),
            pltpu.VMEM((groups, TILE, COVER, cover), F32),
            pltpu.VMEM((cover, GROUP * head_dim), BF16),
        ]
        + sems
        + [pltpu.SemaphoreType.DMA((2,)), pltpu.SemaphoreType.DMA((5, groups))],
        2 * rows * width * (wide + 18 * width),
        rows * width * 40,
        group=0,
    )


REACH = math.sqrt(2.0) / 0.3275911
CENTRE = 0.125


def centred():
    rational = (0.254829592, -0.284496736, 1.421413741, -1.453152027, 1.061405429)
    plain = [0.5 * a * REACH ** (k + 1) for k, a in enumerate(rational)]
    out = [0.0] * len(plain)
    for k, a in enumerate(plain):
        for j in range(k + 1):
            out[j] += a * math.comb(k, j) * CENTRE ** (k - j)
    return out


def gelu_and_slope(pre):
    x = pre.astype(BF16)
    t = pl.reciprocal(jnp.abs(pre) + REACH, approx=True)
    s = (t - CENTRE).astype(BF16)
    terms = [BF16(a) for a in centred()]
    poly = terms[4]
    for a in reversed(terms[:4]):
        poly = poly * s + a
    part = poly * t.astype(BF16)
    bell = jnp.exp2((x * x) * BF16(-0.5 * math.log2(math.e)))
    size = jnp.abs(x)
    act = jnp.maximum(x, BF16(0.0)) - size * (part * bell)
    under = (part - size * BF16(1.0 / math.sqrt(2.0 * math.pi))) * bell
    return act, jnp.where(x > BF16(0.0), BF16(1.0) - under, under)


def live_rows(live_ref, start, count, rows, width, window):
    micro = live_ref.shape[1]
    micro_rows = rows // micro
    before = lax.axis_index("mp") * micro_rows
    row = lax.broadcasted_iota(jnp.int32, (count, width), 0) + start
    live = None
    for m in range(micro):
        last = m * micro_rows + jnp.minimum(live_ref[0, m] * window - before, micro_rows)
        inside = (row >= m * micro_rows) & (row < last)
        live = inside if live is None else live | inside
    return live


def ffn_kernel(
    local,
    window,
    live_ref,
    n1_ref,
    att_ref,
    cot_ref,
    stats_ref,
    wp_ref,
    pb_ref,
    g2_ref,
    b2_ref,
    db_ref,
    tail_ref,
    up_ref,
    down_ref,
    base_ref,
    act_ref,
    gmid_ref,
    gatt_ref,
    part_ref,
    gub_ref,
    gproj_ref,
    sums_ref,
    base_s,
    gffn_s,
    att_s,
    n2_s,
    inv_s,
    n_s,
    go_s,
    nt_s,
    gt_s,
    act_s,
    gp_s,
    odd_s,
    even_s,
    near_s,
    far_s,
    near_send,
    near_recv,
    far_send,
    far_recv,
    in_sems,
    out_sems,
    act_sem,
):
    step = pl.program_id(0)
    pairs = even_s.shape[0]
    pair = pairs - 1 - step
    rows, width = gffn_s.shape
    blocks = spans(rows, 512)
    hidden = up_ref.shape[1]
    wp = wp_ref[...].reshape(width, width)

    def near(p):
        return send("mp", 1, odd_s.at[p % 2], near_s.at[p], near_send.at[p], near_recv.at[p])

    def far(p):
        slot = far_s.at[p - 1]
        return send("mp", 2 * p, even_s.at[p], slot, far_send.at[p], far_recv.at[p])

    def bring(b):
        here = pl.ds(*blocks[b])
        whence = ((n1_ref, n_s), (att_ref, att_s), (cot_ref, go_s))
        return [
            pltpu.make_async_copy(src.at[here], dst.at[here], in_sems.at[i, b])
            for i, (src, dst) in enumerate(whence)
        ]

    def take(which, b):
        here = pl.ds(*blocks[b])
        src, dst = ((base_s, base_ref), (go_s, gmid_ref), (n2_s, gatt_ref))[which]
        return pltpu.make_async_copy(src.at[here], dst.at[here], out_sems.at[which, b])

    def take_act():
        return pltpu.make_async_copy(act_s.at[pl.ds(0, rows)], act_ref.at[pair], act_sem)

    @pl.when(step == 0)
    def _():
        for b in range(len(blocks)):
            for c in bring(b):
                c.start()
        greet([("mp", r) for r in [1] + [2 * p for p in range(1, pairs)]])
        bias_proj, gain2, bias2, bias_down = (x[...] for x in (pb_ref, g2_ref, b2_ref, db_ref))
        act_s[rows:, :] = jnp.zeros_like(act_s[rows:, :])
        gp_s[rows:, :] = jnp.zeros_like(gp_s[rows:, :])
        nt_s[width:, :] = jnp.ones_like(nt_s[width:, :])
        down_sum = jnp.zeros((1, width), F32)
        for b, (start, count) in enumerate(blocks):
            here = pl.ds(start, count)
            for c in bring(b):
                c.wait()
            stats = stats_ref[here, :]
            merged = n_s[here, :].astype(F32) * stats[:, 4:5] + stats[:, 2:3]
            middle = merged + dot(att_s[here, :], wp) + bias_proj
            base_s[here, :] = (middle + bias_down).astype(BF16)
            take(0, b).start()
            normed, _, inverse, _ = norm_parts(middle)
            n2_s[here, :] = normed.astype(BF16)
            inv_s[here, :] = jnp.broadcast_to(inverse, (count, inv_s.shape[1]))
            normed_ffn = (normed * gain2 + bias2).astype(BF16)
            n_s[here, :] = normed_ffn
            live = live_rows(live_ref, start, count, rows, width, window)
            grad_out = jnp.where(live, go_s[here, :].astype(F32), 0.0)
            down_sum = down_sum + jnp.sum(grad_out, axis=0, keepdims=True)
            grad_low = grad_out.astype(BF16)
            go_s[here, :] = grad_low
            whole_count = -(-count // 128) * 128
            if whole_count != count:
                filler = jnp.zeros((whole_count - count, width), BF16)
                normed_ffn = jnp.concatenate([normed_ffn, filler], axis=0)
                grad_low = jnp.concatenate([grad_low, filler], axis=0)
            nt_s[:width, start : start + whole_count] = normed_ffn.T
            gt_s[:, start : start + whole_count] = grad_low.T
        sums_ref[...] = jnp.zeros_like(sums_ref)
        sums_ref[3:4, :] = down_sum
        gffn_s[...] = jnp.zeros_like(gffn_s)

    def pass_on():
        @pl.when(step > 0)
        def _():
            near(pair + 1).wait_recv()
            joined = even_s[pair + 1].astype(F32) + near_s[pair + 1].astype(F32)
            even_s[pair + 1] = joined.astype(BF16)

        for p in range(1, pairs):

            @pl.when(pair + 1 == p)
            def _():
                far(p).start()

    up_t = up_ref[...].reshape(2 * hidden, width)
    down = down_ref[...].reshape(2 * hidden, width)
    up_bias = jnp.concatenate(
        [tail_ref[i].astype(F32)[3 + local : 4 + local, :hidden] for i in range(2)], axis=1
    )
    for b, (start, count) in enumerate(blocks):
        if b == 1:
            pass_on()
        here = pl.ds(start, count)
        act, slope = gelu_and_slope(dot_rt(n_s[here, :], up_t) + up_bias)
        grad_pre = dot_rt(go_s[here, :], down).astype(BF16) * slope
        act_s[here, :] = act
        gp_s[here, :] = grad_pre
        gffn_s[here, :] += dot(grad_pre, up_t)
    take_act().start()

    @pl.when(step > 1)
    def _():
        near(pair + 2).wait_send()

    grad_up = dot(nt_s[...], gp_s[...])
    gub_ref[0] = grad_up[width : width + 1, :]
    grad_up = grad_up[:width].astype(BF16)
    even_s[pair, :, :hidden] = grad_up[:, :hidden]
    odd_s[pair % 2, :, :hidden] = grad_up[:, hidden:]
    grad_down = dot(gt_s[...], act_s[...]).astype(BF16)
    even_s[pair, :, hidden:] = grad_down[:, :hidden]
    odd_s[pair % 2, :, hidden:] = grad_down[:, hidden:]
    near(pair).start()
    take_act().wait()

    @pl.when(step == pairs - 1)
    def _():
        gain2 = g2_ref[...]
        gain_sum = jnp.zeros((1, width), F32)
        bias_sum = jnp.zeros((1, width), F32)
        proj_sum = jnp.zeros((1, width), F32)
        grad_proj = jnp.zeros((width, width), F32)
        for b, (start, count) in enumerate(blocks):
            here = pl.ds(start, count)
            grad_ffn = gffn_s[here, :]
            normed = n2_s[here, :].astype(F32)
            gain_sum = gain_sum + jnp.sum(grad_ffn * normed, axis=0, keepdims=True)
            bias_sum = bias_sum + jnp.sum(grad_ffn, axis=0, keepdims=True)
            grad_middle = go_s[here, :].astype(F32) + norm_back(
                grad_ffn * gain2, normed, inv_s[here, :1]
            )
            proj_sum = proj_sum + jnp.sum(grad_middle, axis=0, keepdims=True)
            grad_attn = grad_middle.astype(BF16)
            go_s[here, :] = grad_attn
            take(1, b).start()
            grad_proj = grad_proj + dot_lt(att_s[here, :], grad_attn)
            n2_s[here, :] = dot_rt(grad_attn, wp).astype(BF16)
            take(2, b).start()
        gproj_ref[...] = grad_proj.astype(BF16)
        sums_ref[0:1, :] = proj_sum
        sums_ref[1:2, :] = gain_sum
        sums_ref[2:3, :] = bias_sum
        near(0).wait_recv()
        total = even_s[0].astype(F32) + near_s[0].astype(F32)
        for p in range(1, pairs):
            far(p).wait_recv()
            total = total + far_s[p - 1].astype(F32)
        part_ref[...] = total.astype(BF16)
        for p in range(pairs):
            if p < 2:
                near(p).wait_send()
            if p:
                far(p).wait_send()
        for b in range(len(blocks)):
            for which in range(3):
                take(which, b).wait()


def ffn_rows(live, n1, att, cot, stats, tiles, second, vecs, local, hidden, window):
    rows, width = n1.shape
    size = tiles.shape[0]
    pairs = size // 2
    padded = -(-rows // 128) * 128
    proj_rows = width // size
    proj_at = 2 * hidden // proj_rows
    blocks = len(spans(rows, 512))
    row_out = jax.ShapeDtypeStruct((rows, width), BF16)
    return call(
        functools.partial(ffn_kernel, local, window),
        pairs,
        (live, n1, att, cot, stats, second) + vecs + (tiles, second, second),
        [
            pl.BlockSpec(memory_space=pltpu.SMEM),
            anywhere(),
            anywhere(),
            anywhere(),
            whole(stats.shape),
            pl.BlockSpec(
                (size, proj_rows, width),
                lambda i: (0, proj_at, 0),
                pipeline_mode=pl.Buffered(1),
            ),
        ]
        + [whole((1, width))] * 4
        + [
            pl.BlockSpec((2, TILE, width), lambda i: (pairs - 1 - i, 0, 0)),
            pl.BlockSpec((2, hidden, width), lambda i: (pairs - 1 - i, 0, 0)),
            pl.BlockSpec((2, hidden, width), lambda i: (pairs - 1 - i, 1, 0)),
        ],
        [
            row_out,
            jax.ShapeDtypeStruct((pairs, rows, 2 * hidden), BF16),
            row_out,
            row_out,
            jax.ShapeDtypeStruct((width, 2 * hidden), BF16),
            jax.ShapeDtypeStruct((pairs, 1, 2 * hidden), F32),
            jax.ShapeDtypeStruct((width, width), BF16),
            jax.ShapeDtypeStruct((8, width), F32),
        ],
        [
            anywhere(),
            anywhere(),
            anywhere(),
            anywhere(),
            whole((width, 2 * hidden)),
            pl.BlockSpec((1, 1, 2 * hidden), lambda i: (pairs - 1 - i, 0, 0)),
            whole((width, width)),
            whole((8, width)),
        ],
        [
            pltpu.VMEM((rows, width), BF16),
            pltpu.VMEM((rows, width), F32),
            pltpu.VMEM((rows, width), BF16),
            pltpu.VMEM((rows, width), BF16),
            pltpu.VMEM((rows, 128), F32),
            pltpu.VMEM((rows, width), BF16),
            pltpu.VMEM((rows, width), BF16),
            pltpu.VMEM((width + TILE, padded), BF16),
            pltpu.VMEM((width, padded), BF16),
            pltpu.VMEM((padded, 2 * hidden), BF16),
            pltpu.VMEM((padded, 2 * hidden), BF16),
        ]
        + [pltpu.VMEM((min(pairs, 2), width, 2 * hidden), BF16)]
        + [pltpu.VMEM((pairs, width, 2 * hidden), BF16)] * 2
        + [pltpu.VMEM((max(pairs - 1, 1), width, 2 * hidden), BF16)]
        + [pltpu.SemaphoreType.DMA((pairs,))] * 4
        + [pltpu.SemaphoreType.DMA((3, blocks))] * 2
        + [pltpu.SemaphoreType.DMA(())],
        2 * rows * width * hidden * size * 6,
        rows * width * 20,
        group=1,
    )


LEVELS = 4
PARTS = 3


def back_kernel(
    head_dim,
    local,
    near_size,
    far_size,
    dense_steps,
    q_ref,
    k_ref,
    v_ref,
    ga_ref,
    rinv_ref,
    att_ref,
    n1_ref,
    wt_ref,
    p_ref,
    idx_ref,
    ffn_ref,
    gmid_ref,
    stats_ref,
    x_ref,
    g1_ref,
    b1_ref,
    gproj_ref,
    gub_ref,
    sums2_ref,
    act_ref,
    base_ref,
    second_ref,
    wm_ref,
    g0_ref,
    raw_ref,
    gin_ref,
    ffnsum_ref,
    main_ref,
    tail_ref,
    full_ref,
    sums_ref,
    q_s,
    k_s,
    v_s,
    ga_s,
    rinv_s,
    att_s,
    n1_s,
    wt_s,
    gq_s,
    gk_s,
    gv_s,
    ds_s,
    base_s,
    mask_s,
    gtab_s,
    ffncame_s,
    ffnown_s,
    merged_s,
    mnear_s,
    mfar_s,
    mpiece_s,
    tparts_s,
    tnear_s,
    tfar_s,
    parts_s,
    pnear_s,
    pfar_s,
    main_s,
    mainsum_s,
    tails_s,
    linein_s,
    lineout_s,
    lines_s,
    n0_s,
    inv0_s,
    wm_s,
    down_s,
    in_sems,
    more_sems,
    late_sems,
    out_sems,
    sems,
):
    step = pl.program_id(0)
    rows, width = gq_s.shape
    lanes = GROUP * head_dim
    groups = width // lanes
    scale = 1.0 / math.sqrt(head_dim)
    sets = p_ref.shape[2]
    block = rows // sets
    jump = block // TILE - 1
    pairs = near_size // 2
    span = local * head_dim
    me, deep = lax.axis_index("mp"), lax.axis_index("dp")
    beside = list(range(1, near_size))
    behind = list(range(1, far_size))
    evens = list(range(2, near_size, 2))
    piece = ffnsum_ref.shape[1]
    at_sem = [0]

    def copy(axis, r, src, dst):
        at_sem[0] += 2
        return send(axis, r, src, dst, sems.at[at_sem[0] - 2], sems.at[at_sem[0] - 1])

    def rows_at(ref, index, count):
        return ref.at[pl.ds(pl.multiple_of(index * count, TILE), count)]

    def bring(level):
        copies = []
        whence = (
            (q_ref, q_s),
            (k_ref, k_s),
            (v_ref, v_s),
            (ga_ref, ga_s),
            (rinv_ref, rinv_s),
            (att_ref, att_s),
        )
        part = TILE // LEVELS * jump
        first = COVER - jump
        for i, (src, dst) in enumerate(whence):
            for u in range(sets):
                if level == 0:
                    here = pl.ds(u * block, part + first)
                else:
                    here = pl.ds(u * block + first + level * part, part)
                copies.append(
                    pltpu.make_async_copy(src.at[here], dst.at[here], in_sems.at[i, level, u])
                )
        return copies

    def bring_more():
        return [
            pltpu.make_async_copy(n1_ref, n1_s, more_sems.at[0]),
            pltpu.make_async_copy(wt_ref, wt_s, more_sems.at[1]),
        ]

    act_bufs = (k_s, v_s, ga_s, rinv_s)
    chunks = act_ref.shape[0] * act_ref.shape[2] // width

    def bring_late():
        copies = [(base_ref, att_s), (wm_ref, wm_s)]
        per = act_ref.shape[2]
        each = width // per
        for p in range(act_ref.shape[0]):
            dst = act_bufs[p // each].at[:, pl.ds(p % each * per, per)]
            copies.append((act_ref.at[p], dst))
        hidden = per // 2
        for r in range(near_size):
            src = second_ref.at[r, pl.ds(hidden, hidden)]
            copies.append((src, down_s.at[pl.ds(r * hidden, hidden)]))
        return [
            pltpu.make_async_copy(src, dst, late_sems.at[i]) for i, (src, dst) in enumerate(copies)
        ]

    def dense_span(j):
        return pl.ds(j * (rows // PARTS), rows // PARTS)

    def take_gin(j):
        here = dense_span(j)
        return pltpu.make_async_copy(n0_s.at[here], gin_ref.at[here], out_sems.at[0, j])

    def take_raw(j):
        here = dense_span(j)
        return pltpu.make_async_copy(att_s.at[here], raw_ref.at[here], out_sems.at[1, j])

    def input_part(j):
        here = dense_span(j)
        grad_low = dot_rt(q_s[here, :], wm_s[...])
        normed = n0_s[here, :].astype(F32)
        grad = norm_back(grad_low * g0_ref[...], normed, inv0_s[here, :1])
        n0_s[here, :] = grad.astype(BF16)
        take_gin(j).start()

    def output_part(j):
        here = dense_span(j)
        total = att_s[here, :].astype(F32)
        for i in range(chunks):
            total = total + dot(act_bufs[i][here, :], down_s[i * width : (i + 1) * width, :])
        att_s[here, :] = total.astype(BF16)
        take_raw(j).start()

    def keep_main():
        return pltpu.make_async_copy(mainsum_s, main_ref.at[deep], more_sems.at[3])

    def keep_merge(h):
        src = mpiece_s.at[h, 0]
        return pltpu.make_async_copy(src, full_ref.at[h, me, deep], more_sems.at[4 + h])

    def keep_ffn():
        return pltpu.make_async_copy(ffnown_s, ffnsum_ref.at[deep], more_sems.at[2])

    ffn_out = [
        copy("dp", r, rows_at(ffn_ref, partner("dp", r), piece), ffncame_s.at[r]) for r in behind
    ]
    ffn_all = [copy("dp", r, ffnown_s, ffnsum_ref.at[deep]) for r in behind]

    halves = mfar_s.shape[0]
    half_rows = merged_s.shape[0] // halves
    share = half_rows // near_size
    small = share // far_size
    main_piece = parts_s.shape[1] // far_size

    def share_at(h, index):
        return h * half_rows + index * share

    def share_of(h, index):
        return merged_s.at[pl.ds(pl.multiple_of(share_at(h, index), TILE), share)]

    mnear, mfar, across, back, spread, onward = [], [], [], [], [], []
    for h in range(halves):
        mnear.append([])
        for p in range(pairs):
            src = share_of(h, partner("mp", 2 * p + 1))
            mnear[h].append(copy("mp", 1, src, mnear_s.at[h, p]))
        mfar.append({})
        for p in range(1, pairs):
            src = share_of(h, partner("mp", 2 * p))
            mfar[h][p] = copy("mp", 2 * p, src, mfar_s.at[h, p])
        across.append([])
        for r in behind:
            src = rows_at(mfar_s.at[h, 0], partner("dp", r), small)
            across[h].append(copy("dp", r, src, mpiece_s.at[h, r]))
        mine = full_ref.at[h, me]
        back.append([copy("dp", r, mpiece_s.at[h, 0], mine.at[deep]) for r in behind])
        spread.append([copy("mp", r, mine, mine) for r in evens + [1]])
        onward.append([])
        for r in evens:
            came = full_ref.at[h, partner("mp", r)]
            onward[h].append(copy("mp", 1, came, came))
    lines_in = [copy("mp", r, linein_s.at[0], linein_s.at[r]) for r in beside]
    lines_out = [copy("dp", r, lineout_s.at[0], lineout_s.at[r]) for r in behind]
    pnear = [copy("mp", 1, parts_s.at[2 * p + 1], pnear_s.at[p]) for p in range(pairs)]
    pfar = {p: copy("mp", 2 * p, parts_s.at[2 * p], pfar_s.at[p]) for p in range(1, pairs)}
    main_out = [
        copy("dp", r, rows_at(parts_s.at[0], partner("dp", r), main_piece), main_s.at[r])
        for r in behind
    ]
    main_all = [copy("dp", r, mainsum_s, main_ref.at[deep]) for r in behind]
    tnear = [copy("mp", 1, tparts_s.at[2 * p + 1], tnear_s.at[p]) for p in range(pairs)]
    tfar = {p: copy("mp", 2 * p, tparts_s.at[2 * p], tfar_s.at[p]) for p in range(1, pairs)}
    tails = [copy("dp", r, tparts_s.at[0], tails_s.at[r]) for r in behind]

    @pl.when(step == 0)
    def _():
        for level in range(LEVELS):
            for c in bring(level):
                c.start()
        for c in bring_more():
            c.start()
        greet([("mp", r) for r in beside] + [("dp", r) for r in behind])
        for c in ffn_out:
            c.start()
        mask_s[...] = head_mask(head_dim)
        gq_s[...] = jnp.zeros_like(gq_s)
        gk_s[...] = jnp.zeros_like(gk_s)
        gv_s[...] = jnp.zeros_like(gv_s)

    @pl.when(step == TILE // 2)
    def _():
        total = ffn_ref[pl.ds(pl.multiple_of(deep * piece, TILE), piece), :].astype(F32)
        for c, r in zip(ffn_out, behind):
            c.wait_recv()
            total = total + ffncame_s[r].astype(F32)
        ffnown_s[...] = total.astype(BF16)
        keep_ffn().start()
        for c in ffn_all:
            c.start()

    for level in range(LEVELS):

        @pl.when(step == level * (TILE // LEVELS))
        def _():
            for c in bring(level):
                c.wait()

    @pl.when(step < TILE)
    def _():
        mask = mask_s[...]
        minus = -mask
        starts = [pl.multiple_of(step * jump + u * block, TILE) for u in range(sets)]
        lane_head = lax.broadcasted_iota(jnp.int32, (COVER, 2 * lanes), 1) % lanes // head_dim
        zeros = jnp.zeros((COVER, lanes), BF16)
        units = [(u, g) for g in range(groups) for u in range(sets)]

        def at(ref, u, g):
            return ref[pl.ds(starts[u], COVER), pl.ds(g * lanes, lanes)]

        scaled = [at(ga_s, u, g) * at(rinv_s, u, g) for u, g in units]
        grads = []
        for (u, g), ga in zip(units, scaled):
            left = jnp.concatenate([ga, ga * at(att_s, u, g)], axis=1)
            right = jnp.concatenate([tiled(at(v_s, u, g), mask), minus], axis=1)
            grads.append(dot_rt(left, right))
        score_grads = []
        totals = {}
        for (u, g), grad in zip(units, grads):
            ds = p_ref[g, 0, u].astype(F32) * grad
            totals[g] = ds if g not in totals else totals[g] + ds
            score_grads.append(ds.astype(BF16))
        for g in range(groups):
            ds_s[step, g] = totals[g]
        query_grads = []
        for (u, g), ds in zip(units, score_grads):
            query_grads.append(dot(ds, tiled(at(k_s, u, g), mask)))
        pair_grads = []
        for (u, g), ds, ga in zip(units, score_grads, scaled):
            left = jnp.concatenate([ds, p_ref[g, 0, u]], axis=0)
            right = jnp.concatenate(
                [
                    jnp.concatenate([at(q_s, u, g), zeros], axis=1),
                    jnp.concatenate([zeros, ga], axis=1),
                ],
                axis=0,
            )
            pair_grads.append(dot_lt(left, right))
        for (u, g), grad_q, grad_kv in zip(units, query_grads, pair_grads):
            here, cols = pl.ds(starts[u], COVER), pl.ds(g * lanes, lanes)
            gq_s[here, cols] += (grad_q * scale).astype(BF16)
            both = jnp.where(lane_head == 0, grad_kv[:COVER], 0.0)
            for h in range(1, GROUP):
                both = jnp.where(lane_head == h, grad_kv[h * COVER : (h + 1) * COVER], both)
            both = both.astype(BF16)
            gk_s[here, cols] += both[:, :lanes]
            gv_s[here, cols] += both[:, lanes:]

    def table_grads():
        def unshift(g, _):
            full = ds_s[0, g]
            for o in range(1, TILE):
                turned = pltpu.roll(ds_s[o, g], COVER - o, 0)
                full = full + pltpu.roll(turned, GROUP * COVER - o, 1)
            for h in range(GROUP):
                base_s[g * GROUP + h] = full[:, h * COVER : (h + 1) * COVER]
            return 0

        lax.fori_loop(0, groups, unshift, 0)
        sums = []
        for pair in range((idx_ref.shape[0] + 1) // 2):
            onehot = index_onehot(pair_row(idx_ref, pair), gtab_s.shape[1])
            vals = jnp.concatenate([base_s[:, 2 * pair, :], base_s[:, 2 * pair + 1, :]], axis=1)
            high = vals.astype(BF16)
            both = jnp.concatenate([high, (vals - high.astype(F32)).astype(BF16)], axis=0)
            sums.append(dot_rt(both, onehot))
        count = base_s.shape[0]
        grad = sums[0]
        for x in sums[1:]:
            grad = grad + x
        gtab_s[...] = grad[:count] + grad[count:]

    @pl.when(step == TILE)
    def _():
        for c in bring_late():
            c.start()
        lines_s[...] = jnp.zeros_like(lines_s)
        for c in bring_more():
            c.wait()
        normed_t = n1_s[...].T
        for t, ref in enumerate((gq_s, gk_s, gv_s)):
            grad = dot(normed_t, ref[...]).T
            sums = jnp.sum(ref[...].astype(F32), axis=0, keepdims=True)
            lines_s[4 + t : 5 + t, :] = sums
            sums = jnp.broadcast_to(sums, (8, width)).T[:, :1]
            grad = (grad * g1_ref[...] + sums * b1_ref[...]).astype(BF16)
            for r in range(near_size):
                parts_s[r, t * span : (t + 1) * span, :] = grad[r * span : (r + 1) * span]
        for r in range(near_size):
            parts_s[r, 3 * span :, :] = gproj_ref[r * span : (r + 1) * span, :]
        for c in pnear:
            c.start()

    @pl.when(step == TILE + 1)
    def _():
        for p in reversed(range(pairs)):
            pnear[p].wait_recv()
            joined = parts_s[2 * p].astype(F32) + pnear_s[p].astype(F32)
            parts_s[2 * p] = joined.astype(BF16)
            if p:
                pfar[p].start()

    @pl.when(step >= TILE)
    def _():
        count = gmid_ref.shape[0]
        here = pl.ds(pl.multiple_of((step - TILE) * count, TILE), count)
        grad_mid = None
        for t, ref in enumerate((gq_s, gk_s, gv_s)):
            part = dot(ref[here, :], wt_s[t * width : (t + 1) * width, :])
            grad_mid = part if grad_mid is None else grad_mid + part
        stats = stats_ref[...]
        normed1 = n1_s[here, :].astype(F32)
        lines_s[0:1, :] += jnp.sum(grad_mid * normed1, axis=0, keepdims=True)
        lines_s[1:2, :] += jnp.sum(grad_mid, axis=0, keepdims=True)
        grad_merged = gmid_ref[...].astype(F32) + norm_back(
            grad_mid * g1_ref[...], normed1, stats[:, 3:4]
        )
        lines_s[2:3, :] += jnp.sum(grad_merged, axis=0, keepdims=True)
        grad_merged = grad_merged.astype(BF16)
        q_s[here, :] = grad_merged
        normed0 = ((x_ref[...].astype(F32) - stats[:, 0:1]) * stats[:, 1:2]).astype(BF16)
        n0_s[here, :] = normed0
        inv0_s[here, :] = jnp.broadcast_to(stats[:, 1:2], (count, inv0_s.shape[1]))

    @pl.when(step == TILE + dense_steps - 1)
    def _():
        narrow = merged_s.shape[1]
        per_half = n0_s.shape[1] // narrow // halves
        merged_t = q_s[...].T
        for h in range(halves):
            for j in range(h * per_half, (h + 1) * per_half):
                part = dot(merged_t, n0_s[:, j * narrow : (j + 1) * narrow])
                merged_s[j * width : (j + 1) * width, :] = part.astype(BF16)
            for c in mnear[h]:
                c.start()
        linein_s[0] = jnp.concatenate([sums2_ref[0:4, :], lines_s[0:4, :]], axis=0)
        for c in lines_in:
            c.start()
        for c in bring_late():
            c.wait()
        table_grads()
        for r in range(near_size):
            bias_sums = lines_s[4:7, r * span : (r + 1) * span]
            hidden = gub_ref.shape[2] // 2
            half = (r % 2) * hidden
            lines = [
                fill(bias_sums, width),
                fill(gtab_s[r * local : (r + 1) * local, :], width),
                fill(gub_ref[r // 2][:, half : half + hidden], width),
                jnp.zeros((TILE - 4 - local, width), F32),
            ]
            tparts_s[r] = jnp.concatenate(lines, axis=0).astype(BF16)
        for h in range(halves):
            for p in reversed(range(pairs)):
                mnear[h][p].wait_recv()
                spot = pl.ds(pl.multiple_of(share_at(h, partner("mp", 2 * p)), TILE), share)
                joined = merged_s[spot, :].astype(F32) + mnear_s[h, p].astype(F32)
                merged_s[spot, :] = joined.astype(BF16)
                if p:
                    mfar[h][p].start()
        for c in tnear:
            c.start()
        total = linein_s[0]
        for c, r in zip(lines_in, beside):
            c.wait_recv()
            total = total + linein_s[r]
        lineout_s[0] = total
        for c in lines_out:
            c.start()
        total = parts_s[0].astype(F32)
        for p in reversed(range(1, pairs)):
            pfar[p].wait_recv()
            total = total + pfar_s[p].astype(F32)
        parts_s[0] = total.astype(BF16)
        for c in main_out:
            c.start()
        input_part(0)

        for h in range(halves):
            mine = pl.ds(pl.multiple_of(share_at(h, me), TILE), share)
            total = merged_s[mine, :].astype(F32)
            for p in reversed(range(1, pairs)):
                mfar[h][p].wait_recv()
                total = total + mfar_s[h, p].astype(F32)
            mfar_s[h, 0] = total.astype(BF16)
            for c in across[h]:
                c.start()
        for p in reversed(range(pairs)):
            tnear[p].wait_recv()
            tparts_s[2 * p] = (tparts_s[2 * p].astype(F32) + tnear_s[p].astype(F32)).astype(BF16)
            if p:
                tfar[p].start()
        input_part(1)

        for h in range(halves):
            spot = pl.ds(pl.multiple_of(deep * small, TILE), small)
            total = mfar_s[h, 0, spot, :].astype(F32)
            for c, r in zip(across[h], behind):
                c.wait_recv()
                total = total + mpiece_s[h, r].astype(F32)
            mpiece_s[h, 0] = total.astype(BF16)
            keep_merge(h).start()
            for c in back[h]:
                c.start()
        spot = pl.ds(pl.multiple_of(deep * main_piece, TILE), main_piece)
        total = parts_s[0, spot, :].astype(F32)
        for c, r in zip(main_out, behind):
            c.wait_recv()
            total = total + main_s[r].astype(F32)
        mainsum_s[...] = total.astype(BF16)
        keep_main().start()
        for c in main_all:
            c.start()
        input_part(2)

        for h in range(halves):
            keep_merge(h).wait()
            for c in back[h]:
                c.wait_recv()
            for c in spread[h][-1:] + spread[h][-2::-1]:
                c.start()
        total = tparts_s[0].astype(F32)
        for p in reversed(range(1, pairs)):
            tfar[p].wait_recv()
            total = total + tfar_s[p].astype(F32)
        tparts_s[0] = total.astype(BF16)
        for c in tails:
            c.start()
        output_part(0)
        output_part(1)
        for h in range(halves):
            for c, after in zip(spread[h], onward[h]):
                c.wait_recv()
                after.start()
            if h == 0:
                output_part(2)

        total = lineout_s[0]
        for c, r in zip(lines_out, behind):
            c.wait_recv()
            total = total + lineout_s[r]
        sums_ref[...] = total
        total = tparts_s[0].astype(F32)
        for c, r in zip(tails, behind):
            c.wait_recv()
            total = total + tails_s[r].astype(F32)
        tail_ref[...] = total
        for h in range(halves):
            spread[h][-1].wait_recv()
            for c in onward[h]:
                c.wait_recv()
        for c in main_all + ffn_all:
            c.wait_recv()
        keep_ffn().wait()
        keep_main().wait()
        for h in range(halves):
            for c in mnear[h] + list(mfar[h].values()) + across[h] + back[h] + spread[h]:
                c.wait_send()
            for c in onward[h]:
                c.wait_send()
        for c in ffn_out + ffn_all + lines_in + lines_out + tnear + list(tfar.values()):
            c.wait_send()
        for c in pnear + list(pfar.values()) + main_out + tails + main_all:
            c.wait_send()
        for j in range(PARTS):
            take_gin(j).wait()
            take_raw(j).wait()


def back_rows(
    q,
    k,
    v,
    ga,
    rinv,
    att,
    n1,
    wt,
    p,
    idx,
    ffn,
    gmid,
    stats,
    x,
    g1,
    b1,
    gproj,
    gub,
    sums2,
    act,
    base,
    second,
    wm,
    g0,
    table_width,
    head_dim,
    local,
    near_size,
    far_size,
):
    rows, width = q.shape
    wide = x.shape[1]
    heads = width // head_dim
    groups, steps, sets, _, cover = p.shape
    dense_steps = 7
    count = rows // dense_steps
    narrow = 256
    pairs = near_size // 2
    piece = (ffn.shape[0] // far_size, ffn.shape[1])
    part = (4 * local * head_dim, width)
    main_piece = (4 * local * head_dim // far_size, width)
    total_rows = wide // narrow * width
    halves = 2 if total_rows // (2 * near_size * far_size) % TILE == 0 else 1
    share = total_rows // halves // near_size
    small = share // far_size
    near, far = near_size - 1, far_size - 1
    copies = 2 * far + halves * (4 * pairs - 2 + 2 * far) + near + far
    copies += (2 * pairs - 1) + 2 * far + (2 * pairs - 1) + far

    def place(i):
        return (jnp.maximum(i - steps, 0), 0)

    def p_place(i):
        return (0, jnp.minimum(i, steps - 1), 0, 0, 0)

    return call(
        functools.partial(back_kernel, head_dim, local, near_size, far_size, dense_steps),
        steps + dense_steps,
        (q, k, v, ga, rinv, att, n1, wt, p, idx, ffn, gmid, stats, x, g1, b1, gproj, gub, sums2)
        + (act, base, second, wm, g0),
        [anywhere()] * 8
        + [
            pl.BlockSpec((groups, 1, sets, COVER, cover), p_place),
            whole(idx.shape),
            whole(ffn.shape),
            pl.BlockSpec((count, width), place),
            pl.BlockSpec((count, 8), place),
            pl.BlockSpec((count, wide), place),
            whole(g1.shape),
            whole(b1.shape),
            whole(gproj.shape),
            whole(gub.shape),
            whole(sums2.shape),
        ]
        + [anywhere()] * 4
        + [whole(g0.shape)],
        [
            jax.ShapeDtypeStruct((rows, width), BF16),
            jax.ShapeDtypeStruct((rows, wide), BF16),
            jax.ShapeDtypeStruct((far_size,) + piece, BF16),
            jax.ShapeDtypeStruct((far_size,) + main_piece, BF16),
            jax.ShapeDtypeStruct((TILE, width), F32),
            jax.ShapeDtypeStruct((halves, near_size, far_size, small, narrow), BF16),
            jax.ShapeDtypeStruct((8, width), F32),
        ],
        [
            anywhere(),
            anywhere(),
            anywhere(),
            anywhere(),
            whole((TILE, width)),
            anywhere(),
            whole((8, width)),
        ],
        [pltpu.VMEM((rows, width), BF16)] * 7
        + [pltpu.VMEM((3 * width, width), BF16)]
        + [pltpu.VMEM((rows, width), BF16)] * 3
        + [
            pltpu.VMEM((TILE, groups, COVER, cover), F32),
            pltpu.VMEM((heads, COVER, COVER), F32),
            pltpu.VMEM((cover, GROUP * head_dim), BF16),
            pltpu.VMEM((heads, table_width), F32),
            pltpu.VMEM((far_size,) + piece, BF16),
            pltpu.VMEM(piece, BF16),
            pltpu.VMEM((total_rows, narrow), BF16),
            pltpu.VMEM((halves, pairs, share, narrow), BF16),
            pltpu.VMEM((halves, pairs, share, narrow), BF16),
            pltpu.VMEM((halves, far_size, small, narrow), BF16),
            pltpu.VMEM((near_size, TILE, width), BF16),
            pltpu.VMEM((pairs, TILE, width), BF16),
            pltpu.VMEM((pairs, TILE, width), BF16),
            pltpu.VMEM((near_size,) + part, BF16),
            pltpu.VMEM((pairs,) + part, BF16),
            pltpu.VMEM((pairs,) + part, BF16),
            pltpu.VMEM((far_size,) + main_piece, BF16),
            pltpu.VMEM(main_piece, BF16),
            pltpu.VMEM((far_size, TILE, width), BF16),
            pltpu.VMEM((near_size, 8, width), F32),
            pltpu.VMEM((far_size, 8, width), F32),
            pltpu.VMEM((8, width), F32),
            pltpu.VMEM((rows, wide), BF16),
            pltpu.VMEM((rows, 128), F32),
            pltpu.VMEM(wm.shape, BF16),
            pltpu.VMEM((act.shape[0] * act.shape[2], width), BF16),
            pltpu.SemaphoreType.DMA((6, LEVELS, sets)),
            pltpu.SemaphoreType.DMA((4 + halves,)),
            pltpu.SemaphoreType.DMA((2 + act.shape[0] + near_size,)),
            pltpu.SemaphoreType.DMA((2, PARTS)),
            pltpu.SemaphoreType.DMA((2 * copies,)),
        ],
        2 * rows * width * (24 * width + wide),
        rows * width * 20,
        group=2,
    )


def last_kernel(
    head_dim,
    local,
    window,
    live_ref,
    raw_ref,
    gin16_ref,
    g0_ref,
    b0_ref,
    sums_ref,
    tail_ref,
    wm_hbm,
    main_hbm,
    ffn_hbm,
    full_hbm,
    out_ref,
    gin_ref,
    gain0_ref,
    bias0_ref,
    gqkv_ref,
    gproj_ref,
    gqb_ref,
    gtab_ref,
    gub_ref,
    *rest,
):
    line_refs, rest = rest[:6], rest[6:]
    gmerge_hbm, gup_hbm, gdown_hbm, wm_ref, main_ref, ffn_ref, full_ref = rest[:7]
    gmerge_ref, gup_ref, gdown_ref, in_sems, out_sems = rest[7:]
    step = pl.program_id(0)
    count, width = raw_ref.shape
    rows = count * pl.num_programs(0)
    halves = full_ref.shape[0]
    narrow = full_ref.shape[2]

    def bring(i):
        pair = (
            (main_hbm, main_ref),
            (ffn_hbm, ffn_ref),
            (wm_hbm, wm_ref),
            (full_hbm, full_ref),
        )[i]
        return pltpu.make_async_copy(*pair, in_sems.at[i])

    def take(i):
        if i < 2:
            pair = ((gup_ref, gup_hbm), (gdown_ref, gdown_hbm))[i]
        else:
            here = pl.ds((i - 2) * narrow, narrow)
            pair = (gmerge_ref.at[here], gmerge_hbm.at[here])
        return pltpu.make_async_copy(*pair, out_sems.at[i])

    @pl.when(step == 0)
    def _():
        for i in range(4):
            bring(i).start()

    live = live_rows(live_ref, step * count, count, rows, width, window)
    out_ref[...] = jnp.where(live, raw_ref[...].astype(F32), 0.0)
    gin_ref[...] = gin16_ref[...].astype(F32)

    @pl.when(step == 0)
    def _():
        span = local * head_dim
        bring(0).wait()
        main = main_ref[...].astype(F32)
        for l in range(local):
            for t in range(3):
                at = t * span + l * head_dim
                gqkv_ref[l, t * head_dim : (t + 1) * head_dim, :] = main[at : at + head_dim]
        gproj_ref[...] = main[3 * span :]
        rows_of = []
        for l in range(local):
            here = slice(l * head_dim, (l + 1) * head_dim)
            rows_of.append(
                jnp.concatenate([tail_ref[t : t + 1, here] for t in range(3)], axis=1)
            )
        gqb_ref[...] = jnp.concatenate(rows_of, axis=0)
        gtab_ref[...] = tail_ref[3 : 3 + local, : gtab_ref.shape[1]]
        gub_ref[...] = tail_ref[3 + local : 4 + local, : gub_ref.shape[1]]
        for i, ref in enumerate(line_refs):
            ref[...] = sums_ref[i : i + 1, :]

    @pl.when(step == 1)
    def _():
        hidden = gup_ref.shape[1]
        bring(1).wait()
        gup_ref[...] = ffn_ref[:, :hidden].astype(F32)
        take(0).start()
        gdown_ref[...] = ffn_ref[:, hidden:].astype(F32).T
        take(1).start()
        bring(2).wait()
        bring(3).wait()

    low_sum = sums_ref[6:7, :]
    for j in range(halves):

        @pl.when(step == 2 + j)
        def _():
            cols = pl.ds(j * narrow, narrow)
            grad = full_ref[j].astype(F32).T
            weight = wm_ref[cols, :].astype(F32)
            gain = jnp.sum(weight * grad, axis=1, keepdims=True)
            shift = jnp.sum(weight * low_sum, axis=1, keepdims=True)
            gain0_ref[:, cols] = jnp.broadcast_to(gain, (narrow, 128)).T[:1, :]
            bias0_ref[:, cols] = jnp.broadcast_to(shift, (narrow, 128)).T[:1, :]
            scale = jnp.broadcast_to(g0_ref[:, cols], (8, narrow)).T[:, :1]
            offset = jnp.broadcast_to(b0_ref[:, cols], (8, narrow)).T[:, :1]
            gmerge_ref[cols, :] = grad * scale + offset * low_sum
            take(2 + j).start()

    @pl.when(step == pl.num_programs(0) - 1)
    def _():
        for i in range(2 + halves):
            take(i).wait()


def last_rows(
    live, raw, gin16, wm, g0, b0, main, ffn, full, sums, tail, local, head_dim, rel, window
):
    rows, width = raw.shape
    wide = gin16.shape[1]
    step = rows // 7
    hidden = ffn.shape[1] // 2
    span = local * head_dim
    narrow_block = pl.BlockSpec((step, width), lambda i: (i, 0))
    wide_block = pl.BlockSpec((step, wide), lambda i: (i, 0))
    rest = [g0, b0, sums, tail]
    later = [wm, main, ffn, full]
    shapes = [
        (1, wide),
        (1, wide),
        (local, 3 * head_dim, width),
        (span, width),
        (local, 3 * head_dim),
        (local, rel),
        (1, hidden),
    ] + [(1, width)] * 6
    large = [(wide, width), (width, hidden), (hidden, width)]
    return call(
        functools.partial(last_kernel, head_dim, local, window),
        7,
        [live, raw, gin16] + rest + later,
        [pl.BlockSpec(memory_space=pltpu.SMEM), narrow_block, wide_block]
        + [whole(a.shape) for a in rest]
        + [anywhere()] * len(later),
        [
            jax.ShapeDtypeStruct((rows, width), F32),
            jax.ShapeDtypeStruct((rows, wide), F32),
        ]
        + [jax.ShapeDtypeStruct(shape, F32) for shape in shapes + large],
        [narrow_block, wide_block]
        + [whole(shape) for shape in shapes]
        + [anywhere()] * len(large),
        [pltpu.VMEM(a.shape, BF16) for a in later]
        + [pltpu.VMEM(shape, F32) for shape in large]
        + [
            pltpu.SemaphoreType.DMA((len(later),)),
            pltpu.SemaphoreType.DMA((2 + full.shape[0],)),
        ],
        2 * rows * width,
        rows * wide * 9,
    )


def shards(
    inputs,
    norm0_gain,
    norm0_bias,
    merge_weight,
    norm1_gain,
    norm1_bias,
    qkv_weight,
    qkv_bias,
    rel_table,
    rel_index,
    regions,
    live_windows,
    proj_weight,
    proj_bias,
    norm2_gain,
    norm2_bias,
    up_weight,
    up_bias,
    down_weight,
    down_bias,
    cotangent,
    n_dp,
    n_mp,
):
    micro, strip_rows, wide = inputs.shape
    width = merge_weight.shape[1]
    win = rel_index.shape[0]
    local, packed = qkv_bias.shape
    head_dim = packed // 3
    heads = local * n_mp
    hidden = up_bias.shape[0]
    rel = rel_table.shape[1]
    rows = micro * strip_rows
    windows = rows // win
    sets = windows // TILE
    strip = lax.axis_index("mp")

    region = lax.dynamic_slice_in_dim(regions, strip * strip_rows, strip_rows, axis=1)
    region = region.reshape(sets, rows // sets)
    jump = rows // sets // TILE - 1
    region = jnp.stack([region[:, o * jump : o * jump + COVER] for o in range(TILE)])
    region = jnp.tile(region[:, :, None, :], (1, 1, 1, GROUP))
    table_width = -(-rel // 128) * 128
    live = live_windows.T
    vecs = (proj_bias[None], norm2_gain[None], norm2_bias[None], down_bias[None])
    gain0, bias0 = norm0_gain[None], norm0_bias[None]
    gain1, bias1 = norm1_gain[None], norm1_bias[None]

    x = inputs.reshape(rows, wide)
    stats, n1, q, k, v, att, rinv, p, tiles, wt, second = front_rows(
        x,
        gain0,
        bias0,
        merge_weight,
        gain1,
        bias1,
        jnp.transpose(qkv_weight, (1, 2, 0)).reshape(local * packed, width),
        qkv_bias,
        rel_table,
        up_bias.reshape(-1, 128),
        up_weight,
        down_weight,
        proj_weight.reshape(local * head_dim, width),
        rel_index,
        region,
        n_mp,
        head_dim,
    )
    base, act, gmid, gatt, ffn_part, gub, gproj, sums2 = ffn_rows(
        live,
        n1,
        att,
        cotangent.reshape(rows, width),
        stats,
        tiles,
        second,
        vecs,
        local,
        hidden,
        win,
    )
    raw, gin16, ffn_sum, main, tail, gmerge, sums = back_rows(
        q,
        k,
        v,
        gatt,
        rinv,
        att,
        n1,
        wt,
        p,
        rel_index,
        ffn_part,
        gmid,
        stats,
        x,
        gain1,
        bias1,
        gproj,
        gub,
        sums2,
        act,
        base,
        second,
        merge_weight,
        gain0,
        table_width,
        head_dim,
        local,
        n_mp,
        n_dp,
    )
    span = local * head_dim
    out, grad_input, ggain0, gbias0, gqkv, gproj, gqb, gtab, gub, *lines, gmerge, gup, gdown = (
        last_rows(
            live,
            raw,
            gin16,
            merge_weight,
            gain0,
            bias0,
            main.reshape(4 * span, width),
            ffn_sum.reshape(width, 2 * hidden),
            gmerge.reshape(-1, width, gmerge.shape[4]),
            sums,
            tail,
            local,
            head_dim,
            rel,
            win,
        )
    )
    gpb, gain2, bias2, gdb, gain1, bias1 = (x.reshape(width) for x in lines)
    return (
        out.reshape(micro, strip_rows, width),
        grad_input.reshape(micro, strip_rows, wide),
        ggain0.reshape(wide),
        gbias0.reshape(wide),
        gmerge,
        gain1,
        bias1,
        jnp.transpose(gqkv, (2, 0, 1)),
        gqb,
        gtab,
        gproj.reshape(local, head_dim, width),
        gpb,
        gain2,
        bias2,
        gup,
        gub.reshape(hidden),
        gdown,
        gdb,
    )


def solution(mesh):
    placed = (
        P(None, ("dp", "mp"), None),
        P(),
        P(),
        P(),
        P(),
        P(),
        P(None, "mp", None),
        P("mp", None),
        P("mp", None),
        P(),
        P(None, "dp"),
        P(None, "dp"),
        P("mp", None, None),
        P(),
        P(),
        P(),
        P(None, "mp"),
        P("mp"),
        P("mp", None),
        P(),
        P(None, ("dp", "mp"), None),
    )
    return jax.shard_map(
        functools.partial(shards, n_dp=mesh.shape["dp"], n_mp=mesh.shape["mp"]),
        mesh=mesh,
        in_specs=placed,
        out_specs=(
            P(None, ("dp", "mp"), None),
            P(None, ("dp", "mp"), None),
            P(),
            P(),
            P(),
            P(),
            P(),
            P(None, "mp", None),
            P("mp", None),
            P("mp", None),
            P("mp", None, None),
            P(),
            P(),
            P(),
            P(None, "mp"),
            P("mp"),
            P("mp", None),
            P(),
        ),
        check_vma=False,
    )
```

```python
import functools
import math

import jax
import jax.numpy as jnp
from jax import lax
from jax.experimental import pallas as pl
from jax.experimental.pallas import tpu as pltpu
from jax.sharding import PartitionSpec as P

F32 = jnp.float32
BF16 = jnp.bfloat16
EPSILON = 1e-05
MASKED = -1e30
COVER = 64
TILE = 16
GROUP = 4
VMEM_LIMIT = 60 << 20


def dot(left, right):
    return jnp.dot(left, right, preferred_element_type=F32)


def dot_rt(left, right):
    return lax.dot_general(left, right, (((1,), (1,)), ((), ())), preferred_element_type=F32)


def dot_lt(left, right):
    return lax.dot_general(left, right, (((0,), (0,)), ((), ())), preferred_element_type=F32)


def whole(shape):
    return pl.BlockSpec(shape, lambda i: (0,) * len(shape), pipeline_mode=pl.Buffered(1))


def anywhere():
    return pl.BlockSpec(memory_space=pl.ANY)


def call(kernel, grid, ins, in_specs, outs, out_specs, scratch, flops, nbytes, group=None):
    extra = {} if group is None else {"collective_id": group, "has_side_effects": True}
    return pl.pallas_call(
        kernel,
        grid=(grid,),
        in_specs=in_specs,
        out_specs=out_specs,
        out_shape=outs,
        scratch_shapes=scratch,
        compiler_params=pltpu.CompilerParams(
            dimension_semantics=("arbitrary",), vmem_limit_bytes=VMEM_LIMIT, **extra
        ),
        cost_estimate=pl.CostEstimate(flops=flops, bytes_accessed=nbytes, transcendentals=0),
    )(*ins)


def partner(axis, flips):
    at = lax.axis_index(axis)
    bit = 1
    while bit <= flips:
        if flips & bit:
            at = at + bit * (1 - 2 * lax.rem(lax.div(at, jnp.int32(bit)), jnp.int32(2)))
        bit *= 2
    return at


def send(axis, flips, src, dst, send_sem, recv_sem):
    return pltpu.make_async_remote_copy(
        src_ref=src,
        dst_ref=dst,
        send_sem=send_sem,
        recv_sem=recv_sem,
        device_id={axis: partner(axis, flips)},
        device_id_type=pl.DeviceIdType.MESH,
    )


def greet(peers):
    barrier = pltpu.get_barrier_semaphore()
    for axis, flips in peers:
        pl.semaphore_signal(
            barrier,
            inc=1,
            device_id={axis: partner(axis, flips)},
            device_id_type=pl.DeviceIdType.MESH,
        )
    pl.semaphore_wait(barrier, len(peers))


class Gather:
    def __init__(self, axis, size, own, held, send_sems, recv_sems, own_sem):
        self.axis, self.size, self.own, self.held = axis, size, own, held
        self.send_sems, self.recv_sems, self.own_sem = send_sems, recv_sems, own_sem

    def straight(self, r):
        return send(
            self.axis, r, self.own, self.held.at[r], self.send_sems.at[r], self.recv_sems.at[r]
        )

    def onward(self, r):
        return send(
            self.axis,
            1,
            self.held.at[r],
            self.held.at[r + 1],
            self.send_sems.at[r + 1],
            self.recv_sems.at[r + 1],
        )

    def keep(self):
        return pltpu.make_async_copy(self.own, self.held.at[0], self.own_sem)

    def start(self, flips=None):
        evens = list(range(2, self.size, 2))
        for r in evens + [1] if flips is None else flips:
            self.straight(r).start()
        if flips is None or 1 in flips:
            self.keep().start()

    def forward(self, r):
        self.straight(r).wait_recv()
        self.onward(r).start()

    def finish(self):
        self.keep().wait()
        self.straight(1).wait()
        for r in range(2, self.size, 2):
            self.straight(r).wait_send()
            self.onward(r).wait()


def spans(total, step):
    return [(start, min(step, total - start)) for start in range(0, total, step)]


def norm_parts(values):
    mean = jnp.mean(values, axis=-1, keepdims=True)
    center = values - mean
    spread = jnp.mean(center * center, axis=-1, keepdims=True) + EPSILON
    inverse = lax.rsqrt(spread)
    return center * inverse, mean, inverse, spread


def norm_back(grad, normed, inverse):
    mean_grad = jnp.mean(grad, axis=-1, keepdims=True)
    mean_cross = jnp.mean(grad * normed, axis=-1, keepdims=True)
    return inverse * (grad - mean_grad - normed * mean_cross)


def head_mask(head_dim):
    rows = lax.broadcasted_iota(jnp.int32, (GROUP * COVER, GROUP * head_dim), 0) // COVER
    cols = lax.broadcasted_iota(jnp.int32, (GROUP * COVER, GROUP * head_dim), 1) // head_dim
    return (rows == cols).astype(F32).astype(BF16)


def tiled(block, mask):
    return jnp.concatenate([block] * GROUP, axis=0) * mask


def pair_row(idx_ref, pair):
    win = idx_ref.shape[0]
    gap = jnp.full((1, COVER - win), -1, jnp.int32)
    parts = []
    for i in (2 * pair, 2 * pair + 1):
        parts.append(idx_ref[i : i + 1, :] if i < win else jnp.full((1, win), -1, jnp.int32))
        parts.append(gap)
    return jnp.concatenate(parts, axis=1)


def index_onehot(row, table_width):
    entry = lax.broadcasted_iota(jnp.int32, (table_width, row.shape[1]), 0)
    return (entry == row).astype(F32).astype(BF16)


def fill(x, width):
    return jnp.concatenate([x, jnp.zeros((x.shape[0], width - x.shape[1]), x.dtype)], axis=1)


def front_kernel(
    head_dim,
    local,
    size,
    merge_steps,
    x_ref,
    g0_ref,
    b0_ref,
    wm_ref,
    g1_ref,
    b1_ref,
    qkvw_ref,
    qkvb_ref,
    tab_ref,
    ub_ref,
    up_ref,
    down_ref,
    proj_ref,
    idx_ref,
    rid_ref,
    stats_ref,
    n1_ref,
    q_ref,
    k_ref,
    v_ref,
    att_ref,
    rinv_ref,
    p_ref,
    tiles_ref,
    wt_ref,
    second_ref,
    first_s,
    tiles_s,
    own_s,
    tile_s,
    second_s,
    mid_s,
    q_s,
    k_s,
    v_s,
    att_s,
    rinv_s,
    base_s,
    bias_s,
    mask_s,
    tile_send,
    tile_recv,
    first_send,
    first_recv,
    second_send,
    second_recv,
    own_sems,
    out_sems,
):
    step = pl.program_id(0)
    rows, width = mid_s.shape
    heads = width // head_dim
    lanes = GROUP * head_dim
    groups = heads // GROUP
    per_group = size // groups
    scale = 1.0 / math.sqrt(head_dim)
    span = local * head_dim
    evens = list(range(2, size, 2))
    main = Gather("mp", size, own_s, first_s, first_send, first_recv, own_sems.at[0])
    rest = Gather("mp", size, second_s, second_ref, second_send, second_recv, own_sems.at[1])

    def tile_copy(r):
        return send("mp", r, tile_s, tiles_s.at[r], tile_send.at[r], tile_recv.at[r])

    @pl.when(step == 0)
    def _():
        own_s[...] = qkvw_ref[...]
        bias = qkvb_ref[...].astype(F32)
        lines = []
        for t in range(3):
            parts = [
                bias[l : l + 1, t * head_dim : (t + 1) * head_dim] for l in range(local)
            ]
            lines.append(fill(jnp.concatenate(parts, axis=1), width))
        lines.append(fill(tab_ref[...].astype(F32), width))
        up_bias = ub_ref[...].astype(F32)
        parts = [up_bias[i : i + 1, :] for i in range(up_bias.shape[0])]
        lines.append(fill(jnp.concatenate(parts, axis=1), width))
        lines.append(jnp.zeros((TILE - 4 - local, width), F32))
        tile_s[...] = jnp.concatenate(lines, axis=0).astype(BF16)
        greet([("mp", r) for r in range(1, size)])
        for r in range(1, size):
            tile_copy(r).start()
        tiles_s[0] = tile_s[...]
        main.start([r for r in evens if r < 2 * per_group] + [1])
        hidden = up_ref.shape[1]
        second_s[:hidden, :] = up_ref[...].T
        second_s[hidden : 2 * hidden, :] = down_ref[...]
        second_s[2 * hidden :, :] = proj_ref[...]

    @pl.when(step == 2)
    def _():
        main.start([r for r in evens if r >= 2 * per_group])

    @pl.when(step == merge_steps - 3)
    def _():
        rest.start()

    @pl.when(step < merge_steps)
    def _():
        count = x_ref.shape[0]
        here = pl.ds(pl.multiple_of(step * count, TILE), count)
        normed, mean, inverse, _ = norm_parts(x_ref[...].astype(F32))
        normed_in = (normed * g0_ref[...] + b0_ref[...]).astype(BF16)
        normed1, mean1, inverse1, spread1 = norm_parts(dot(normed_in, wm_ref[...]))
        n1_ref[...] = normed1.astype(BF16)
        stats = [mean, inverse, mean1, inverse1, spread1 * inverse1]
        stats_ref[...] = jnp.concatenate(stats + [mean] * (8 - len(stats)), axis=1)
        mid_s[here, :] = (normed1 * g1_ref[...] + b1_ref[...]).astype(BF16)

    table_step = merge_steps - 3

    @pl.when(step == merge_steps - 1)
    def _():
        for r in evens:
            if r < 2 * per_group:
                main.forward(r)

    @pl.when(step == table_step)
    def _():
        mask_s[...] = head_mask(head_dim)
        att_s[...] = jnp.zeros_like(att_s)
        rinv_s[...] = jnp.zeros_like(rinv_s)
        base_s[...] = jnp.full(base_s.shape, MASKED, F32)
        for r in range(1, size):
            tile_copy(r).wait_recv()

    all_pairs = list(range((idx_ref.shape[0] + 1) // 2))
    for i in range(2):

        @pl.when(step == table_step + i)
        def _():
            table = jnp.concatenate(
                [tiles_s[r].astype(F32)[3 : 3 + local, : 2 * 128] for r in range(size)], axis=0
            ).astype(BF16)
            here = all_pairs[i::2]
            rows_of = [pair_row(idx_ref, pair) for pair in here]
            found = [dot(table, index_onehot(row, table.shape[1])) for row in rows_of]
            found = [jnp.where(row < 0, MASKED, x) for row, x in zip(rows_of, found)]
            for pair, vals in zip(here, found):
                base_s[:, 2 * pair, :] = vals[:, :COVER]
                base_s[:, 2 * pair + 1, :] = vals[:, COVER:]

    @pl.when(step == table_step + 2)
    def _():
        tiles_ref[...] = tiles_s[...]

        def shift(g, _):
            full = jnp.concatenate([base_s[g * GROUP + h] for h in range(GROUP)], axis=1)
            for o in range(TILE):
                bias_s[g, o] = pltpu.roll(pltpu.roll(full, o, 0), o, 1) if o else full
            return 0

        lax.fori_loop(0, groups, shift, 0)
        for r in range(1, size):
            tile_copy(r).wait_send()

    def outward(ref, out, which, g):
        cols = pl.ds(pl.multiple_of(g * lanes, lanes), lanes)
        return pltpu.make_async_copy(ref.at[:, cols], out.at[:, cols], out_sems.at[which, g])

    def early_out(g):
        return [
            outward(ref, out, i, g)
            for i, (ref, out) in enumerate(((q_s, q_ref), (k_s, k_ref), (v_s, v_ref)))
        ]

    def late_out(g):
        return [outward(att_s, att_ref, 3, g), outward(rinv_s, rinv_ref, 4, g)]

    low_half = lax.broadcasted_iota(jnp.int32, (COVER, 2 * COVER), 1) < COVER
    region_of = lax.broadcasted_iota(jnp.int32, (8, GROUP * COVER), 0)
    sets = rid_ref.shape[1]
    block = rows // sets

    def attend(it, g):
        mask = mask_s[...]
        cols = pl.ds(pl.multiple_of(g * lanes, lanes), lanes)
        units = [(2 * it + i, u) for i in range(2) for u in range(sets)]
        starts = [pl.multiple_of(o * (block // TILE - 1) + u * block, TILE) for o, u in units]
        scores = []
        for start in starts:
            here = pl.ds(start, COVER)
            scores.append(dot_rt(q_s[here, cols], tiled(k_s[here, cols], mask)))
        weights = []
        for (o, u), s in zip(units, scores):
            member = (region_of == rid_ref[o, u]).astype(F32).astype(BF16)
            same = dot_lt(member[:, :COVER], member)
            s = s + bias_s[g, o] + jnp.where(same > 0.5, 0.0, MASKED)
            parts = []
            for c in range(GROUP // 2):
                x = s[:, c * 2 * COVER : (c + 1) * 2 * COVER]
                top0 = jnp.max(jnp.where(low_half, x, MASKED), axis=1, keepdims=True)
                top1 = jnp.max(jnp.where(low_half, MASKED, x), axis=1, keepdims=True)
                top = jnp.maximum(jnp.where(low_half, top0, top1), MASKED * 0.1)
                parts.append(jnp.exp(x - top).astype(BF16))
            w = jnp.concatenate(parts, axis=1)
            p_ref[0, o, u] = w
            weights.append(w)
        mixed = []
        for start, w in zip(starts, weights):
            vals = tiled(v_s[pl.ds(start, COVER), cols], mask)
            mixed.append(dot(w, jnp.concatenate([vals, mask], axis=1)))
        for start, a in zip(starts, mixed):
            here = pl.ds(start, COVER)
            total = a[:, lanes:]
            inv = jnp.where(total > 0.0, 1.0 / jnp.maximum(total, 0.5), 0.0)
            att_s[here, cols] += (a[:, :lanes] * inv).astype(BF16)
            rinv_s[here, cols] += inv.astype(BF16)

    @pl.when(step >= merge_steps)
    def _():
        g = step - merge_steps
        twice = 2 * per_group

        @pl.when(g == 0)
        def _():
            main.keep().wait()
            main.straight(1).wait_recv()
            for r in evens:
                if r < twice:
                    main.onward(r).wait_recv()

        for known in range(2, groups, 2):

            @pl.when(g == known)
            def _():
                for r in evens:
                    if known * per_group <= r < known * per_group + twice:
                        main.onward(r).wait_recv()

        @pl.when(g % 2 == 0)
        def _():
            shards = [g * per_group + j for j in range(twice)]
            cols = pl.ds(pl.multiple_of(g * lanes, 2 * lanes), 2 * lanes)
            outs = (q_s, k_s, v_s)
            part = rows // 3
            weights, biases = [], []
            for t in range(3):
                weight = []
                for s in shards:
                    for l in range(local):
                        at = (3 * l + t) * head_dim
                        weight.append(first_s[s, at : at + head_dim, :])
                    biases.append(tiles_s[s].astype(F32)[t : t + 1, :span])
                weight = jnp.concatenate(weight, axis=0)
                spot = pl.ds(pl.multiple_of(t * width + g * lanes, 2 * lanes), 2 * lanes)
                wt_ref[spot, :] = weight
                weights.append(weight.T)
            weight = jnp.concatenate(weights, axis=1)
            bias = jnp.concatenate(biases, axis=1)

            def project(i, _):
                here = pl.ds(pl.multiple_of(i * part, TILE), part)
                y = dot(mid_s[here, :], weight) + bias
                for t in range(3):
                    z = y[:, 2 * t * lanes : 2 * (t + 1) * lanes]
                    outs[t][here, cols] = (z * scale if t == 0 else z).astype(BF16)
                return 0

            lax.fori_loop(0, 3, project, 0)

        for c in early_out(g):
            c.start()

        def run(it, _):
            attend(it, g)
            return 0

        lax.fori_loop(0, TILE // 4, run, 0)

        @pl.when(g == 0)
        def _():
            for r in evens:
                if r >= twice:
                    main.forward(r)

        @pl.when(g == groups - 1)
        def _():
            for r in evens:
                rest.forward(r)

        lax.fori_loop(TILE // 4, TILE // 2, run, 0)
        for c in late_out(g):
            c.start()

        @pl.when(g == groups - 1)
        def _():
            main.straight(1).wait_send()
            for r in evens:
                main.straight(r).wait_send()
                main.onward(r).wait_send()
            rest.finish()
            for known in range(groups):
                for c in early_out(known) + late_out(known):
                    c.wait()


def front_rows(
    x, g0, b0, wm, g1, b1, qkvw, qkvb, tab, ub, up, down, proj, idx, rid, size, head_dim
):
    rows, wide = x.shape
    width = wm.shape[1]
    local = qkvb.shape[0]
    hidden = up.shape[1]
    heads = width // head_dim
    groups = heads // GROUP
    offsets, sets = rid.shape[0], rid.shape[1]
    cover = GROUP * COVER
    merge_steps = 7
    step = rows // merge_steps
    first = (3 * local * head_dim, width)
    second = (2 * hidden + local * head_dim, width)

    def place(i):
        return (jnp.minimum(i, merge_steps - 1), 0)

    def group_place(i):
        return (jnp.maximum(i - merge_steps, 0), 0, 0, 0, 0)

    small = [g0, b0, wm, g1, b1, qkvw, qkvb, tab, ub, up, down, proj, idx, rid]
    row_out = jax.ShapeDtypeStruct((rows, width), BF16)
    sems = [pltpu.SemaphoreType.DMA((size,))] * 6
    return call(
        functools.partial(front_kernel, head_dim, local, size, merge_steps),
        merge_steps + groups,
        [x] + small,
        [pl.BlockSpec((step, wide), place)] + [whole(a.shape) for a in small],
        [jax.ShapeDtypeStruct((rows, 8), F32), row_out]
        + [row_out] * 5
        + [
            jax.ShapeDtypeStruct((groups, offsets, sets, COVER, cover), BF16),
            jax.ShapeDtypeStruct((size, TILE, width), BF16),
            jax.ShapeDtypeStruct((3 * width, width), BF16),
            jax.ShapeDtypeStruct((size,) + second, BF16),
        ],
        [pl.BlockSpec((step, 8), place), pl.BlockSpec((step, width), place)]
        + [anywhere()] * 5
        + [
            pl.BlockSpec((1, offsets, sets, COVER, cover), group_place),
            whole((size, TILE, width)),
            whole((3 * width, width)),
            anywhere(),
        ],
        [
            pltpu.VMEM((size,) + first, BF16),
            pltpu.VMEM((size, TILE, width), BF16),
            pltpu.VMEM(first, BF16),
            pltpu.VMEM((TILE, width), BF16),
            pltpu.VMEM(second, BF16),
        ]
        + [pltpu.VMEM((rows, width), BF16)] * 6
        + [
            pltpu.VMEM((heads, COVER, COVER), F32),
            pltpu.VMEM((groups, TILE, COVER, cover), F32),
            pltpu.VMEM((cover, GROUP * head_dim), BF16),
        ]
        + sems
        + [pltpu.SemaphoreType.DMA((2,)), pltpu.SemaphoreType.DMA((5, groups))],
        2 * rows * width * (wide + 18 * width),
        rows * width * 40,
        group=0,
    )


REACH = math.sqrt(2.0) / 0.3275911
CENTRE = 0.125


def centred():
    rational = (0.254829592, -0.284496736, 1.421413741, -1.453152027, 1.061405429)
    plain = [0.5 * a * REACH ** (k + 1) for k, a in enumerate(rational)]
    out = [0.0] * len(plain)
    for k, a in enumerate(plain):
        for j in range(k + 1):
            out[j] += a * math.comb(k, j) * CENTRE ** (k - j)
    return out


def gelu_and_slope(pre):
    x = pre.astype(BF16)
    t = pl.reciprocal(jnp.abs(pre) + REACH, approx=True)
    s = (t - CENTRE).astype(BF16)
    terms = [BF16(a) for a in centred()]
    poly = terms[4]
    for a in reversed(terms[:4]):
        poly = poly * s + a
    part = poly * t.astype(BF16)
    bell = jnp.exp2((x * x) * BF16(-0.5 * math.log2(math.e)))
    size = jnp.abs(x)
    act = jnp.maximum(x, BF16(0.0)) - size * (part * bell)
    under = (part - size * BF16(1.0 / math.sqrt(2.0 * math.pi))) * bell
    return act, jnp.where(x > BF16(0.0), BF16(1.0) - under, under)


def live_rows(live_ref, start, count, rows, width, window):
    micro = live_ref.shape[1]
    micro_rows = rows // micro
    before = lax.axis_index("mp") * micro_rows
    row = lax.broadcasted_iota(jnp.int32, (count, width), 0) + start
    live = None
    for m in range(micro):
        last = m * micro_rows + jnp.minimum(live_ref[0, m] * window - before, micro_rows)
        inside = (row >= m * micro_rows) & (row < last)
        live = inside if live is None else live | inside
    return live


def ffn_kernel(
    local,
    window,
    live_ref,
    n1_ref,
    att_ref,
    cot_ref,
    stats_ref,
    wp_ref,
    pb_ref,
    g2_ref,
    b2_ref,
    db_ref,
    tail_ref,
    up_ref,
    down_ref,
    base_ref,
    act_ref,
    gmid_ref,
    gatt_ref,
    part_ref,
    gub_ref,
    gproj_ref,
    sums_ref,
    base_s,
    gffn_s,
    att_s,
    n2_s,
    inv_s,
    n_s,
    go_s,
    nt_s,
    gt_s,
    act_s,
    gp_s,
    odd_s,
    even_s,
    near_s,
    far_s,
    near_send,
    near_recv,
    far_send,
    far_recv,
    in_sems,
    out_sems,
    act_sem,
):
    step = pl.program_id(0)
    pairs = even_s.shape[0]
    pair = pairs - 1 - step
    rows, width = gffn_s.shape
    blocks = spans(rows, 512)
    hidden = up_ref.shape[1]
    wp = wp_ref[...].reshape(width, width)

    def near(p):
        return send("mp", 1, odd_s.at[p % 2], near_s.at[p], near_send.at[p], near_recv.at[p])

    def far(p):
        slot = far_s.at[p - 1]
        return send("mp", 2 * p, even_s.at[p], slot, far_send.at[p], far_recv.at[p])

    def bring(b):
        here = pl.ds(*blocks[b])
        whence = ((n1_ref, n_s), (att_ref, att_s), (cot_ref, go_s))
        return [
            pltpu.make_async_copy(src.at[here], dst.at[here], in_sems.at[i, b])
            for i, (src, dst) in enumerate(whence)
        ]

    def take(which, b):
        here = pl.ds(*blocks[b])
        src, dst = ((base_s, base_ref), (go_s, gmid_ref), (n2_s, gatt_ref))[which]
        return pltpu.make_async_copy(src.at[here], dst.at[here], out_sems.at[which, b])

    def take_act():
        return pltpu.make_async_copy(act_s.at[pl.ds(0, rows)], act_ref.at[pair], act_sem)

    @pl.when(step == 0)
    def _():
        for b in range(len(blocks)):
            for c in bring(b):
                c.start()
        greet([("mp", r) for r in [1] + [2 * p for p in range(1, pairs)]])
        bias_proj, gain2, bias2, bias_down = (x[...] for x in (pb_ref, g2_ref, b2_ref, db_ref))
        act_s[rows:, :] = jnp.zeros_like(act_s[rows:, :])
        gp_s[rows:, :] = jnp.zeros_like(gp_s[rows:, :])
        nt_s[width:, :] = jnp.ones_like(nt_s[width:, :])
        down_sum = jnp.zeros((1, width), F32)
        for b, (start, count) in enumerate(blocks):
            here = pl.ds(start, count)
            for c in bring(b):
                c.wait()
            stats = stats_ref[here, :]
            merged = n_s[here, :].astype(F32) * stats[:, 4:5] + stats[:, 2:3]
            middle = merged + dot(att_s[here, :], wp) + bias_proj
            base_s[here, :] = (middle + bias_down).astype(BF16)
            take(0, b).start()
            normed, _, inverse, _ = norm_parts(middle)
            n2_s[here, :] = normed.astype(BF16)
            inv_s[here, :] = jnp.broadcast_to(inverse, (count, inv_s.shape[1]))
            normed_ffn = (normed * gain2 + bias2).astype(BF16)
            n_s[here, :] = normed_ffn
            live = live_rows(live_ref, start, count, rows, width, window)
            grad_out = jnp.where(live, go_s[here, :].astype(F32), 0.0)
            down_sum = down_sum + jnp.sum(grad_out, axis=0, keepdims=True)
            grad_low = grad_out.astype(BF16)
            go_s[here, :] = grad_low
            whole_count = -(-count // 128) * 128
            if whole_count != count:
                filler = jnp.zeros((whole_count - count, width), BF16)
                normed_ffn = jnp.concatenate([normed_ffn, filler], axis=0)
                grad_low = jnp.concatenate([grad_low, filler], axis=0)
            nt_s[:width, start : start + whole_count] = normed_ffn.T
            gt_s[:, start : start + whole_count] = grad_low.T
        sums_ref[...] = jnp.zeros_like(sums_ref)
        sums_ref[3:4, :] = down_sum
        gffn_s[...] = jnp.zeros_like(gffn_s)

    def pass_on():
        @pl.when(step > 0)
        def _():
            near(pair + 1).wait_recv()
            joined = even_s[pair + 1].astype(F32) + near_s[pair + 1].astype(F32)
            even_s[pair + 1] = joined.astype(BF16)

        for p in range(1, pairs):

            @pl.when(pair + 1 == p)
            def _():
                far(p).start()

    up_t = up_ref[...].reshape(2 * hidden, width)
    down = down_ref[...].reshape(2 * hidden, width)
    up_bias = jnp.concatenate(
        [tail_ref[i].astype(F32)[3 + local : 4 + local, :hidden] for i in range(2)], axis=1
    )
    for b, (start, count) in enumerate(blocks):
        if b == 1:
            pass_on()
        here = pl.ds(start, count)
        act, slope = gelu_and_slope(dot_rt(n_s[here, :], up_t) + up_bias)
        grad_pre = dot_rt(go_s[here, :], down).astype(BF16) * slope
        act_s[here, :] = act
        gp_s[here, :] = grad_pre
        gffn_s[here, :] += dot(grad_pre, up_t)
    take_act().start()

    @pl.when(step > 1)
    def _():
        near(pair + 2).wait_send()

    grad_up = dot(nt_s[...], gp_s[...])
    gub_ref[0] = grad_up[width : width + 1, :]
    grad_up = grad_up[:width].astype(BF16)
    even_s[pair, :, :hidden] = grad_up[:, :hidden]
    odd_s[pair % 2, :, :hidden] = grad_up[:, hidden:]
    grad_down = dot(gt_s[...], act_s[...]).astype(BF16)
    even_s[pair, :, hidden:] = grad_down[:, :hidden]
    odd_s[pair % 2, :, hidden:] = grad_down[:, hidden:]
    near(pair).start()
    take_act().wait()

    @pl.when(step == pairs - 1)
    def _():
        gain2 = g2_ref[...]
        gain_sum = jnp.zeros((1, width), F32)
        bias_sum = jnp.zeros((1, width), F32)
        proj_sum = jnp.zeros((1, width), F32)
        grad_proj = jnp.zeros((width, width), F32)
        for b, (start, count) in enumerate(blocks):
            here = pl.ds(start, count)
            grad_ffn = gffn_s[here, :]
            normed = n2_s[here, :].astype(F32)
            gain_sum = gain_sum + jnp.sum(grad_ffn * normed, axis=0, keepdims=True)
            bias_sum = bias_sum + jnp.sum(grad_ffn, axis=0, keepdims=True)
            grad_middle = go_s[here, :].astype(F32) + norm_back(
                grad_ffn * gain2, normed, inv_s[here, :1]
            )
            proj_sum = proj_sum + jnp.sum(grad_middle, axis=0, keepdims=True)
            grad_attn = grad_middle.astype(BF16)
            go_s[here, :] = grad_attn
            take(1, b).start()
            grad_proj = grad_proj + dot_lt(att_s[here, :], grad_attn)
            n2_s[here, :] = dot_rt(grad_attn, wp).astype(BF16)
            take(2, b).start()
        gproj_ref[...] = grad_proj.astype(BF16)
        sums_ref[0:1, :] = proj_sum
        sums_ref[1:2, :] = gain_sum
        sums_ref[2:3, :] = bias_sum
        near(0).wait_recv()
        total = even_s[0].astype(F32) + near_s[0].astype(F32)
        for p in range(1, pairs):
            far(p).wait_recv()
            total = total + far_s[p - 1].astype(F32)
        part_ref[...] = total.astype(BF16)
        for p in range(pairs):
            if p < 2:
                near(p).wait_send()
            if p:
                far(p).wait_send()
        for b in range(len(blocks)):
            for which in range(3):
                take(which, b).wait()


def ffn_rows(live, n1, att, cot, stats, tiles, second, vecs, local, hidden, window):
    rows, width = n1.shape
    size = tiles.shape[0]
    pairs = size // 2
    padded = -(-rows // 128) * 128
    proj_rows = width // size
    proj_at = 2 * hidden // proj_rows
    blocks = len(spans(rows, 512))
    row_out = jax.ShapeDtypeStruct((rows, width), BF16)
    return call(
        functools.partial(ffn_kernel, local, window),
        pairs,
        (live, n1, att, cot, stats, second) + vecs + (tiles, second, second),
        [
            pl.BlockSpec(memory_space=pltpu.SMEM),
            anywhere(),
            anywhere(),
            anywhere(),
            whole(stats.shape),
            pl.BlockSpec(
                (size, proj_rows, width),
                lambda i: (0, proj_at, 0),
                pipeline_mode=pl.Buffered(1),
            ),
        ]
        + [whole((1, width))] * 4
        + [
            pl.BlockSpec((2, TILE, width), lambda i: (pairs - 1 - i, 0, 0)),
            pl.BlockSpec((2, hidden, width), lambda i: (pairs - 1 - i, 0, 0)),
            pl.BlockSpec((2, hidden, width), lambda i: (pairs - 1 - i, 1, 0)),
        ],
        [
            row_out,
            jax.ShapeDtypeStruct((pairs, rows, 2 * hidden), BF16),
            row_out,
            row_out,
            jax.ShapeDtypeStruct((width, 2 * hidden), BF16),
            jax.ShapeDtypeStruct((pairs, 1, 2 * hidden), F32),
            jax.ShapeDtypeStruct((width, width), BF16),
            jax.ShapeDtypeStruct((8, width), F32),
        ],
        [
            anywhere(),
            anywhere(),
            anywhere(),
            anywhere(),
            whole((width, 2 * hidden)),
            pl.BlockSpec((1, 1, 2 * hidden), lambda i: (pairs - 1 - i, 0, 0)),
            whole((width, width)),
            whole((8, width)),
        ],
        [
            pltpu.VMEM((rows, width), BF16),
            pltpu.VMEM((rows, width), F32),
            pltpu.VMEM((rows, width), BF16),
            pltpu.VMEM((rows, width), BF16),
            pltpu.VMEM((rows, 128), F32),
            pltpu.VMEM((rows, width), BF16),
            pltpu.VMEM((rows, width), BF16),
            pltpu.VMEM((width + TILE, padded), BF16),
            pltpu.VMEM((width, padded), BF16),
            pltpu.VMEM((padded, 2 * hidden), BF16),
            pltpu.VMEM((padded, 2 * hidden), BF16),
        ]
        + [pltpu.VMEM((min(pairs, 2), width, 2 * hidden), BF16)]
        + [pltpu.VMEM((pairs, width, 2 * hidden), BF16)] * 2
        + [pltpu.VMEM((max(pairs - 1, 1), width, 2 * hidden), BF16)]
        + [pltpu.SemaphoreType.DMA((pairs,))] * 4
        + [pltpu.SemaphoreType.DMA((3, blocks))] * 2
        + [pltpu.SemaphoreType.DMA(())],
        2 * rows * width * hidden * size * 6,
        rows * width * 20,
        group=1,
    )


LEVELS = 4
PARTS = 3


def back_kernel(
    head_dim,
    local,
    near_size,
    far_size,
    dense_steps,
    q_ref,
    k_ref,
    v_ref,
    ga_ref,
    rinv_ref,
    att_ref,
    n1_ref,
    wt_ref,
    p_ref,
    idx_ref,
    ffn_ref,
    gmid_ref,
    stats_ref,
    x_ref,
    g1_ref,
    b1_ref,
    gproj_ref,
    gub_ref,
    sums2_ref,
    act_ref,
    base_ref,
    second_ref,
    wm_ref,
    g0_ref,
    raw_ref,
    gin_ref,
    ffnsum_ref,
    main_ref,
    tail_ref,
    full_ref,
    sums_ref,
    q_s,
    k_s,
    v_s,
    ga_s,
    rinv_s,
    att_s,
    n1_s,
    wt_s,
    gq_s,
    gk_s,
    gv_s,
    ds_s,
    base_s,
    mask_s,
    gtab_s,
    ffncame_s,
    ffnown_s,
    merged_s,
    mnear_s,
    mfar_s,
    mpiece_s,
    tparts_s,
    tnear_s,
    tfar_s,
    parts_s,
    pnear_s,
    pfar_s,
    main_s,
    mainsum_s,
    tails_s,
    linein_s,
    lineout_s,
    lines_s,
    n0_s,
    inv0_s,
    wm_s,
    down_s,
    in_sems,
    more_sems,
    late_sems,
    out_sems,
    sems,
):
    step = pl.program_id(0)
    rows, width = gq_s.shape
    lanes = GROUP * head_dim
    groups = width // lanes
    scale = 1.0 / math.sqrt(head_dim)
    sets = p_ref.shape[2]
    block = rows // sets
    jump = block // TILE - 1
    pairs = near_size // 2
    span = local * head_dim
    me, deep = lax.axis_index("mp"), lax.axis_index("dp")
    beside = list(range(1, near_size))
    behind = list(range(1, far_size))
    evens = list(range(2, near_size, 2))
    piece = ffnsum_ref.shape[1]
    at_sem = [0]

    def copy(axis, r, src, dst):
        at_sem[0] += 2
        return send(axis, r, src, dst, sems.at[at_sem[0] - 2], sems.at[at_sem[0] - 1])

    def rows_at(ref, index, count):
        return ref.at[pl.ds(pl.multiple_of(index * count, TILE), count)]

    def bring(level):
        copies = []
        whence = (
            (q_ref, q_s),
            (k_ref, k_s),
            (v_ref, v_s),
            (ga_ref, ga_s),
            (rinv_ref, rinv_s),
            (att_ref, att_s),
        )
        part = TILE // LEVELS * jump
        first = COVER - jump
        for i, (src, dst) in enumerate(whence):
            for u in range(sets):
                if level == 0:
                    here = pl.ds(u * block, part + first)
                else:
                    here = pl.ds(u * block + first + level * part, part)
                copies.append(
                    pltpu.make_async_copy(src.at[here], dst.at[here], in_sems.at[i, level, u])
                )
        return copies

    def bring_more():
        return [
            pltpu.make_async_copy(n1_ref, n1_s, more_sems.at[0]),
            pltpu.make_async_copy(wt_ref, wt_s, more_sems.at[1]),
        ]

    act_bufs = (k_s, v_s, ga_s, rinv_s)
    chunks = act_ref.shape[0] * act_ref.shape[2] // width

    def bring_late():
        copies = [(base_ref, att_s), (wm_ref, wm_s)]
        per = act_ref.shape[2]
        each = width // per
        for p in range(act_ref.shape[0]):
            dst = act_bufs[p // each].at[:, pl.ds(p % each * per, per)]
            copies.append((act_ref.at[p], dst))
        hidden = per // 2
        for r in range(near_size):
            src = second_ref.at[r, pl.ds(hidden, hidden)]
            copies.append((src, down_s.at[pl.ds(r * hidden, hidden)]))
        return [
            pltpu.make_async_copy(src, dst, late_sems.at[i]) for i, (src, dst) in enumerate(copies)
        ]

    def dense_span(j):
        return pl.ds(j * (rows // PARTS), rows // PARTS)

    def take_gin(j):
        here = dense_span(j)
        return pltpu.make_async_copy(n0_s.at[here], gin_ref.at[here], out_sems.at[0, j])

    def take_raw(j):
        here = dense_span(j)
        return pltpu.make_async_copy(att_s.at[here], raw_ref.at[here], out_sems.at[1, j])

    def input_part(j):
        here = dense_span(j)
        grad_low = dot_rt(q_s[here, :], wm_s[...])
        normed = n0_s[here, :].astype(F32)
        grad = norm_back(grad_low * g0_ref[...], normed, inv0_s[here, :1])
        n0_s[here, :] = grad.astype(BF16)
        take_gin(j).start()

    def output_part(j):
        here = dense_span(j)
        total = att_s[here, :].astype(F32)
        for i in range(chunks):
            total = total + dot(act_bufs[i][here, :], down_s[i * width : (i + 1) * width, :])
        att_s[here, :] = total.astype(BF16)
        take_raw(j).start()

    def keep_main():
        return pltpu.make_async_copy(mainsum_s, main_ref.at[deep], more_sems.at[3])

    def keep_merge(h):
        src = mpiece_s.at[h, 0]
        return pltpu.make_async_copy(src, full_ref.at[h, me, deep], more_sems.at[4 + h])

    def keep_ffn():
        return pltpu.make_async_copy(ffnown_s, ffnsum_ref.at[deep], more_sems.at[2])

    ffn_out = [
        copy("dp", r, rows_at(ffn_ref, partner("dp", r), piece), ffncame_s.at[r]) for r in behind
    ]
    ffn_all = [copy("dp", r, ffnown_s, ffnsum_ref.at[deep]) for r in behind]

    halves = mfar_s.shape[0]
    half_rows = merged_s.shape[0] // halves
    share = half_rows // near_size
    small = share // far_size
    main_piece = parts_s.shape[1] // far_size

    def share_at(h, index):
        return h * half_rows + index * share

    def share_of(h, index):
        return merged_s.at[pl.ds(pl.multiple_of(share_at(h, index), TILE), share)]

    mnear, mfar, across, back, spread, onward = [], [], [], [], [], []
    for h in range(halves):
        mnear.append([])
        for p in range(pairs):
            src = share_of(h, partner("mp", 2 * p + 1))
            mnear[h].append(copy("mp", 1, src, mnear_s.at[h, p]))
        mfar.append({})
        for p in range(1, pairs):
            src = share_of(h, partner("mp", 2 * p))
            mfar[h][p] = copy("mp", 2 * p, src, mfar_s.at[h, p])
        across.append([])
        for r in behind:
            src = rows_at(mfar_s.at[h, 0], partner("dp", r), small)
            across[h].append(copy("dp", r, src, mpiece_s.at[h, r]))
        mine = full_ref.at[h, me]
        back.append([copy("dp", r, mpiece_s.at[h, 0], mine.at[deep]) for r in behind])
        spread.append([copy("mp", r, mine, mine) for r in evens + [1]])
        onward.append([])
        for r in evens:
            came = full_ref.at[h, partner("mp", r)]
            onward[h].append(copy("mp", 1, came, came))
    lines_in = [copy("mp", r, linein_s.at[0], linein_s.at[r]) for r in beside]
    lines_out = [copy("dp", r, lineout_s.at[0], lineout_s.at[r]) for r in behind]
    pnear = [copy("mp", 1, parts_s.at[2 * p + 1], pnear_s.at[p]) for p in range(pairs)]
    pfar = {p: copy("mp", 2 * p, parts_s.at[2 * p], pfar_s.at[p]) for p in range(1, pairs)}
    main_out = [
        copy("dp", r, rows_at(parts_s.at[0], partner("dp", r), main_piece), main_s.at[r])
        for r in behind
    ]
    main_all = [copy("dp", r, mainsum_s, main_ref.at[deep]) for r in behind]
    tnear = [copy("mp", 1, tparts_s.at[2 * p + 1], tnear_s.at[p]) for p in range(pairs)]
    tfar = {p: copy("mp", 2 * p, tparts_s.at[2 * p], tfar_s.at[p]) for p in range(1, pairs)}
    tails = [copy("dp", r, tparts_s.at[0], tails_s.at[r]) for r in behind]

    @pl.when(step == 0)
    def _():
        for level in range(LEVELS):
            for c in bring(level):
                c.start()
        for c in bring_more():
            c.start()
        greet([("mp", r) for r in beside] + [("dp", r) for r in behind])
        for c in ffn_out:
            c.start()
        mask_s[...] = head_mask(head_dim)
        gq_s[...] = jnp.zeros_like(gq_s)
        gk_s[...] = jnp.zeros_like(gk_s)
        gv_s[...] = jnp.zeros_like(gv_s)

    @pl.when(step == TILE // 2)
    def _():
        total = ffn_ref[pl.ds(pl.multiple_of(deep * piece, TILE), piece), :].astype(F32)
        for c, r in zip(ffn_out, behind):
            c.wait_recv()
            total = total + ffncame_s[r].astype(F32)
        ffnown_s[...] = total.astype(BF16)
        keep_ffn().start()
        for c in ffn_all:
            c.start()

    for level in range(LEVELS):

        @pl.when(step == level * (TILE // LEVELS))
        def _():
            for c in bring(level):
                c.wait()

    @pl.when(step < TILE)
    def _():
        mask = mask_s[...]
        minus = -mask
        starts = [pl.multiple_of(step * jump + u * block, TILE) for u in range(sets)]
        lane_head = lax.broadcasted_iota(jnp.int32, (COVER, 2 * lanes), 1) % lanes // head_dim
        zeros = jnp.zeros((COVER, lanes), BF16)
        units = [(u, g) for g in range(groups) for u in range(sets)]

        def at(ref, u, g):
            return ref[pl.ds(starts[u], COVER), pl.ds(g * lanes, lanes)]

        scaled = [at(ga_s, u, g) * at(rinv_s, u, g) for u, g in units]
        grads = []
        for (u, g), ga in zip(units, scaled):
            left = jnp.concatenate([ga, ga * at(att_s, u, g)], axis=1)
            right = jnp.concatenate([tiled(at(v_s, u, g), mask), minus], axis=1)
            grads.append(dot_rt(left, right))
        score_grads = []
        totals = {}
        for (u, g), grad in zip(units, grads):
            ds = p_ref[g, 0, u].astype(F32) * grad
            totals[g] = ds if g not in totals else totals[g] + ds
            score_grads.append(ds.astype(BF16))
        for g in range(groups):
            ds_s[step, g] = totals[g]
        query_grads = []
        for (u, g), ds in zip(units, score_grads):
            query_grads.append(dot(ds, tiled(at(k_s, u, g), mask)))
        pair_grads = []
        for (u, g), ds, ga in zip(units, score_grads, scaled):
            left = jnp.concatenate([ds, p_ref[g, 0, u]], axis=0)
            right = jnp.concatenate(
                [
                    jnp.concatenate([at(q_s, u, g), zeros], axis=1),
                    jnp.concatenate([zeros, ga], axis=1),
                ],
                axis=0,
            )
            pair_grads.append(dot_lt(left, right))
        for (u, g), grad_q, grad_kv in zip(units, query_grads, pair_grads):
            here, cols = pl.ds(starts[u], COVER), pl.ds(g * lanes, lanes)
            gq_s[here, cols] += (grad_q * scale).astype(BF16)
            both = jnp.where(lane_head == 0, grad_kv[:COVER], 0.0)
            for h in range(1, GROUP):
                both = jnp.where(lane_head == h, grad_kv[h * COVER : (h + 1) * COVER], both)
            both = both.astype(BF16)
            gk_s[here, cols] += both[:, :lanes]
            gv_s[here, cols] += both[:, lanes:]

    def table_grads():
        def unshift(g, _):
            full = ds_s[0, g]
            for o in range(1, TILE):
                turned = pltpu.roll(ds_s[o, g], COVER - o, 0)
                full = full + pltpu.roll(turned, GROUP * COVER - o, 1)
            for h in range(GROUP):
                base_s[g * GROUP + h] = full[:, h * COVER : (h + 1) * COVER]
            return 0

        lax.fori_loop(0, groups, unshift, 0)
        sums = []
        for pair in range((idx_ref.shape[0] + 1) // 2):
            onehot = index_onehot(pair_row(idx_ref, pair), gtab_s.shape[1])
            vals = jnp.concatenate([base_s[:, 2 * pair, :], base_s[:, 2 * pair + 1, :]], axis=1)
            high = vals.astype(BF16)
            both = jnp.concatenate([high, (vals - high.astype(F32)).astype(BF16)], axis=0)
            sums.append(dot_rt(both, onehot))
        count = base_s.shape[0]
        grad = sums[0]
        for x in sums[1:]:
            grad = grad + x
        gtab_s[...] = grad[:count] + grad[count:]

    @pl.when(step == TILE)
    def _():
        for c in bring_late():
            c.start()
        lines_s[...] = jnp.zeros_like(lines_s)
        for c in bring_more():
            c.wait()
        normed_t = n1_s[...].T
        for t, ref in enumerate((gq_s, gk_s, gv_s)):
            grad = dot(normed_t, ref[...]).T
            sums = jnp.sum(ref[...].astype(F32), axis=0, keepdims=True)
            lines_s[4 + t : 5 + t, :] = sums
            sums = jnp.broadcast_to(sums, (8, width)).T[:, :1]
            grad = (grad * g1_ref[...] + sums * b1_ref[...]).astype(BF16)
            for r in range(near_size):
                parts_s[r, t * span : (t + 1) * span, :] = grad[r * span : (r + 1) * span]
        for r in range(near_size):
            parts_s[r, 3 * span :, :] = gproj_ref[r * span : (r + 1) * span, :]
        for c in pnear:
            c.start()

    @pl.when(step == TILE + 1)
    def _():
        for p in reversed(range(pairs)):
            pnear[p].wait_recv()
            joined = parts_s[2 * p].astype(F32) + pnear_s[p].astype(F32)
            parts_s[2 * p] = joined.astype(BF16)
            if p:
                pfar[p].start()

    @pl.when(step >= TILE)
    def _():
        count = gmid_ref.shape[0]
        here = pl.ds(pl.multiple_of((step - TILE) * count, TILE), count)
        grad_mid = None
        for t, ref in enumerate((gq_s, gk_s, gv_s)):
            part = dot(ref[here, :], wt_s[t * width : (t + 1) * width, :])
            grad_mid = part if grad_mid is None else grad_mid + part
        stats = stats_ref[...]
        normed1 = n1_s[here, :].astype(F32)
        lines_s[0:1, :] += jnp.sum(grad_mid * normed1, axis=0, keepdims=True)
        lines_s[1:2, :] += jnp.sum(grad_mid, axis=0, keepdims=True)
        grad_merged = gmid_ref[...].astype(F32) + norm_back(
            grad_mid * g1_ref[...], normed1, stats[:, 3:4]
        )
        lines_s[2:3, :] += jnp.sum(grad_merged, axis=0, keepdims=True)
        grad_merged = grad_merged.astype(BF16)
        q_s[here, :] = grad_merged
        normed0 = ((x_ref[...].astype(F32) - stats[:, 0:1]) * stats[:, 1:2]).astype(BF16)
        n0_s[here, :] = normed0
        inv0_s[here, :] = jnp.broadcast_to(stats[:, 1:2], (count, inv0_s.shape[1]))

    @pl.when(step == TILE + dense_steps - 1)
    def _():
        narrow = merged_s.shape[1]
        per_half = n0_s.shape[1] // narrow // halves
        merged_t = q_s[...].T
        for h in range(halves):
            for j in range(h * per_half, (h + 1) * per_half):
                part = dot(merged_t, n0_s[:, j * narrow : (j + 1) * narrow])
                merged_s[j * width : (j + 1) * width, :] = part.astype(BF16)
            for c in mnear[h]:
                c.start()
        linein_s[0] = jnp.concatenate([sums2_ref[0:4, :], lines_s[0:4, :]], axis=0)
        for c in lines_in:
            c.start()
        for c in bring_late():
            c.wait()
        table_grads()
        for r in range(near_size):
            bias_sums = lines_s[4:7, r * span : (r + 1) * span]
            hidden = gub_ref.shape[2] // 2
            half = (r % 2) * hidden
            lines = [
                fill(bias_sums, width),
                fill(gtab_s[r * local : (r + 1) * local, :], width),
                fill(gub_ref[r // 2][:, half : half + hidden], width),
                jnp.zeros((TILE - 4 - local, width), F32),
            ]
            tparts_s[r] = jnp.concatenate(lines, axis=0).astype(BF16)
        for h in range(halves):
            for p in reversed(range(pairs)):
                mnear[h][p].wait_recv()
                spot = pl.ds(pl.multiple_of(share_at(h, partner("mp", 2 * p)), TILE), share)
                joined = merged_s[spot, :].astype(F32) + mnear_s[h, p].astype(F32)
                merged_s[spot, :] = joined.astype(BF16)
                if p:
                    mfar[h][p].start()
        for c in tnear:
            c.start()
        total = linein_s[0]
        for c, r in zip(lines_in, beside):
            c.wait_recv()
            total = total + linein_s[r]
        lineout_s[0] = total
        for c in lines_out:
            c.start()
        total = parts_s[0].astype(F32)
        for p in reversed(range(1, pairs)):
            pfar[p].wait_recv()
            total = total + pfar_s[p].astype(F32)
        parts_s[0] = total.astype(BF16)
        for c in main_out:
            c.start()
        input_part(0)

        for h in range(halves):
            mine = pl.ds(pl.multiple_of(share_at(h, me), TILE), share)
            total = merged_s[mine, :].astype(F32)
            for p in reversed(range(1, pairs)):
                mfar[h][p].wait_recv()
                total = total + mfar_s[h, p].astype(F32)
            mfar_s[h, 0] = total.astype(BF16)
            for c in across[h]:
                c.start()
        for p in reversed(range(pairs)):
            tnear[p].wait_recv()
            tparts_s[2 * p] = (tparts_s[2 * p].astype(F32) + tnear_s[p].astype(F32)).astype(BF16)
            if p:
                tfar[p].start()
        input_part(1)

        for h in range(halves):
            spot = pl.ds(pl.multiple_of(deep * small, TILE), small)
            total = mfar_s[h, 0, spot, :].astype(F32)
            for c, r in zip(across[h], behind):
                c.wait_recv()
                total = total + mpiece_s[h, r].astype(F32)
            mpiece_s[h, 0] = total.astype(BF16)
            keep_merge(h).start()
            for c in back[h]:
                c.start()
        spot = pl.ds(pl.multiple_of(deep * main_piece, TILE), main_piece)
        total = parts_s[0, spot, :].astype(F32)
        for c, r in zip(main_out, behind):
            c.wait_recv()
            total = total + main_s[r].astype(F32)
        mainsum_s[...] = total.astype(BF16)
        keep_main().start()
        for c in main_all:
            c.start()
        input_part(2)

        for h in range(halves):
            keep_merge(h).wait()
            for c in back[h]:
                c.wait_recv()
            for c in spread[h][-1:] + spread[h][-2::-1]:
                c.start()
        total = tparts_s[0].astype(F32)
        for p in reversed(range(1, pairs)):
            tfar[p].wait_recv()
            total = total + tfar_s[p].astype(F32)
        tparts_s[0] = total.astype(BF16)
        for c in tails:
            c.start()
        output_part(0)
        output_part(1)
        for h in range(halves):
            for c, after in zip(spread[h], onward[h]):
                c.wait_recv()
                after.start()
            if h == 0:
                output_part(2)

        total = lineout_s[0]
        for c, r in zip(lines_out, behind):
            c.wait_recv()
            total = total + lineout_s[r]
        sums_ref[...] = total
        total = tparts_s[0].astype(F32)
        for c, r in zip(tails, behind):
            c.wait_recv()
            total = total + tails_s[r].astype(F32)
        tail_ref[...] = total
        for h in range(halves):
            spread[h][-1].wait_recv()
            for c in onward[h]:
                c.wait_recv()
        for c in main_all + ffn_all:
            c.wait_recv()
        keep_ffn().wait()
        keep_main().wait()
        for h in range(halves):
            for c in mnear[h] + list(mfar[h].values()) + across[h] + back[h] + spread[h]:
                c.wait_send()
            for c in onward[h]:
                c.wait_send()
        for c in ffn_out + ffn_all + lines_in + lines_out + tnear + list(tfar.values()):
            c.wait_send()
        for c in pnear + list(pfar.values()) + main_out + tails + main_all:
            c.wait_send()
        for j in range(PARTS):
            take_gin(j).wait()
            take_raw(j).wait()


def back_rows(
    q,
    k,
    v,
    ga,
    rinv,
    att,
    n1,
    wt,
    p,
    idx,
    ffn,
    gmid,
    stats,
    x,
    g1,
    b1,
    gproj,
    gub,
    sums2,
    act,
    base,
    second,
    wm,
    g0,
    table_width,
    head_dim,
    local,
    near_size,
    far_size,
):
    rows, width = q.shape
    wide = x.shape[1]
    heads = width // head_dim
    groups, steps, sets, _, cover = p.shape
    dense_steps = 7
    count = rows // dense_steps
    narrow = 256
    pairs = near_size // 2
    piece = (ffn.shape[0] // far_size, ffn.shape[1])
    part = (4 * local * head_dim, width)
    main_piece = (4 * local * head_dim // far_size, width)
    total_rows = wide // narrow * width
    halves = 2 if total_rows // (2 * near_size * far_size) % TILE == 0 else 1
    share = total_rows // halves // near_size
    small = share // far_size
    near, far = near_size - 1, far_size - 1
    copies = 2 * far + halves * (4 * pairs - 2 + 2 * far) + near + far
    copies += (2 * pairs - 1) + 2 * far + (2 * pairs - 1) + far

    def place(i):
        return (jnp.maximum(i - steps, 0), 0)

    def p_place(i):
        return (0, jnp.minimum(i, steps - 1), 0, 0, 0)

    return call(
        functools.partial(back_kernel, head_dim, local, near_size, far_size, dense_steps),
        steps + dense_steps,
        (q, k, v, ga, rinv, att, n1, wt, p, idx, ffn, gmid, stats, x, g1, b1, gproj, gub, sums2)
        + (act, base, second, wm, g0),
        [anywhere()] * 8
        + [
            pl.BlockSpec((groups, 1, sets, COVER, cover), p_place),
            whole(idx.shape),
            whole(ffn.shape),
            pl.BlockSpec((count, width), place),
            pl.BlockSpec((count, 8), place),
            pl.BlockSpec((count, wide), place),
            whole(g1.shape),
            whole(b1.shape),
            whole(gproj.shape),
            whole(gub.shape),
            whole(sums2.shape),
        ]
        + [anywhere()] * 4
        + [whole(g0.shape)],
        [
            jax.ShapeDtypeStruct((rows, width), BF16),
            jax.ShapeDtypeStruct((rows, wide), BF16),
            jax.ShapeDtypeStruct((far_size,) + piece, BF16),
            jax.ShapeDtypeStruct((far_size,) + main_piece, BF16),
            jax.ShapeDtypeStruct((TILE, width), F32),
            jax.ShapeDtypeStruct((halves, near_size, far_size, small, narrow), BF16),
            jax.ShapeDtypeStruct((8, width), F32),
        ],
        [
            anywhere(),
            anywhere(),
            anywhere(),
            anywhere(),
            whole((TILE, width)),
            anywhere(),
            whole((8, width)),
        ],
        [pltpu.VMEM((rows, width), BF16)] * 7
        + [pltpu.VMEM((3 * width, width), BF16)]
        + [pltpu.VMEM((rows, width), BF16)] * 3
        + [
            pltpu.VMEM((TILE, groups, COVER, cover), F32),
            pltpu.VMEM((heads, COVER, COVER), F32),
            pltpu.VMEM((cover, GROUP * head_dim), BF16),
            pltpu.VMEM((heads, table_width), F32),
            pltpu.VMEM((far_size,) + piece, BF16),
            pltpu.VMEM(piece, BF16),
            pltpu.VMEM((total_rows, narrow), BF16),
            pltpu.VMEM((halves, pairs, share, narrow), BF16),
            pltpu.VMEM((halves, pairs, share, narrow), BF16),
            pltpu.VMEM((halves, far_size, small, narrow), BF16),
            pltpu.VMEM((near_size, TILE, width), BF16),
            pltpu.VMEM((pairs, TILE, width), BF16),
            pltpu.VMEM((pairs, TILE, width), BF16),
            pltpu.VMEM((near_size,) + part, BF16),
            pltpu.VMEM((pairs,) + part, BF16),
            pltpu.VMEM((pairs,) + part, BF16),
            pltpu.VMEM((far_size,) + main_piece, BF16),
            pltpu.VMEM(main_piece, BF16),
            pltpu.VMEM((far_size, TILE, width), BF16),
            pltpu.VMEM((near_size, 8, width), F32),
            pltpu.VMEM((far_size, 8, width), F32),
            pltpu.VMEM((8, width), F32),
            pltpu.VMEM((rows, wide), BF16),
            pltpu.VMEM((rows, 128), F32),
            pltpu.VMEM(wm.shape, BF16),
            pltpu.VMEM((act.shape[0] * act.shape[2], width), BF16),
            pltpu.SemaphoreType.DMA((6, LEVELS, sets)),
            pltpu.SemaphoreType.DMA((4 + halves,)),
            pltpu.SemaphoreType.DMA((2 + act.shape[0] + near_size,)),
            pltpu.SemaphoreType.DMA((2, PARTS)),
            pltpu.SemaphoreType.DMA((2 * copies,)),
        ],
        2 * rows * width * (24 * width + wide),
        rows * width * 20,
        group=2,
    )


def last_kernel(
    head_dim,
    local,
    window,
    live_ref,
    raw_ref,
    gin16_ref,
    g0_ref,
    b0_ref,
    sums_ref,
    tail_ref,
    wm_hbm,
    main_hbm,
    ffn_hbm,
    full_hbm,
    out_ref,
    gin_ref,
    gain0_ref,
    bias0_ref,
    gqkv_ref,
    gproj_ref,
    gqb_ref,
    gtab_ref,
    gub_ref,
    *rest,
):
    line_refs, rest = rest[:6], rest[6:]
    gmerge_hbm, gup_hbm, gdown_hbm, wm_ref, main_ref, ffn_ref, full_ref = rest[:7]
    gmerge_ref, gup_ref, gdown_ref, in_sems, out_sems = rest[7:]
    step = pl.program_id(0)
    count, width = raw_ref.shape
    rows = count * pl.num_programs(0)
    halves = full_ref.shape[0]
    narrow = full_ref.shape[2]

    def bring(i):
        pair = (
            (main_hbm, main_ref),
            (ffn_hbm, ffn_ref),
            (wm_hbm, wm_ref),
            (full_hbm, full_ref),
        )[i]
        return pltpu.make_async_copy(*pair, in_sems.at[i])

    def take(i):
        if i < 2:
            pair = ((gup_ref, gup_hbm), (gdown_ref, gdown_hbm))[i]
        else:
            here = pl.ds((i - 2) * narrow, narrow)
            pair = (gmerge_ref.at[here], gmerge_hbm.at[here])
        return pltpu.make_async_copy(*pair, out_sems.at[i])

    @pl.when(step == 0)
    def _():
        for i in range(4):
            bring(i).start()

    live = live_rows(live_ref, step * count, count, rows, width, window)
    out_ref[...] = jnp.where(live, raw_ref[...].astype(F32), 0.0)
    gin_ref[...] = gin16_ref[...].astype(F32)

    @pl.when(step == 0)
    def _():
        span = local * head_dim
        bring(0).wait()
        main = main_ref[...].astype(F32)
        for l in range(local):
            for t in range(3):
                at = t * span + l * head_dim
                gqkv_ref[l, t * head_dim : (t + 1) * head_dim, :] = main[at : at + head_dim]
        gproj_ref[...] = main[3 * span :]
        rows_of = []
        for l in range(local):
            here = slice(l * head_dim, (l + 1) * head_dim)
            rows_of.append(
                jnp.concatenate([tail_ref[t : t + 1, here] for t in range(3)], axis=1)
            )
        gqb_ref[...] = jnp.concatenate(rows_of, axis=0)
        gtab_ref[...] = tail_ref[3 : 3 + local, : gtab_ref.shape[1]]
        gub_ref[...] = tail_ref[3 + local : 4 + local, : gub_ref.shape[1]]
        for i, ref in enumerate(line_refs):
            ref[...] = sums_ref[i : i + 1, :]

    @pl.when(step == 1)
    def _():
        hidden = gup_ref.shape[1]
        bring(1).wait()
        gup_ref[...] = ffn_ref[:, :hidden].astype(F32)
        take(0).start()
        gdown_ref[...] = ffn_ref[:, hidden:].astype(F32).T
        take(1).start()
        bring(2).wait()
        bring(3).wait()

    low_sum = sums_ref[6:7, :]
    for j in range(halves):

        @pl.when(step == 1 + 2 * j // halves)
        def _():
            cols = pl.ds(j * narrow, narrow)
            grad = full_ref[j].astype(F32).T
            weight = wm_ref[cols, :].astype(F32)
            gain = jnp.sum(weight * grad, axis=1, keepdims=True)
            shift = jnp.sum(weight * low_sum, axis=1, keepdims=True)
            gain0_ref[:, cols] = jnp.broadcast_to(gain, (narrow, 128)).T[:1, :]
            bias0_ref[:, cols] = jnp.broadcast_to(shift, (narrow, 128)).T[:1, :]
            scale = jnp.broadcast_to(g0_ref[:, cols], (8, narrow)).T[:, :1]
            offset = jnp.broadcast_to(b0_ref[:, cols], (8, narrow)).T[:, :1]
            gmerge_ref[cols, :] = grad * scale + offset * low_sum
            take(2 + j).start()

    @pl.when(step == pl.num_programs(0) - 1)
    def _():
        for i in range(2 + halves):
            take(i).wait()


def last_rows(
    live, raw, gin16, wm, g0, b0, main, ffn, full, sums, tail, local, head_dim, rel, window
):
    rows, width = raw.shape
    wide = gin16.shape[1]
    step = rows // 3
    hidden = ffn.shape[1] // 2
    span = local * head_dim
    narrow_block = pl.BlockSpec((step, width), lambda i: (i, 0))
    wide_block = pl.BlockSpec((step, wide), lambda i: (i, 0))
    rest = [g0, b0, sums, tail]
    later = [wm, main, ffn, full]
    shapes = [
        (1, wide),
        (1, wide),
        (local, 3 * head_dim, width),
        (span, width),
        (local, 3 * head_dim),
        (local, rel),
        (1, hidden),
    ] + [(1, width)] * 6
    large = [(wide, width), (width, hidden), (hidden, width)]
    return call(
        functools.partial(last_kernel, head_dim, local, window),
        3,
        [live, raw, gin16] + rest + later,
        [pl.BlockSpec(memory_space=pltpu.SMEM), narrow_block, wide_block]
        + [whole(a.shape) for a in rest]
        + [anywhere()] * len(later),
        [
            jax.ShapeDtypeStruct((rows, width), F32),
            jax.ShapeDtypeStruct((rows, wide), F32),
        ]
        + [jax.ShapeDtypeStruct(shape, F32) for shape in shapes + large],
        [narrow_block, wide_block]
        + [whole(shape) for shape in shapes]
        + [anywhere()] * len(large),
        [pltpu.VMEM(a.shape, BF16) for a in later]
        + [pltpu.VMEM(shape, F32) for shape in large]
        + [
            pltpu.SemaphoreType.DMA((len(later),)),
            pltpu.SemaphoreType.DMA((2 + full.shape[0],)),
        ],
        2 * rows * width,
        rows * wide * 9,
    )


def shards(
    inputs,
    norm0_gain,
    norm0_bias,
    merge_weight,
    norm1_gain,
    norm1_bias,
    qkv_weight,
    qkv_bias,
    rel_table,
    rel_index,
    regions,
    live_windows,
    proj_weight,
    proj_bias,
    norm2_gain,
    norm2_bias,
    up_weight,
    up_bias,
    down_weight,
    down_bias,
    cotangent,
    n_dp,
    n_mp,
):
    micro, strip_rows, wide = inputs.shape
    width = merge_weight.shape[1]
    win = rel_index.shape[0]
    local, packed = qkv_bias.shape
    head_dim = packed // 3
    heads = local * n_mp
    hidden = up_bias.shape[0]
    rel = rel_table.shape[1]
    rows = micro * strip_rows
    windows = rows // win
    sets = windows // TILE
    strip = lax.axis_index("mp")

    region = lax.dynamic_slice_in_dim(regions, strip * strip_rows, strip_rows, axis=1)
    region = region.reshape(sets, rows // sets)
    jump = rows // sets // TILE - 1
    region = jnp.stack([region[:, o * jump : o * jump + COVER] for o in range(TILE)])
    region = jnp.tile(region[:, :, None, :], (1, 1, 1, GROUP))
    table_width = -(-rel // 128) * 128
    live = live_windows.T
    vecs = (proj_bias[None], norm2_gain[None], norm2_bias[None], down_bias[None])
    gain0, bias0 = norm0_gain[None], norm0_bias[None]
    gain1, bias1 = norm1_gain[None], norm1_bias[None]

    x = inputs.reshape(rows, wide)
    stats, n1, q, k, v, att, rinv, p, tiles, wt, second = front_rows(
        x,
        gain0,
        bias0,
        merge_weight,
        gain1,
        bias1,
        jnp.transpose(qkv_weight, (1, 2, 0)).reshape(local * packed, width),
        qkv_bias,
        rel_table,
        up_bias.reshape(-1, 128),
        up_weight,
        down_weight,
        proj_weight.reshape(local * head_dim, width),
        rel_index,
        region,
        n_mp,
        head_dim,
    )
    base, act, gmid, gatt, ffn_part, gub, gproj, sums2 = ffn_rows(
        live,
        n1,
        att,
        cotangent.reshape(rows, width),
        stats,
        tiles,
        second,
        vecs,
        local,
        hidden,
        win,
    )
    raw, gin16, ffn_sum, main, tail, gmerge, sums = back_rows(
        q,
        k,
        v,
        gatt,
        rinv,
        att,
        n1,
        wt,
        p,
        rel_index,
        ffn_part,
        gmid,
        stats,
        x,
        gain1,
        bias1,
        gproj,
        gub,
        sums2,
        act,
        base,
        second,
        merge_weight,
        gain0,
        table_width,
        head_dim,
        local,
        n_mp,
        n_dp,
    )
    span = local * head_dim
    out, grad_input, ggain0, gbias0, gqkv, gproj, gqb, gtab, gub, *lines, gmerge, gup, gdown = (
        last_rows(
            live,
            raw,
            gin16,
            merge_weight,
            gain0,
            bias0,
            main.reshape(4 * span, width),
            ffn_sum.reshape(width, 2 * hidden),
            gmerge.reshape(-1, width, gmerge.shape[4]),
            sums,
            tail,
            local,
            head_dim,
            rel,
            win,
        )
    )
    gpb, gain2, bias2, gdb, gain1, bias1 = (x.reshape(width) for x in lines)
    return (
        out.reshape(micro, strip_rows, width),
        grad_input.reshape(micro, strip_rows, wide),
        ggain0.reshape(wide),
        gbias0.reshape(wide),
        gmerge,
        gain1,
        bias1,
        jnp.transpose(gqkv, (2, 0, 1)),
        gqb,
        gtab,
        gproj.reshape(local, head_dim, width),
        gpb,
        gain2,
        bias2,
        gup,
        gub.reshape(hidden),
        gdown,
        gdb,
    )


def solution(mesh):
    placed = (
        P(None, ("dp", "mp"), None),
        P(),
        P(),
        P(),
        P(),
        P(),
        P(None, "mp", None),
        P("mp", None),
        P("mp", None),
        P(),
        P(None, "dp"),
        P(None, "dp"),
        P("mp", None, None),
        P(),
        P(),
        P(),
        P(None, "mp"),
        P("mp"),
        P("mp", None),
        P(),
        P(None, ("dp", "mp"), None),
    )
    return jax.shard_map(
        functools.partial(shards, n_dp=mesh.shape["dp"], n_mp=mesh.shape["mp"]),
        mesh=mesh,
        in_specs=placed,
        out_specs=(
            P(None, ("dp", "mp"), None),
            P(None, ("dp", "mp"), None),
            P(),
            P(),
            P(),
            P(),
            P(),
            P(None, "mp", None),
            P("mp", None),
            P("mp", None),
            P("mp", None, None),
            P(),
            P(),
            P(),
            P(None, "mp"),
            P("mp"),
            P("mp", None),
            P(),
        ),
        check_vma=False,
    )
```
